128 devices in a mesh: lat: 8 (over z, x_hi), lon: 16 (over x_lo, y, core).
Axes of the slice: x: 4 (x_hi: 2, x_lo: 2; x = x_hi * 2 + x_lo), y: 4, z: 4, core: 2. Of those that a mesh axis runs over, the one named last changes fastest.
Arguments:
- tokens: bfloat16 [96, 2048, 384], P('lat', 'lon'), may hold values from -7 to 7
- neighbor_mask: int32 [96, 5, 3], P('lat'), may hold values from 0 to 1, as said below
- w_query: bfloat16 [384, 384], replicated
- w_key: bfloat16 [384, 384], replicated
- w_value: bfloat16 [384, 384], replicated, may hold values from -0.3125 to 0.3125
- w_out: bfloat16 [384, 384], replicated, may hold values from -0.3125 to 0.3125
Outputs:
- layer_output: bfloat16 [96, 2048, 384], P('lat', 'lon')
The draws below stay inside these ranges and needn't reach their ends.
Inputs may be any that keep to these rules, and one draw needn't show every extreme that they name: `neighbor_mask`: entry [i, 2, 1] is 1 for every row; for the 2 rows nearest either pole every entry of column 1 is 1.
All inputs are finite; a program needn't handle non-finite values.
Results may differ from the reference program's by a relative error of at most 0.011.
Values may be sent and summed in bfloat16 or wider, within the bound.
A program may use at most 128 MiB of HBM per device.

```python
import jax
import jax.numpy as jnp
from jax import lax

WIDTH = 384
HEADS = 8
HEAD_DIM = 48
BLOCK = 128
RADIUS = 2
POLAR = 1
CAP = 3
NLAT = 96
NLON = 2048


def shared_weight(key):
    return jax.random.truncated_normal(key, -3.0, 3.0, (WIDTH, WIDTH), jnp.float32) * WIDTH ** (-0.5)


def draw_w_query(key, part):
    common = shared_weight(key)
    return common.astype(jnp.bfloat16)


def draw_w_key(key, part):
    key = jax.random.fold_in(key, 2)
    own_part = shared_weight(key)
    mixed = own_part
    return mixed.astype(jnp.bfloat16)


def draw_tokens(key, part):
    key = jax.random.fold_in(key, 5)
    shape = (NLAT, NLON, WIDTH)
    values = jax.random.truncated_normal(key, -6.0, 6.0, shape, jnp.float32)
    return values.astype(jnp.bfloat16)


def draw_neighbor_mask(key, part):
    key = jax.random.fold_in(key, 9)
    span = 2 * RADIUS + 1
    row_ids = jnp.arange(NLAT, dtype=jnp.int32)
    distance = jnp.minimum(row_ids, NLAT - 1 - row_ids)
    closeness = 1000 - 2000 * distance // NLAT
    offsets = jnp.abs(jnp.arange(span, dtype=jnp.int32) - RADIUS)
    row_level = 900 - 150 * offsets
    side_level = 300 + 600 * closeness // 1000
    column = jnp.arange(3, dtype=jnp.int32)
    factor = jnp.where(column[None, None, :] == 1, 1000, side_level[:, None, None])
    level = row_level[None, :, None] * factor // 1000
    drawn = jax.random.randint(key, (NLAT, span, 3), 0, 1000)
    bits = (drawn < level).astype(jnp.int32)
    near_pole = (distance < RADIUS)[:, None, None] & (column == 1)[None, None, :]
    middle = (offsets == 0)[None, :, None] & (column == 1)[None, None, :]
    return jnp.where(near_pole | middle, 1, bits).astype(jnp.int32)


def scatter_about(rng, dims, scale, most, kind=jnp.bfloat16):
    values = scale * jax.random.normal(rng, dims, jnp.float32)
    return jnp.clip(values, min=-most, max=most).astype(kind)


def setup_inputs(seed: int = 0) -> dict:
    arg_keys = jax.random.split(jax.random.key(seed), 7)
    return {
        "tokens": draw_tokens(jax.random.fold_in(arg_keys[6], 71), 0),
        "neighbor_mask": draw_neighbor_mask(jax.random.fold_in(arg_keys[6], 71), 0),
        "w_query": draw_w_query(jax.random.fold_in(arg_keys[6], 71), 0),
        "w_key": draw_w_key(jax.random.fold_in(arg_keys[6], 71), 0),
        "w_value": scatter_about(arg_keys[4], (WIDTH, WIDTH), WIDTH ** -0.5, 0.3125),
        "w_out": scatter_about(arg_keys[5], (WIDTH, WIDTH), WIDTH ** -0.5, 0.3125),
    }


BIG_NEG = -1.0e30


def project(field_data, weight):
    flattened = field_data.reshape(-1, field_data.shape[-1])
    result = jnp.dot(flattened, weight, preferred_element_type=jnp.float32)
    return result.astype(jnp.bfloat16).reshape(field_data.shape[:-1] + (weight.shape[1],))


def reflect_pad(field_data):
    half_turn = field_data.shape[1] // 2
    top_rows = jnp.roll(field_data[:RADIUS][::-1], half_turn, axis=1)
    bottom_rows = jnp.roll(field_data[-RADIUS:][::-1], half_turn, axis=1)
    with_rows = jnp.concatenate([top_rows, field_data, bottom_rows], axis=0)
    return jnp.concatenate([with_rows[:, -BLOCK:], with_rows, with_rows[:, :BLOCK]], axis=1)


def attend(row_queries, row_keys, row_values, counts):
    query_count = row_queries.shape[0]
    head_queries = row_queries.astype(jnp.float32).reshape(query_count, HEADS, HEAD_DIM)
    head_keys = row_keys.astype(jnp.float32).reshape(-1, HEADS, HEAD_DIM)
    head_values = row_values.astype(jnp.float32).reshape(-1, HEADS, HEAD_DIM)
    scores = jnp.einsum("qhd,khd->hqk", head_queries, head_keys) * (HEAD_DIM ** -0.5)
    allowed = counts > 0
    scores = jnp.where(allowed[None, None, :], scores, BIG_NEG)
    highest = jnp.max(scores, axis=-1, keepdims=True)
    unscaled = counts[None, None, :] * jnp.exp(scores - highest)
    weights = unscaled.astype(jnp.bfloat16)
    running_sum = jnp.sum(unscaled, axis=-1)
    numerator = jnp.einsum("hqk,khd->qhd", weights.astype(jnp.float32), head_values)
    return (numerator / running_sum.T[:, :, None]).reshape(query_count, -1).astype(jnp.bfloat16)


def cap_counts(center, sign):
    offsets = jnp.arange(2 * RADIUS + 1) - RADIUS
    target = jnp.arange(POLAR)[:, None] + sign * offsets[None, :]
    target = jnp.where(target < 0, -1 - target, target)
    matches = target[:, :, None] == jnp.arange(CAP)[None, None, :]
    return jnp.sum(jnp.where(matches, center[:, :, None], 0), axis=1).astype(jnp.float32)


def polar_rows(cap_queries, cap_keys, cap_values, cap_count):
    flat_keys = cap_keys.reshape(-1, WIDTH)
    flat_values = cap_values.reshape(-1, WIDTH)

    def one_polar(row_index):
        key_counts = jnp.repeat(cap_count[row_index], NLON)
        row_queries = cap_queries[row_index].reshape(-1, BLOCK, WIDTH)

        def one_block(block_queries):
            return attend(block_queries, flat_keys, flat_values, key_counts)

        return lax.map(one_block, row_queries).reshape(NLON, WIDTH)

    return lax.map(one_polar, jnp.arange(POLAR))


def reference(tokens, neighbor_mask, w_query, w_key, w_value, w_out):
    queries = project(tokens, w_query)
    keys = project(tokens, w_key)
    values = project(tokens, w_value)
    key_frame = reflect_pad(keys)
    value_frame = reflect_pad(values)
    lon_blocks = NLON // BLOCK
    span = 2 * RADIUS + 1

    def arrange(window):
        stacked = jnp.stack([window[:, column * BLOCK: column * BLOCK + NLON] for column in range(3)], axis=1)
        stacked = stacked.reshape(span, 3, lon_blocks, BLOCK, WIDTH)
        return stacked.transpose(2, 0, 1, 3, 4).reshape(lon_blocks, -1, WIDTH)

    def one_row(row_index):
        key_parts = arrange(lax.dynamic_slice_in_dim(key_frame, row_index, span, 0))
        value_parts = arrange(lax.dynamic_slice_in_dim(value_frame, row_index, span, 0))
        mask_row = lax.dynamic_index_in_dim(neighbor_mask, row_index, 0, keepdims=False)
        counts = jnp.repeat(mask_row.reshape(-1), BLOCK).astype(jnp.float32)
        row_queries = lax.dynamic_index_in_dim(queries, row_index, 0, keepdims=False).reshape(lon_blocks, BLOCK, WIDTH)

        def one_block(triple):
            return attend(triple[0], triple[1], triple[2], counts)

        return lax.map(one_block, (row_queries, key_parts, value_parts)).reshape(NLON, WIDTH)

    attended = lax.map(one_row, jnp.arange(NLAT))
    center = neighbor_mask[:, :, 1]
    north_rows = polar_rows(queries[:POLAR], keys[:CAP], values[:CAP], cap_counts(center[:POLAR], 1))
    south_rows = polar_rows(queries[NLAT - POLAR:][::-1], keys[NLAT - CAP:][::-1], values[NLAT - CAP:][::-1], cap_counts(center[NLAT - POLAR:][::-1], -1))
    attended = jnp.concatenate([north_rows, attended[POLAR:NLAT - POLAR], south_rows[::-1]], axis=0)
    return project(attended, w_out)
```

```python
import functools

import jax
import jax.numpy as jnp
from jax import lax
from jax.experimental import pallas as pl
from jax.experimental.pallas import tpu as pltpu
from jax.sharding import PartitionSpec as P

HEADS = 8
HEAD_DIM = 48
PAIRS = 4
WIDTH = 384
BLOCK = 128
ROWS = 12
RADIUS = 2
SPAN = 5
FRAME = ROWS + 2 * RADIUS
DUMMY = 3 * FRAME
VROWS = 112
LANES = 128 * PAIRS
GROUP = 8
AHEAD = 8
SCORE_SCALE = HEAD_DIM ** -0.5 * 1.4426950408889634
SUM_LOW = 1e-30
SUM_HIGH = 1e30
VMEM_LIMIT = 56 * 2**20
F32 = jnp.float32
BF16 = jnp.bfloat16
VMEM_SPEC = pl.BlockSpec(memory_space=pltpu.VMEM)
SMEM_SPEC = pl.BlockSpec(memory_space=pltpu.SMEM)
ANY_SPEC = pl.BlockSpec(memory_space=pl.ANY)


def dot(a, b, dims=((1,), (0,))):
    return lax.dot_general(a, b, (dims, ((), ())), preferred_element_type=F32)


def prepare_keys(w_key_ref, wide_ref):
    wide_ref[...] = jnp.zeros_like(wide_ref)
    for p in range(PAIRS):
        wide_ref[:, 128 * p : 128 * p + 96] = w_key_ref[:, 96 * p : 96 * p + 96]


def flipped(ref):
    return ref[...].astype(F32).T.astype(BF16)


def put_keys_values(tokens, slots, wide_ref, value_t_ref, k_ref, vt_ref):
    keys = dot(tokens, wide_ref[...]).astype(BF16)
    values = dot(value_t_ref[...], tokens, ((1,), (1,))).astype(BF16)
    for n, slot in enumerate(slots):
        k_ref[slot] = keys[128 * n : 128 * n + 128]
        for p in range(PAIRS):
            vt_ref[slot, p, 0:96] = values[96 * p : 96 * p + 96, 128 * n : 128 * n + 128]


def put_queries(tokens, rows, query_t_ref, qd_ref):
    queries = dot(query_t_ref[...], tokens, ((1,), (1,))).astype(BF16)
    for n, row in enumerate(rows):
        for p in range(PAIRS):
            part = queries[96 * p : 96 * p + 96, 128 * n : 128 * n + 128]
            qd_ref[row, p, 0:48, 0:128] = part[0:48]
            qd_ref[row, p, 48:96, 128:256] = part[48:96]


def clear_slots(k_ref, vt_ref, dummy):
    ones = jnp.ones((VROWS - 96, 128), BF16)

    def body(slot, carry):
        for p in range(PAIRS):
            vt_ref[slot, p, 96:VROWS] = ones
        return carry

    lax.fori_loop(0, vt_ref.shape[0], body, 0)
    if dummy is not None:
        k_ref[dummy] = jnp.zeros(k_ref.shape[1:], BF16)
        vt_ref[dummy] = jnp.zeros(vt_ref.shape[1:], BF16)


def run_tiles(tiles, count, q_of, k_ref, vt_ref, qd_ref, acc_ref):
    chunks = [(u, p) for u in range(count) for p in range(PAIRS)]

    def scores(chunk):
        u, p = chunk
        keys = jnp.concatenate([k_ref[s, :, 128 * p : 128 * p + 128] for s in tiles[u]], axis=0)
        return dot(keys, qd_ref[q_of[u], p])

    def values(chunk, weights):
        u, p = chunk
        return dot(jnp.concatenate([vt_ref[s, p] for s in tiles[u]], axis=1), weights)

    held = {}
    for step in range(len(chunks) + AHEAD):
        if step < len(chunks):
            held[step] = scores(chunks[step])
        if step >= AHEAD:
            chunk = chunks[step - AHEAD]
            weights = jnp.exp2(held.pop(step - AHEAD) * SCORE_SCALE).astype(BF16)
            acc_ref[q_of[chunk[0]], chunk[1]] += values(chunk, weights)


def build_lists(mask_ref, wanted, list_ref, row_ref, begin_ref, keep_of):
    pos = jnp.int32(0)
    for i in range(ROWS):
        begin_ref[2 * i] = pos
        keep = keep_of(i)
        for d in range(SPAN):
            for e in range(3):
                if not wanted(i, d, e):
                    continue
                list_ref[pos] = e * FRAME + i + d
                row_ref[pos] = i
                bit = (mask_ref[i, d, e] > 0).astype(jnp.int32)
                pos = pos + (bit if keep is None else bit * keep)
        begin_ref[2 * i + 1] = pos
        list_ref[pos] = DUMMY
        row_ref[pos] = i
        pos = (pos + 1) // 2 * 2
    for n in range(2 * GROUP):
        list_ref[pos + n] = DUMMY
        row_ref[pos + n] = 0
    return (pos + 2 * GROUP - 1) // (2 * GROUP)


def fast_rows(steps, list_ref, row_ref, k_ref, vt_ref, qd_ref, acc_ref):
    def step(t, carry):
        at = t * (2 * GROUP)
        tiles = [(list_ref[at + 2 * u], list_ref[at + 2 * u + 1]) for u in range(GROUP)]
        q_of = [row_ref[at + 2 * u] for u in range(GROUP)]
        run_tiles(tiles, GROUP, q_of, k_ref, vt_ref, qd_ref, acc_ref)
        return carry

    lax.fori_loop(0, steps, step, 0)


def safe_row(q, acc_at, begin, end, slot_of, k_ref, vt_ref, qd_ref, acc_ref, top_ref):
    top_ref[...] = jnp.full(top_ref.shape, -jnp.inf, F32)

    def scores(n, p):
        return dot(k_ref[slot_of(n), :, 128 * p : 128 * p + 128], qd_ref[q, p]) * SCORE_SCALE

    def find_top(n, carry):
        for p in range(PAIRS):
            top_ref[p] = jnp.maximum(top_ref[p], jnp.max(scores(n, p), axis=0, keepdims=True))
        return carry

    lax.fori_loop(begin, end, find_top, 0)
    acc_ref[acc_at] = jnp.zeros(acc_ref.shape[1:], F32)

    def add(n, carry):
        for p in range(PAIRS):
            weights = jnp.exp2(scores(n, p) - top_ref[p, 0:1]).astype(BF16)
            acc_ref[acc_at, p] += dot(vt_ref[slot_of(n), p], weights)
        return carry

    lax.fori_loop(begin, end, add, 0)


def sums_hold(sums):
    return jnp.where((sums >= SUM_LOW) & (sums <= SUM_HIGH), 1.0, 0.0)


def normalised(acc_ref, row):
    parts = []
    for p in range(PAIRS):
        sums = 1.0 / acc_ref[row, p, 96:97, :]
        parts.append(acc_ref[row, p, 0:48, 0:128] * sums[:, 0:128])
        parts.append(acc_ref[row, p, 48:96, 128:256] * sums[:, 128:256])
    return jnp.concatenate(parts, axis=0).astype(BF16)


def own_slot(n):
    return FRAME + RADIUS + n


def own_kernel(
    mask_ref, tokens_ref, w_query_ref, w_key_ref, w_value_ref,
    k_out, vt_out, qd_out, first_out, second_out, sums_out,
    k_ref, vt_ref, qd_ref, acc_ref, wide_ref, query_t_ref, value_t_ref, list_ref, row_ref, begin_ref, sem,
):
    prepare_keys(w_key_ref, wide_ref)
    query_t_ref[...] = flipped(w_query_ref)
    value_t_ref[...] = flipped(w_value_ref)
    clear_slots(k_ref, vt_ref, ROWS)
    qd_ref[...] = jnp.zeros_like(qd_ref)
    acc_ref[...] = jnp.zeros_like(acc_ref)

    def load(t, carry):
        tokens = tokens_ref[pl.ds(2 * t, 2)].reshape(2 * BLOCK, WIDTH)
        rows = (2 * t, 2 * t + 1)
        put_keys_values(tokens, rows, wide_ref, value_t_ref, k_ref, vt_ref)
        put_queries(tokens, rows, query_t_ref, qd_ref)
        return carry

    lax.fori_loop(0, ROWS // 2, load, 0)
    copies = [
        pltpu.make_async_copy(k_ref.at[pl.ds(0, ROWS)], k_out, sem.at[0]),
        pltpu.make_async_copy(vt_ref.at[pl.ds(0, ROWS)], vt_out, sem.at[1]),
        pltpu.make_async_copy(qd_ref, qd_out, sem.at[2]),
    ]
    for copy in copies:
        copy.start()
    pos = jnp.int32(0)
    for i in range(ROWS):
        for d in range(SPAN):
            r = i + d - RADIUS
            if not 0 <= r < ROWS:
                continue
            list_ref[pos] = r
            row_ref[pos] = i
            pos = pos + (mask_ref[i, d, 1] > 0).astype(jnp.int32)
        list_ref[pos] = ROWS
        row_ref[pos] = i
        pos = (pos + 1) // 2 * 2
    for n in range(2 * GROUP):
        list_ref[pos + n] = ROWS
        row_ref[pos + n] = 0
    steps = (pos + 2 * GROUP - 1) // (2 * GROUP)
    fast_rows(steps, list_ref, row_ref, k_ref, vt_ref, qd_ref, acc_ref)
    tail = [
        pltpu.make_async_copy(acc_ref.at[:, :, pl.ds(0, 48), pl.ds(0, 128)], first_out, sem.at[3]),
        pltpu.make_async_copy(acc_ref.at[:, :, pl.ds(48, 48), pl.ds(128, 128)], second_out, sem.at[4]),
        pltpu.make_async_copy(acc_ref.at[:, :, pl.ds(96, 8)], sums_out, sem.at[5]),
    ]
    for copy in tail:
        copy.start()
    for copy in copies + tail:
        copy.wait()


def frame_kernel(
    mask_ref, west_ref, east_ref, halo_ref, west_halo_ref, east_halo_ref,
    w_key_ref, w_value_ref, w_out_ref, own_k, own_vt, own_qd, first_in, second_in, sums_in,
    out_ref,
    k_ref, vt_ref, qd_ref, acc_ref, top_ref, hold_ref, wide_ref, value_t_ref, list_ref, row_ref, begin_ref, sem,
):
    lat = lax.axis_index("lat")
    last = lax.axis_size("lat") - 1
    own = pl.ds(own_slot(0), ROWS)
    copies = [
        pltpu.make_async_copy(own_qd, qd_ref, sem.at[2]),
        pltpu.make_async_copy(first_in, acc_ref.at[:, :, pl.ds(0, 48), pl.ds(0, 128)], sem.at[3]),
        pltpu.make_async_copy(second_in, acc_ref.at[:, :, pl.ds(48, 48), pl.ds(128, 128)], sem.at[4]),
        pltpu.make_async_copy(sums_in, acc_ref.at[:, :, pl.ds(96, 8)], sem.at[5]),
    ]
    for copy in copies:
        copy.start()
    prepare_keys(w_key_ref, wide_ref)
    value_t_ref[...] = flipped(w_value_ref)
    clear_slots(k_ref, vt_ref, DUMMY)

    def take(tokens, slots):
        put_keys_values(tokens.reshape(2 * BLOCK, WIDTH), slots, wide_ref, value_t_ref, k_ref, vt_ref)

    def load(t, carry):
        for column, ref in ((0, west_ref), (2, east_ref)):
            slot = column * FRAME + RADIUS + 2 * t
            take(ref[pl.ds(2 * t, 2)], (slot, slot + 1))
        return carry

    lax.fori_loop(0, ROWS // 2, load, 0)
    for column, ref in ((0, west_halo_ref), (1, halo_ref), (2, east_halo_ref)):
        for n, row in ((0, 0), (2, ROWS + RADIUS)):
            slot = column * FRAME + row
            take(ref[n : n + 2], (slot, slot + 1))

    def keep_of(i):
        if i == 0:
            return (lat != 0).astype(jnp.int32)
        if i == ROWS - 1:
            return (lat != last).astype(jnp.int32)
        return None

    def inside(i, d, e):
        return e == 1 and 0 <= i + d - RADIUS < ROWS

    steps = build_lists(mask_ref, lambda i, d, e: not inside(i, d, e), list_ref, row_ref, begin_ref, keep_of)
    for copy in copies:
        copy.wait()
    fast_rows(steps, list_ref, row_ref, k_ref, vt_ref, qd_ref, acc_ref)

    def finish(t, carry):
        mixed = jnp.concatenate([normalised(acc_ref, 2 * t), normalised(acc_ref, 2 * t + 1)], axis=1)
        result = dot(mixed, w_out_ref[...], ((0,), (0,))).astype(BF16)
        out_ref[pl.ds(2 * t, 2)] = result.reshape(2, BLOCK, WIDTH)
        return carry

    lax.fori_loop(0, ROWS // 2, finish, 0)
    hold_ref[...] = jnp.ones_like(hold_ref)
    for i in range(ROWS):
        for p in range(PAIRS):
            hold_ref[0:1] = jnp.minimum(hold_ref[0:1], sums_hold(acc_ref[i, p, 96:97, :]))
    holds = jnp.min(hold_ref[...]) > 0.5

    @pl.when(jnp.logical_not(holds))
    def _():
        more = [
            pltpu.make_async_copy(own_k, k_ref.at[own], sem.at[0]),
            pltpu.make_async_copy(own_vt, vt_ref.at[own], sem.at[1]),
        ]
        for copy in more:
            copy.start()
        for copy in more:
            copy.wait()
        build_lists(mask_ref, lambda i, d, e: True, list_ref, row_ref, begin_ref, lambda i: None)

        def again(i, carry):
            safe_row(
                i, i, begin_ref[2 * i], begin_ref[2 * i + 1], lambda n: list_ref[n],
                k_ref, vt_ref, qd_ref, acc_ref, top_ref,
            )
            return carry

        lax.fori_loop(0, ROWS, again, 0)
        lax.fori_loop(0, ROWS // 2, finish, 0)


def cap_kernel(
    query_tokens_ref, tokens_ref, w_query_ref, w_key_ref, w_value_ref, out_ref,
    k_ref, vt_ref, qd_ref, acc_ref, top_ref, hold_ref, wide_ref, query_t_ref, value_t_ref,
):
    lat = lax.axis_index("lat")
    last = lax.axis_size("lat") - 1
    blocks = tokens_ref.shape[0] // BLOCK

    def give(shift):
        for p in range(PAIRS):
            out_ref[96 * p : 96 * p + 48] = acc_ref[0, p, 0:48, 0:128]
            out_ref[96 * p + 48 : 96 * p + 96] = acc_ref[0, p, 48:96, 128:256]
            for half in range(2):
                lanes = slice(128 * half, 128 * half + 128)
                n = 2 * p + half
                out_ref[WIDTH + n : WIDTH + n + 1] = acc_ref[0, p, 96:97, lanes]
                out_ref[WIDTH + HEADS + n : WIDTH + HEADS + n + 1] = shift(p)[:, lanes]

    @pl.when(jnp.logical_and(lat != 0, lat != last))
    def _():
        prepare_keys(w_key_ref, wide_ref)
        query_t_ref[...] = flipped(w_query_ref)
        value_t_ref[...] = flipped(w_value_ref)
        clear_slots(k_ref, vt_ref, None)
        qd_ref[...] = jnp.zeros_like(qd_ref)
        acc_ref[...] = jnp.zeros_like(acc_ref)
        put_queries(query_tokens_ref[...], (0,), query_t_ref, qd_ref)

        def load(t, carry):
            tokens = tokens_ref[pl.ds(pl.multiple_of(t * 2 * BLOCK, 2 * BLOCK), 2 * BLOCK)]
            put_keys_values(tokens, (2 * t, 2 * t + 1), wide_ref, value_t_ref, k_ref, vt_ref)
            return carry

        lax.fori_loop(0, blocks // 2, load, 0)
        tiles = [(2 * t, 2 * t + 1) for t in range(blocks // 2)]
        run_tiles(tiles, blocks // 2, [0] * (blocks // 2), k_ref, vt_ref, qd_ref, acc_ref)
        give(lambda p: jnp.zeros((1, 256), F32))
        hold_ref[...] = jnp.ones_like(hold_ref)
        for p in range(PAIRS):
            hold_ref[0:1] = jnp.minimum(hold_ref[0:1], sums_hold(acc_ref[0, p, 96:97, :]))
        holds = jnp.min(hold_ref[...]) > 0.5

        @pl.when(jnp.logical_not(holds))
        def _():
            safe_row(0, 0, 0, blocks, lambda n: n, k_ref, vt_ref, qd_ref, acc_ref, top_ref)
            give(lambda p: top_ref[p, 0:1])


def join_kernel(mask_ref, a_ref, b_ref, c_ref, w_out_ref, layer_ref, out_ref, row_ref, sem):
    lat = lax.axis_index("lat")
    last = lax.axis_size("lat") - 1

    @pl.when(jnp.logical_or(lat == 0, lat == last))
    def _():
        row = jnp.where(lat == 0, 0, ROWS - 1)
        counts = [0, 0, 0]
        for d in range(SPAN):
            north = d - RADIUS if d >= RADIUS else RADIUS - 1 - d
            south = RADIUS - d if d <= RADIUS else d - RADIUS - 1
            bit = (mask_ref[row, d, 1] > 0).astype(jnp.int32)
            for r in range(3):
                hit = jnp.where(lat == 0, jnp.int32(north == r), jnp.int32(south == r))
                counts[r] = counts[r] + bit * hit
        parts = (a_ref, b_ref, c_ref)
        shifts = [ref[WIDTH + HEADS : WIDTH + 2 * HEADS] for ref in parts]
        low = [jnp.where(n > 0, s, -jnp.inf) for n, s in zip(counts, shifts)]
        top = jnp.maximum(jnp.maximum(low[0], low[1]), low[2])
        factors = [jnp.where(n > 0, jnp.exp2(s - top), 0.0) * n.astype(F32) for n, s in zip(counts, low)]
        total = sum(f * ref[WIDTH : WIDTH + HEADS] for f, ref in zip(factors, parts))
        heads = []
        for h in range(HEADS):
            rows = slice(HEAD_DIM * h, HEAD_DIM * h + HEAD_DIM)
            mixed = sum(f[h : h + 1] * ref[rows] for f, ref in zip(factors, parts))
            heads.append(mixed / total[h : h + 1])
        mixed = jnp.concatenate(heads, axis=0).astype(BF16)
        row_ref[...] = dot(mixed, w_out_ref[...], ((0,), (0,))).astype(BF16)
        copy = pltpu.make_async_copy(row_ref, out_ref.at[row], sem)
        copy.start()
        copy.wait()


def per_device(tokens, neighbor_mask, w_query, w_key, w_value, w_out):
    lat_count = lax.axis_size("lat")
    lon_count = lax.axis_size("lon")
    lat = lax.axis_index("lat")
    at_north = lat == 0
    at_south = lat == lat_count - 1
    last = lat_count - 1
    params = pltpu.CompilerParams(vmem_limit_bytes=VMEM_LIMIT)
    eastward = [(j, (j + 1) % lon_count) for j in range(lon_count)]
    westward = [((j + 1) % lon_count, j) for j in range(lon_count)]

    west = lax.ppermute(tokens, "lon", eastward)
    east = lax.ppermute(tokens, "lon", westward)
    north = lax.ppermute(tokens[ROWS - RADIUS :], "lat", [(i, i + 1) for i in range(last)])
    south = lax.ppermute(tokens[:RADIUS], "lat", [(i + 1, i) for i in range(last)])
    pole_row = jnp.where(at_north, tokens[:1], tokens[ROWS - 1 :])
    half = lon_count // 2
    far = lax.ppermute(pole_row, "lon", [(j, (j + half) % lon_count) for j in range(lon_count)])
    cap = jnp.where(at_north, tokens[:3], tokens[ROWS - 3 :][::-1])
    given = []
    for r in range(3):
        rows = cap[:1] if r == 0 else jnp.concatenate([cap[:1], cap[r : r + 1]], axis=0)
        given.append(lax.ppermute(rows, "lat", [(0, 1 + r), (last, last - 1 - r)]))
    helper = jnp.minimum(lat, last - lat)
    query_tokens = given[0][0] + given[1][0] + given[2][0]
    key_tokens = given[0][0] + given[1][1] + given[2][1]
    cap_tokens = lax.all_gather(key_tokens, "lon", axis=0, tiled=True)
    halo = jnp.concatenate(
        [
            north[:1],
            jnp.where(at_north, far, north[1:]),
            jnp.where(at_south, far, south[:1]),
            south[1:],
        ],
        axis=0,
    )
    west_halo = lax.ppermute(halo, "lon", eastward)
    east_halo = lax.ppermute(halo, "lon", westward)

    lists = [pltpu.SMEM((272,), jnp.int32), pltpu.SMEM((272,), jnp.int32), pltpu.SMEM((2 * ROWS,), jnp.int32)]
    k_shape = lambda n: (n, BLOCK, LANES)
    vt_shape = lambda n: (n, PAIRS, VROWS, BLOCK)
    qd_shape = lambda n: (n, PAIRS, 128, 256)
    acc_shape = lambda n: (n, PAIRS, VROWS, 256)
    square = pltpu.VMEM((WIDTH, WIDTH), BF16)
    wide = pltpu.VMEM((WIDTH, LANES), BF16)
    own = pl.pallas_call(
        own_kernel,
        out_shape=[
            jax.ShapeDtypeStruct(k_shape(ROWS), BF16),
            jax.ShapeDtypeStruct(vt_shape(ROWS), BF16),
            jax.ShapeDtypeStruct(qd_shape(ROWS), BF16),
            jax.ShapeDtypeStruct((ROWS, PAIRS, 48, 128), F32),
            jax.ShapeDtypeStruct((ROWS, PAIRS, 48, 128), F32),
            jax.ShapeDtypeStruct((ROWS, PAIRS, 8, 256), F32),
        ],
        in_specs=[SMEM_SPEC] + [VMEM_SPEC] * 4,
        out_specs=[ANY_SPEC] * 6,
        scratch_shapes=[
            pltpu.VMEM(k_shape(ROWS + 1), BF16),
            pltpu.VMEM(vt_shape(ROWS + 1), BF16),
            pltpu.VMEM(qd_shape(ROWS), BF16),
            pltpu.VMEM(acc_shape(ROWS), F32),
            wide, square, square, *lists,
            pltpu.SemaphoreType.DMA((6,)),
        ],
        compiler_params=params,
        cost_estimate=pl.CostEstimate(flops=8 * 10**9, bytes_accessed=12 * 2**20, transcendentals=0),
        name="own_column",
    )(neighbor_mask, tokens, w_query, w_key, w_value)
    capped = pl.pallas_call(
        cap_kernel,
        out_shape=jax.ShapeDtypeStruct((WIDTH + 2 * HEADS, BLOCK), F32),
        in_specs=[VMEM_SPEC] * 5,
        out_specs=VMEM_SPEC,
        scratch_shapes=[
            pltpu.VMEM(k_shape(lon_count), BF16),
            pltpu.VMEM(vt_shape(lon_count), BF16),
            pltpu.VMEM(qd_shape(1), BF16),
            pltpu.VMEM(acc_shape(1), F32),
            pltpu.VMEM((PAIRS, 8, 256), F32),
            pltpu.VMEM((8, 256), F32),
            wide, square, square,
        ],
        compiler_params=params,
        cost_estimate=pl.CostEstimate(flops=4 * 10**9, bytes_accessed=3 * 2**20, transcendentals=0),
        name="cap_rows",
    )(query_tokens, cap_tokens, w_query, w_key, w_value)
    returned = [
        lax.ppermute(capped, "lat", [(1 + r, 0), (last - 1 - r, last)]) for r in range(3)
    ]
    layer = pl.pallas_call(
        frame_kernel,
        out_shape=jax.ShapeDtypeStruct((ROWS, BLOCK, WIDTH), BF16),
        in_specs=[SMEM_SPEC] + [VMEM_SPEC] * 8 + [ANY_SPEC] * 6,
        out_specs=VMEM_SPEC,
        scratch_shapes=[
            pltpu.VMEM(k_shape(DUMMY + 1), BF16),
            pltpu.VMEM(vt_shape(DUMMY + 1), BF16),
            pltpu.VMEM(qd_shape(ROWS), BF16),
            pltpu.VMEM(acc_shape(ROWS), F32),
            pltpu.VMEM((PAIRS, 8, 256), F32),
            pltpu.VMEM((8, 256), F32),
            wide, square, *lists,
            pltpu.SemaphoreType.DMA((6,)),
        ],
        compiler_params=params,
        cost_estimate=pl.CostEstimate(flops=12 * 10**9, bytes_accessed=16 * 2**20, transcendentals=0),
        name="frame_columns",
    )(neighbor_mask, west, east, halo, west_halo, east_halo, w_key, w_value, w_out, *own)
    return pl.pallas_call(
        join_kernel,
        out_shape=jax.ShapeDtypeStruct((ROWS, BLOCK, WIDTH), BF16),
        in_specs=[SMEM_SPEC] + [VMEM_SPEC] * 4 + [ANY_SPEC],
        out_specs=ANY_SPEC,
        scratch_shapes=[pltpu.VMEM((BLOCK, WIDTH), BF16), pltpu.SemaphoreType.DMA],
        input_output_aliases={5: 0},
        compiler_params=params,
        name="join_cap",
    )(neighbor_mask, *returned, w_out, layer)


def solution(mesh):
    placed = (P("lat", "lon", None), P("lat", None, None), P(), P(), P(), P())
    return jax.shard_map(
        per_device, mesh=mesh, in_specs=placed, out_specs=P("lat", "lon", None), check_vma=False
    )
```

```python
import functools

import jax
import jax.numpy as jnp
from jax import lax
from jax.experimental import pallas as pl
from jax.experimental.pallas import tpu as pltpu
from jax.sharding import PartitionSpec as P

HEADS = 8
HEAD_DIM = 48
PAIRS = 4
WIDTH = 384
BLOCK = 128
ROWS = 12
RADIUS = 2
SPAN = 5
FRAME = ROWS + 2 * RADIUS
DUMMY = 3 * FRAME
VROWS = 112
LANES = 128 * PAIRS
GROUP = 8
AHEAD = 8
SCORE_SCALE = HEAD_DIM ** -0.5 * 1.4426950408889634
SUM_LOW = 1e-30
SUM_HIGH = 1e30
VMEM_LIMIT = 56 * 2**20
F32 = jnp.float32
BF16 = jnp.bfloat16
VMEM_SPEC = pl.BlockSpec(memory_space=pltpu.VMEM)
SMEM_SPEC = pl.BlockSpec(memory_space=pltpu.SMEM)
ANY_SPEC = pl.BlockSpec(memory_space=pl.ANY)


def dot(a, b, dims=((1,), (0,))):
    return lax.dot_general(a, b, (dims, ((), ())), preferred_element_type=F32)


def prepare_keys(w_key_ref, wide_ref):
    wide_ref[...] = jnp.zeros_like(wide_ref)
    for p in range(PAIRS):
        wide_ref[:, 128 * p : 128 * p + 96] = w_key_ref[:, 96 * p : 96 * p + 96]


def flipped(ref):
    return ref[...].astype(F32).T.astype(BF16)


def put_keys_values(tokens, slots, wide_ref, value_t_ref, k_ref, vt_ref):
    keys = dot(tokens, wide_ref[...]).astype(BF16)
    values = dot(value_t_ref[...], tokens, ((1,), (1,))).astype(BF16)
    for n, slot in enumerate(slots):
        k_ref[slot] = keys[128 * n : 128 * n + 128]
        for p in range(PAIRS):
            vt_ref[slot, p, 0:96] = values[96 * p : 96 * p + 96, 128 * n : 128 * n + 128]


def put_queries(tokens, rows, query_t_ref, qd_ref):
    queries = dot(query_t_ref[...], tokens, ((1,), (1,))).astype(BF16)
    for n, row in enumerate(rows):
        for p in range(PAIRS):
            part = queries[96 * p : 96 * p + 96, 128 * n : 128 * n + 128]
            qd_ref[row, p, 0:48, 0:128] = part[0:48]
            qd_ref[row, p, 48:96, 128:256] = part[48:96]


def clear_slots(k_ref, vt_ref, dummy):
    ones = jnp.ones((VROWS - 96, 128), BF16)

    def body(slot, carry):
        for p in range(PAIRS):
            vt_ref[slot, p, 96:VROWS] = ones
        return carry

    lax.fori_loop(0, vt_ref.shape[0], body, 0)
    if dummy is not None:
        k_ref[dummy] = jnp.zeros(k_ref.shape[1:], BF16)
        vt_ref[dummy] = jnp.zeros(vt_ref.shape[1:], BF16)


def run_tiles(tiles, count, q_of, k_ref, vt_ref, qd_ref, acc_ref):
    chunks = [(u, p) for u in range(count) for p in range(PAIRS)]

    def scores(chunk):
        u, p = chunk
        keys = jnp.concatenate([k_ref[s, :, 128 * p : 128 * p + 128] for s in tiles[u]], axis=0)
        return dot(keys, qd_ref[q_of[u], p])

    def values(chunk, weights):
        u, p = chunk
        return dot(jnp.concatenate([vt_ref[s, p] for s in tiles[u]], axis=1), weights)

    held = {}
    for step in range(len(chunks) + AHEAD):
        if step < len(chunks):
            held[step] = scores(chunks[step])
        if step >= AHEAD:
            chunk = chunks[step - AHEAD]
            weights = jnp.exp2(held.pop(step - AHEAD) * SCORE_SCALE).astype(BF16)
            acc_ref[q_of[chunk[0]], chunk[1]] += values(chunk, weights)


def build_lists(mask_ref, wanted, list_ref, row_ref, begin_ref, keep_of):
    pos = jnp.int32(0)
    for i in range(ROWS):
        begin_ref[2 * i] = pos
        keep = keep_of(i)
        for d in range(SPAN):
            for e in range(3):
                if not wanted(i, d, e):
                    continue
                list_ref[pos] = e * FRAME + i + d
                row_ref[pos] = i
                bit = (mask_ref[i, d, e] > 0).astype(jnp.int32)
                pos = pos + (bit if keep is None else bit * keep)
        begin_ref[2 * i + 1] = pos
        list_ref[pos] = DUMMY
        row_ref[pos] = i
        pos = (pos + 1) // 2 * 2
    for n in range(2 * GROUP):
        list_ref[pos + n] = DUMMY
        row_ref[pos + n] = 0
    return (pos + 2 * GROUP - 1) // (2 * GROUP)


def fast_rows(steps, list_ref, row_ref, k_ref, vt_ref, qd_ref, acc_ref):
    def step(t, carry):
        at = t * (2 * GROUP)
        tiles = [(list_ref[at + 2 * u], list_ref[at + 2 * u + 1]) for u in range(GROUP)]
        q_of = [row_ref[at + 2 * u] for u in range(GROUP)]
        run_tiles(tiles, GROUP, q_of, k_ref, vt_ref, qd_ref, acc_ref)
        return carry

    lax.fori_loop(0, steps, step, 0)


def safe_row(q, acc_at, begin, end, slot_of, k_ref, vt_ref, qd_ref, acc_ref, top_ref):
    top_ref[...] = jnp.full(top_ref.shape, -jnp.inf, F32)

    def scores(n, p):
        return dot(k_ref[slot_of(n), :, 128 * p : 128 * p + 128], qd_ref[q, p]) * SCORE_SCALE

    def find_top(n, carry):
        for p in range(PAIRS):
            top_ref[p] = jnp.maximum(top_ref[p], jnp.max(scores(n, p), axis=0, keepdims=True))
        return carry

    lax.fori_loop(begin, end, find_top, 0)
    acc_ref[acc_at] = jnp.zeros(acc_ref.shape[1:], F32)

    def add(n, carry):
        for p in range(PAIRS):
            weights = jnp.exp2(scores(n, p) - top_ref[p, 0:1]).astype(BF16)
            acc_ref[acc_at, p] += dot(vt_ref[slot_of(n), p], weights)
        return carry

    lax.fori_loop(begin, end, add, 0)


def sums_hold(sums):
    return jnp.where((sums >= SUM_LOW) & (sums <= SUM_HIGH), 1.0, 0.0)


def normalised(acc_ref, row):
    parts = []
    for p in range(PAIRS):
        sums = 1.0 / acc_ref[row, p, 96:97, :]
        parts.append(acc_ref[row, p, 0:48, 0:128] * sums[:, 0:128])
        parts.append(acc_ref[row, p, 48:96, 128:256] * sums[:, 128:256])
    return jnp.concatenate(parts, axis=0).astype(BF16)


def own_slot(n):
    return FRAME + RADIUS + n


def own_kernel(
    mask_ref, tokens_ref, w_query_ref, w_key_ref, w_value_ref,
    k_out, vt_out, qd_out, first_out, second_out, sums_out,
    k_ref, vt_ref, qd_ref, acc_ref, wide_ref, query_t_ref, value_t_ref, list_ref, row_ref, begin_ref, sem,
):
    prepare_keys(w_key_ref, wide_ref)
    query_t_ref[...] = flipped(w_query_ref)
    value_t_ref[...] = flipped(w_value_ref)
    clear_slots(k_ref, vt_ref, ROWS)
    qd_ref[...] = jnp.zeros_like(qd_ref)
    acc_ref[...] = jnp.zeros_like(acc_ref)

    def load(t, carry):
        tokens = tokens_ref[pl.ds(2 * t, 2)].reshape(2 * BLOCK, WIDTH)
        rows = (2 * t, 2 * t + 1)
        put_keys_values(tokens, rows, wide_ref, value_t_ref, k_ref, vt_ref)
        put_queries(tokens, rows, query_t_ref, qd_ref)
        return carry

    lax.fori_loop(0, ROWS // 2, load, 0)
    copies = [
        pltpu.make_async_copy(k_ref.at[pl.ds(0, ROWS)], k_out, sem.at[0]),
        pltpu.make_async_copy(vt_ref.at[pl.ds(0, ROWS)], vt_out, sem.at[1]),
        pltpu.make_async_copy(qd_ref, qd_out, sem.at[2]),
    ]
    for copy in copies:
        copy.start()
    pos = jnp.int32(0)
    for i in range(ROWS):
        for d in range(SPAN):
            r = i + d - RADIUS
            if not 0 <= r < ROWS:
                continue
            list_ref[pos] = r
            row_ref[pos] = i
            pos = pos + (mask_ref[i, d, 1] > 0).astype(jnp.int32)
        list_ref[pos] = ROWS
        row_ref[pos] = i
        pos = (pos + 1) // 2 * 2
    for n in range(2 * GROUP):
        list_ref[pos + n] = ROWS
        row_ref[pos + n] = 0
    steps = (pos + 2 * GROUP - 1) // (2 * GROUP)
    fast_rows(steps, list_ref, row_ref, k_ref, vt_ref, qd_ref, acc_ref)
    tail = [
        pltpu.make_async_copy(acc_ref.at[:, :, pl.ds(0, 48), pl.ds(0, 128)], first_out, sem.at[3]),
        pltpu.make_async_copy(acc_ref.at[:, :, pl.ds(48, 48), pl.ds(128, 128)], second_out, sem.at[4]),
        pltpu.make_async_copy(acc_ref.at[:, :, pl.ds(96, 8)], sums_out, sem.at[5]),
    ]
    for copy in tail:
        copy.start()
    for copy in copies + tail:
        copy.wait()


def frame_kernel(
    mask_ref, west_ref, east_ref, halo_ref, west_halo_ref, east_halo_ref,
    w_key_ref, w_value_ref, w_out_ref, own_k, own_vt, own_qd, first_in, second_in, sums_in,
    out_ref,
    k_ref, vt_ref, qd_ref, acc_ref, top_ref, hold_ref, wide_ref, value_t_ref, list_ref, row_ref, begin_ref, sem,
):
    lat = lax.axis_index("lat")
    last = lax.axis_size("lat") - 1
    own = pl.ds(own_slot(0), ROWS)
    copies = [
        pltpu.make_async_copy(own_qd, qd_ref, sem.at[2]),
        pltpu.make_async_copy(first_in, acc_ref.at[:, :, pl.ds(0, 48), pl.ds(0, 128)], sem.at[3]),
        pltpu.make_async_copy(second_in, acc_ref.at[:, :, pl.ds(48, 48), pl.ds(128, 128)], sem.at[4]),
        pltpu.make_async_copy(sums_in, acc_ref.at[:, :, pl.ds(96, 8)], sem.at[5]),
    ]
    for copy in copies:
        copy.start()
    prepare_keys(w_key_ref, wide_ref)
    value_t_ref[...] = flipped(w_value_ref)
    clear_slots(k_ref, vt_ref, DUMMY)

    def take(tokens, slots):
        put_keys_values(tokens.reshape(2 * BLOCK, WIDTH), slots, wide_ref, value_t_ref, k_ref, vt_ref)

    def load(t, carry):
        for column, ref in ((0, west_ref), (2, east_ref)):
            slot = column * FRAME + RADIUS + 2 * t
            take(ref[pl.ds(2 * t, 2)], (slot, slot + 1))
        return carry

    lax.fori_loop(0, ROWS // 2, load, 0)
    for column, ref in ((0, west_halo_ref), (1, halo_ref), (2, east_halo_ref)):
        for n, row in ((0, 0), (2, ROWS + RADIUS)):
            slot = column * FRAME + row
            take(ref[n : n + 2], (slot, slot + 1))

    def keep_of(i):
        if i == 0:
            return (lat != 0).astype(jnp.int32)
        if i == ROWS - 1:
            return (lat != last).astype(jnp.int32)
        return None

    def inside(i, d, e):
        return e == 1 and 0 <= i + d - RADIUS < ROWS

    steps = build_lists(mask_ref, lambda i, d, e: not inside(i, d, e), list_ref, row_ref, begin_ref, keep_of)
    for copy in copies:
        copy.wait()
    fast_rows(steps, list_ref, row_ref, k_ref, vt_ref, qd_ref, acc_ref)

    def finish(t, carry):
        mixed = jnp.concatenate([normalised(acc_ref, 2 * t), normalised(acc_ref, 2 * t + 1)], axis=1)
        result = dot(mixed, w_out_ref[...], ((0,), (0,))).astype(BF16)
        out_ref[pl.ds(2 * t, 2)] = result.reshape(2, BLOCK, WIDTH)
        return carry

    lax.fori_loop(0, ROWS // 2, finish, 0)
    hold_ref[...] = jnp.ones_like(hold_ref)
    for i in range(ROWS):
        for p in range(PAIRS):
            hold_ref[0:1] = jnp.minimum(hold_ref[0:1], sums_hold(acc_ref[i, p, 96:97, :]))
    holds = jnp.min(hold_ref[...]) > 0.5

    @pl.when(jnp.logical_not(holds))
    def _():
        more = [
            pltpu.make_async_copy(own_k, k_ref.at[own], sem.at[0]),
            pltpu.make_async_copy(own_vt, vt_ref.at[own], sem.at[1]),
        ]
        for copy in more:
            copy.start()
        for copy in more:
            copy.wait()
        build_lists(mask_ref, lambda i, d, e: True, list_ref, row_ref, begin_ref, lambda i: None)

        def again(i, carry):
            safe_row(
                i, i, begin_ref[2 * i], begin_ref[2 * i + 1], lambda n: list_ref[n],
                k_ref, vt_ref, qd_ref, acc_ref, top_ref,
            )
            return carry

        lax.fori_loop(0, ROWS, again, 0)
        lax.fori_loop(0, ROWS // 2, finish, 0)


def cap_kernel(
    query_tokens_ref, tokens_ref, w_query_ref, w_key_ref, w_value_ref, out_ref,
    k_ref, vt_ref, qd_ref, acc_ref, top_ref, hold_ref, wide_ref, query_t_ref, value_t_ref,
):
    lat = lax.axis_index("lat")
    last = lax.axis_size("lat") - 1
    blocks = tokens_ref.shape[0] // BLOCK

    def give(shift):
        for p in range(PAIRS):
            out_ref[96 * p : 96 * p + 48] = acc_ref[0, p, 0:48, 0:128]
            out_ref[96 * p + 48 : 96 * p + 96] = acc_ref[0, p, 48:96, 128:256]
            for half in range(2):
                lanes = slice(128 * half, 128 * half + 128)
                n = 2 * p + half
                out_ref[WIDTH + n : WIDTH + n + 1] = acc_ref[0, p, 96:97, lanes]
                out_ref[WIDTH + HEADS + n : WIDTH + HEADS + n + 1] = shift(p)[:, lanes]

    @pl.when(jnp.logical_and(lat != 0, lat != last))
    def _():
        prepare_keys(w_key_ref, wide_ref)
        query_t_ref[...] = flipped(w_query_ref)
        value_t_ref[...] = flipped(w_value_ref)
        clear_slots(k_ref, vt_ref, None)
        qd_ref[...] = jnp.zeros_like(qd_ref)
        acc_ref[...] = jnp.zeros_like(acc_ref)
        put_queries(query_tokens_ref[...], (0,), query_t_ref, qd_ref)

        def load(t, carry):
            tokens = tokens_ref[pl.ds(pl.multiple_of(t * 2 * BLOCK, 2 * BLOCK), 2 * BLOCK)]
            put_keys_values(tokens, (2 * t, 2 * t + 1), wide_ref, value_t_ref, k_ref, vt_ref)
            return carry

        lax.fori_loop(0, blocks // 2, load, 0)
        tiles = [(2 * t, 2 * t + 1) for t in range(blocks // 2)]
        run_tiles(tiles, blocks // 2, [0] * (blocks // 2), k_ref, vt_ref, qd_ref, acc_ref)
        give(lambda p: jnp.zeros((1, 256), F32))
        hold_ref[...] = jnp.ones_like(hold_ref)
        for p in range(PAIRS):
            hold_ref[0:1] = jnp.minimum(hold_ref[0:1], sums_hold(acc_ref[0, p, 96:97, :]))
        holds = jnp.min(hold_ref[...]) > 0.5

        @pl.when(jnp.logical_not(holds))
        def _():
            safe_row(0, 0, 0, blocks, lambda n: n, k_ref, vt_ref, qd_ref, acc_ref, top_ref)
            give(lambda p: top_ref[p, 0:1])


def join_kernel(mask_ref, a_ref, b_ref, c_ref, w_out_ref, layer_ref, out_ref, row_ref, sem):
    lat = lax.axis_index("lat")
    last = lax.axis_size("lat") - 1

    @pl.when(jnp.logical_or(lat == 0, lat == last))
    def _():
        row = jnp.where(lat == 0, 0, ROWS - 1)
        counts = [0, 0, 0]
        for d in range(SPAN):
            north = d - RADIUS if d >= RADIUS else RADIUS - 1 - d
            south = RADIUS - d if d <= RADIUS else d - RADIUS - 1
            bit = (mask_ref[row, d, 1] > 0).astype(jnp.int32)
            for r in range(3):
                hit = jnp.where(lat == 0, jnp.int32(north == r), jnp.int32(south == r))
                counts[r] = counts[r] + bit * hit
        parts = (a_ref, b_ref, c_ref)
        shifts = [ref[WIDTH + HEADS : WIDTH + 2 * HEADS] for ref in parts]
        low = [jnp.where(n > 0, s, -jnp.inf) for n, s in zip(counts, shifts)]
        top = jnp.maximum(jnp.maximum(low[0], low[1]), low[2])
        factors = [jnp.where(n > 0, jnp.exp2(s - top), 0.0) * n.astype(F32) for n, s in zip(counts, low)]
        total = sum(f * ref[WIDTH : WIDTH + HEADS] for f, ref in zip(factors, parts))
        heads = []
        for h in range(HEADS):
            rows = slice(HEAD_DIM * h, HEAD_DIM * h + HEAD_DIM)
            mixed = sum(f[h : h + 1] * ref[rows] for f, ref in zip(factors, parts))
            heads.append(mixed / total[h : h + 1])
        mixed = jnp.concatenate(heads, axis=0).astype(BF16)
        row_ref[...] = dot(mixed, w_out_ref[...], ((0,), (0,))).astype(BF16)
        copy = pltpu.make_async_copy(row_ref, out_ref.at[row], sem)
        copy.start()
        copy.wait()


def at_device(lat, lon):
    return {"lat": lat, "lon": lon}


def exchange_kernel(
    tokens_ref, west_ref, east_ref, halo_ref, west_halo_ref, east_halo_ref, query_ref, cap_ref,
    side_send, side_recv, halo_send, halo_recv, corner_send, corner_recv,
    give_send, query_recv, cap_recv, ring_send, ring_recv,
):
    lat, lon = lax.axis_index("lat"), lax.axis_index("lon")
    lat_count, lon_count = lax.axis_size("lat"), lax.axis_size("lon")
    last = lat_count - 1
    half = lon_count // 2
    is_north, is_south = lat == 0, lat == last
    at_pole = jnp.logical_or(is_north, is_south)
    east_lon, west_lon = lax.rem(lon + 1, lon_count), lax.rem(lon + lon_count - 1, lon_count)
    far_lon = lax.rem(lon + half, lon_count)
    pole = jnp.where(lat < lat_count // 2, 0, last)
    down = (jnp.where(is_south, lat, lat + 1), jnp.where(is_south, far_lon, lon))
    up = (jnp.where(is_north, lat, lat - 1), jnp.where(is_north, far_lon, lon))

    def send(src, dst, send_sem, recv_sem, to):
        copy = pltpu.make_async_remote_copy(
            src_ref=src, dst_ref=dst, send_sem=send_sem, recv_sem=recv_sem,
            device_id=at_device(*to), device_id_type=pl.DeviceIdType.MESH,
        )
        copy.start()
        return copy

    barrier = pltpu.get_barrier_semaphore()
    for to in ((lat, east_lon), (lat, west_lon), down, up):
        pl.semaphore_signal(barrier, inc=1, device_id=at_device(*to), device_id_type=pl.DeviceIdType.MESH)

    @pl.when(jnp.logical_not(at_pole))
    def _():
        pl.semaphore_signal(
            barrier, inc=1, device_id=at_device(pole, lon), device_id_type=pl.DeviceIdType.MESH
        )

    @pl.when(at_pole)
    def _():
        pl.semaphore_wait(barrier, 7)

    @pl.when(jnp.logical_not(at_pole))
    def _():
        pl.semaphore_wait(barrier, 4)

    def cap_row(r):
        return jnp.where(is_north, r, ROWS - 1 - r)

    def helper(r):
        return (jnp.where(is_north, 1 + r, last - 1 - r), lon)

    def gifts():
        copies = []
        for r in range(3):
            copies.append((tokens_ref.at[cap_row(r)], cap_ref.at[lon], give_send.at[r], cap_recv, helper(r)))
            copies.append((tokens_ref.at[cap_row(0)], query_ref, give_send.at[3 + r], query_recv, helper(r)))
        return copies

    @pl.when(at_pole)
    def _():
        for gift in gifts():
            send(*gift)

    sides = []
    for n, (row, slot, to) in enumerate(
        (
            (ROWS - 2, jnp.where(is_south, 3, 0), down),
            (ROWS - 1, jnp.where(is_south, 2, 1), down),
            (0, jnp.where(is_north, 1, 2), up),
            (1, jnp.where(is_north, 0, 3), up),
        )
    ):
        sides.append(send(tokens_ref.at[row], halo_ref.at[slot], halo_send.at[n], halo_recv.at[slot], to))
    wide = [
        send(tokens_ref, west_ref, side_send.at[0], side_recv.at[0], (lat, east_lon)),
        send(tokens_ref, east_ref, side_send.at[1], side_recv.at[1], (lat, west_lon)),
    ]

    def landed(dst, sem):
        pltpu.make_async_copy(dst, dst, sem).wait()

    def ring(step, going_east):
        if going_east:
            block = lax.rem(lon - (step - 1) + lon_count, lon_count)
            to, n = (lat, east_lon), 0
        else:
            block = lax.rem(lon + step - 1, lon_count)
            to, n = (lat, west_lon), 1
        return pltpu.make_async_remote_copy(
            src_ref=cap_ref.at[block], dst_ref=cap_ref.at[block],
            send_sem=ring_send.at[n, step - 1], recv_sem=ring_recv.at[n, step - 1],
            device_id=at_device(*to), device_id_type=pl.DeviceIdType.MESH,
        )

    def got(step, going_east):
        back = lon - step + lon_count if going_east else lon + step
        landed(cap_ref.at[lax.rem(back, lon_count)], ring_recv.at[0 if going_east else 1, step - 1])

    @pl.when(jnp.logical_not(at_pole))
    def _():
        landed(cap_ref.at[lon], cap_recv)
        ring(1, True).start()
        ring(1, False).start()

    for slot in range(4):
        landed(halo_ref.at[slot], halo_recv.at[slot])
    corners = [
        send(halo_ref, west_halo_ref, corner_send.at[0], corner_recv.at[0], (lat, east_lon)),
        send(halo_ref, east_halo_ref, corner_send.at[1], corner_recv.at[1], (lat, west_lon)),
    ]

    @pl.when(jnp.logical_not(at_pole))
    def _():
        for step in range(2, half + 1):
            got(step - 1, True)
            ring(step, True).start()
            if step < half:
                got(step - 1, False)
                ring(step, False).start()
        got(half, True)
        got(half - 1, False)
        landed(query_ref, query_recv)
        for step in range(1, half + 1):
            ring(step, True).wait_send()
            if step < half:
                ring(step, False).wait_send()

    for copy in sides:
        copy.wait_send()
    for copy in wide + corners:
        copy.wait()

    @pl.when(at_pole)
    def _():
        for src, dst, send_sem, recv_sem, to in gifts():
            pltpu.make_async_remote_copy(
                src_ref=src, dst_ref=dst, send_sem=send_sem, recv_sem=recv_sem,
                device_id=at_device(*to), device_id_type=pl.DeviceIdType.MESH,
            ).wait_send()


def per_device(tokens, neighbor_mask, w_query, w_key, w_value, w_out):
    lat_count = lax.axis_size("lat")
    lon_count = lax.axis_size("lon")
    last = lat_count - 1
    params = pltpu.CompilerParams(vmem_limit_bytes=VMEM_LIMIT)
    half = lon_count // 2
    strip = lambda *dims: jax.ShapeDtypeStruct((*dims, BLOCK, WIDTH), BF16)
    west, east, halo, west_halo, east_halo, query_tokens, cap_blocks = pl.pallas_call(
        exchange_kernel,
        out_shape=[strip(ROWS), strip(ROWS), strip(4), strip(4), strip(4), strip(), strip(lon_count)],
        in_specs=[ANY_SPEC],
        out_specs=[ANY_SPEC] * 7,
        scratch_shapes=[
            pltpu.SemaphoreType.DMA((2,)), pltpu.SemaphoreType.DMA((2,)),
            pltpu.SemaphoreType.DMA((4,)), pltpu.SemaphoreType.DMA((4,)),
            pltpu.SemaphoreType.DMA((2,)), pltpu.SemaphoreType.DMA((2,)),
            pltpu.SemaphoreType.DMA((6,)), pltpu.SemaphoreType.DMA, pltpu.SemaphoreType.DMA,
            pltpu.SemaphoreType.DMA((2, half)), pltpu.SemaphoreType.DMA((2, half)),
        ],
        compiler_params=pltpu.CompilerParams(collective_id=0, has_side_effects=True),
        name="exchange_tokens",
    )(tokens)
    cap_tokens = cap_blocks.reshape(lon_count * BLOCK, WIDTH)

    lists = [pltpu.SMEM((272,), jnp.int32), pltpu.SMEM((272,), jnp.int32), pltpu.SMEM((2 * ROWS,), jnp.int32)]
    k_shape = lambda n: (n, BLOCK, LANES)
    vt_shape = lambda n: (n, PAIRS, VROWS, BLOCK)
    qd_shape = lambda n: (n, PAIRS, 128, 256)
    acc_shape = lambda n: (n, PAIRS, VROWS, 256)
    square = pltpu.VMEM((WIDTH, WIDTH), BF16)
    wide = pltpu.VMEM((WIDTH, LANES), BF16)
    own = pl.pallas_call(
        own_kernel,
        out_shape=[
            jax.ShapeDtypeStruct(k_shape(ROWS), BF16),
            jax.ShapeDtypeStruct(vt_shape(ROWS), BF16),
            jax.ShapeDtypeStruct(qd_shape(ROWS), BF16),
            jax.ShapeDtypeStruct((ROWS, PAIRS, 48, 128), F32),
            jax.ShapeDtypeStruct((ROWS, PAIRS, 48, 128), F32),
            jax.ShapeDtypeStruct((ROWS, PAIRS, 8, 256), F32),
        ],
        in_specs=[SMEM_SPEC] + [VMEM_SPEC] * 4,
        out_specs=[ANY_SPEC] * 6,
        scratch_shapes=[
            pltpu.VMEM(k_shape(ROWS + 1), BF16),
            pltpu.VMEM(vt_shape(ROWS + 1), BF16),
            pltpu.VMEM(qd_shape(ROWS), BF16),
            pltpu.VMEM(acc_shape(ROWS), F32),
            wide, square, square, *lists,
            pltpu.SemaphoreType.DMA((6,)),
        ],
        compiler_params=params,
        cost_estimate=pl.CostEstimate(flops=8 * 10**9, bytes_accessed=12 * 2**20, transcendentals=0),
        name="own_column",
    )(neighbor_mask, tokens, w_query, w_key, w_value)
    capped = pl.pallas_call(
        cap_kernel,
        out_shape=jax.ShapeDtypeStruct((WIDTH + 2 * HEADS, BLOCK), F32),
        in_specs=[VMEM_SPEC] * 5,
        out_specs=VMEM_SPEC,
        scratch_shapes=[
            pltpu.VMEM(k_shape(lon_count), BF16),
            pltpu.VMEM(vt_shape(lon_count), BF16),
            pltpu.VMEM(qd_shape(1), BF16),
            pltpu.VMEM(acc_shape(1), F32),
            pltpu.VMEM((PAIRS, 8, 256), F32),
            pltpu.VMEM((8, 256), F32),
            wide, square, square,
        ],
        compiler_params=params,
        cost_estimate=pl.CostEstimate(flops=4 * 10**9, bytes_accessed=3 * 2**20, transcendentals=0),
        name="cap_rows",
    )(query_tokens, cap_tokens, w_query, w_key, w_value)
    returned = [
        lax.ppermute(capped, "lat", [(1 + r, 0), (last - 1 - r, last)]) for r in range(3)
    ]
    layer = pl.pallas_call(
        frame_kernel,
        out_shape=jax.ShapeDtypeStruct((ROWS, BLOCK, WIDTH), BF16),
        in_specs=[SMEM_SPEC] + [VMEM_SPEC] * 8 + [ANY_SPEC] * 6,
        out_specs=VMEM_SPEC,
        scratch_shapes=[
            pltpu.VMEM(k_shape(DUMMY + 1), BF16),
            pltpu.VMEM(vt_shape(DUMMY + 1), BF16),
            pltpu.VMEM(qd_shape(ROWS), BF16),
            pltpu.VMEM(acc_shape(ROWS), F32),
            pltpu.VMEM((PAIRS, 8, 256), F32),
            pltpu.VMEM((8, 256), F32),
            wide, square, *lists,
            pltpu.SemaphoreType.DMA((6,)),
        ],
        compiler_params=params,
        cost_estimate=pl.CostEstimate(flops=12 * 10**9, bytes_accessed=16 * 2**20, transcendentals=0),
        name="frame_columns",
    )(neighbor_mask, west, east, halo, west_halo, east_halo, w_key, w_value, w_out, *own)
    return pl.pallas_call(
        join_kernel,
        out_shape=jax.ShapeDtypeStruct((ROWS, BLOCK, WIDTH), BF16),
        in_specs=[SMEM_SPEC] + [VMEM_SPEC] * 4 + [ANY_SPEC],
        out_specs=ANY_SPEC,
        scratch_shapes=[pltpu.VMEM((BLOCK, WIDTH), BF16), pltpu.SemaphoreType.DMA],
        input_output_aliases={5: 0},
        compiler_params=params,
        name="join_cap",
    )(neighbor_mask, *returned, w_out, layer)


def solution(mesh):
    placed = (P("lat", "lon", None), P("lat", None, None), P(), P(), P(), P())
    return jax.shard_map(
        per_device, mesh=mesh, in_specs=placed, out_specs=P("lat", "lon", None), check_vma=False
    )
```

```python
import functools

import jax
import jax.numpy as jnp
from jax import lax
from jax.experimental import pallas as pl
from jax.experimental.pallas import tpu as pltpu
from jax.sharding import PartitionSpec as P

HEADS = 8
HEAD_DIM = 48
PAIRS = 4
WIDTH = 384
BLOCK = 128
ROWS = 12
RADIUS = 2
SPAN = 5
FRAME = ROWS + 2 * RADIUS
DUMMY = 3 * FRAME
VROWS = 112
LANES = 128 * PAIRS
GROUP = 8
AHEAD = 8
SCORE_SCALE = HEAD_DIM ** -0.5 * 1.4426950408889634
SUM_LOW = 1e-30
SUM_HIGH = 1e30
VMEM_LIMIT = 56 * 2**20
F32 = jnp.float32
BF16 = jnp.bfloat16
VMEM_SPEC = pl.BlockSpec(memory_space=pltpu.VMEM)
SMEM_SPEC = pl.BlockSpec(memory_space=pltpu.SMEM)
ANY_SPEC = pl.BlockSpec(memory_space=pl.ANY)


def dot(a, b, dims=((1,), (0,))):
    return lax.dot_general(a, b, (dims, ((), ())), preferred_element_type=F32)


def prepare_keys(w_key_ref, wide_ref):
    wide_ref[...] = jnp.zeros_like(wide_ref)
    for p in range(PAIRS):
        wide_ref[:, 128 * p : 128 * p + 96] = w_key_ref[:, 96 * p : 96 * p + 96]


def flipped(ref):
    return ref[...].astype(F32).T.astype(BF16)


def put_keys_values(tokens, slots, wide_ref, value_t_ref, k_ref, vt_ref):
    keys = dot(tokens, wide_ref[...]).astype(BF16)
    values = dot(value_t_ref[...], tokens, ((1,), (1,))).astype(BF16)
    for n, slot in enumerate(slots):
        k_ref[slot] = keys[128 * n : 128 * n + 128]
        for p in range(PAIRS):
            vt_ref[slot, p, 0:96] = values[96 * p : 96 * p + 96, 128 * n : 128 * n + 128]


def put_queries(tokens, rows, query_t_ref, qd_ref):
    queries = dot(query_t_ref[...], tokens, ((1,), (1,))).astype(BF16)
    for n, row in enumerate(rows):
        for p in range(PAIRS):
            part = queries[96 * p : 96 * p + 96, 128 * n : 128 * n + 128]
            qd_ref[row, p, 0:48, 0:128] = part[0:48]
            qd_ref[row, p, 48:96, 128:256] = part[48:96]


def clear_slots(k_ref, vt_ref, dummy):
    ones = jnp.ones((VROWS - 96, 128), BF16)

    def body(slot, carry):
        for p in range(PAIRS):
            vt_ref[slot, p, 96:VROWS] = ones
        return carry

    lax.fori_loop(0, vt_ref.shape[0], body, 0)
    if dummy is not None:
        k_ref[dummy] = jnp.zeros(k_ref.shape[1:], BF16)
        vt_ref[dummy] = jnp.zeros(vt_ref.shape[1:], BF16)


def run_tiles(tiles, count, q_of, k_ref, vt_ref, qd_ref, acc_ref):
    chunks = [(u, p) for u in range(count) for p in range(PAIRS)]

    def scores(chunk):
        u, p = chunk
        keys = jnp.concatenate([k_ref[s, :, 128 * p : 128 * p + 128] for s in tiles[u]], axis=0)
        return dot(keys, qd_ref[q_of[u], p])

    def values(chunk, weights):
        u, p = chunk
        return dot(jnp.concatenate([vt_ref[s, p] for s in tiles[u]], axis=1), weights)

    held = {}
    for step in range(len(chunks) + AHEAD):
        if step < len(chunks):
            held[step] = scores(chunks[step])
        if step >= AHEAD:
            chunk = chunks[step - AHEAD]
            weights = jnp.exp2(held.pop(step - AHEAD) * SCORE_SCALE).astype(BF16)
            acc_ref[q_of[chunk[0]], chunk[1]] += values(chunk, weights)


def build_lists(mask_ref, wanted, list_ref, row_ref, begin_ref, keep_of):
    pos = jnp.int32(0)
    for i in range(ROWS):
        begin_ref[2 * i] = pos
        keep = keep_of(i)
        for d in range(SPAN):
            for e in range(3):
                if not wanted(i, d, e):
                    continue
                list_ref[pos] = e * FRAME + i + d
                row_ref[pos] = i
                bit = (mask_ref[i, d, e] > 0).astype(jnp.int32)
                pos = pos + (bit if keep is None else bit * keep)
        begin_ref[2 * i + 1] = pos
        list_ref[pos] = DUMMY
        row_ref[pos] = i
        pos = (pos + 1) // 2 * 2
    for n in range(2 * GROUP):
        list_ref[pos + n] = DUMMY
        row_ref[pos + n] = 0
    return (pos + 2 * GROUP - 1) // (2 * GROUP)


def fast_rows(steps, list_ref, row_ref, k_ref, vt_ref, qd_ref, acc_ref):
    def step(t, carry):
        at = t * (2 * GROUP)
        tiles = [(list_ref[at + 2 * u], list_ref[at + 2 * u + 1]) for u in range(GROUP)]
        q_of = [row_ref[at + 2 * u] for u in range(GROUP)]
        run_tiles(tiles, GROUP, q_of, k_ref, vt_ref, qd_ref, acc_ref)
        return carry

    lax.fori_loop(0, steps, step, 0)


def safe_row(q, acc_at, begin, end, slot_of, k_ref, vt_ref, qd_ref, acc_ref, top_ref):
    top_ref[...] = jnp.full(top_ref.shape, -jnp.inf, F32)

    def scores(n, p):
        return dot(k_ref[slot_of(n), :, 128 * p : 128 * p + 128], qd_ref[q, p]) * SCORE_SCALE

    def find_top(n, carry):
        for p in range(PAIRS):
            top_ref[p] = jnp.maximum(top_ref[p], jnp.max(scores(n, p), axis=0, keepdims=True))
        return carry

    lax.fori_loop(begin, end, find_top, 0)
    acc_ref[acc_at] = jnp.zeros(acc_ref.shape[1:], F32)

    def add(n, carry):
        for p in range(PAIRS):
            weights = jnp.exp2(scores(n, p) - top_ref[p, 0:1]).astype(BF16)
            acc_ref[acc_at, p] += dot(vt_ref[slot_of(n), p], weights)
        return carry

    lax.fori_loop(begin, end, add, 0)


def sums_hold(sums):
    return jnp.where((sums >= SUM_LOW) & (sums <= SUM_HIGH), 1.0, 0.0)


def normalised(acc_ref, row):
    parts = []
    for p in range(PAIRS):
        sums = 1.0 / acc_ref[row, p, 96:97, :]
        parts.append(acc_ref[row, p, 0:48, 0:128] * sums[:, 0:128])
        parts.append(acc_ref[row, p, 48:96, 128:256] * sums[:, 128:256])
    return jnp.concatenate(parts, axis=0).astype(BF16)


def own_slot(n):
    return FRAME + RADIUS + n


def own_kernel(
    mask_ref, tokens_ref, w_query_ref, w_key_ref, w_value_ref,
    k_out, vt_out, qd_out, first_out, second_out, sums_out,
    k_ref, vt_ref, qd_ref, acc_ref, wide_ref, query_t_ref, value_t_ref, list_ref, row_ref, begin_ref, sem,
):
    prepare_keys(w_key_ref, wide_ref)
    query_t_ref[...] = flipped(w_query_ref)
    value_t_ref[...] = flipped(w_value_ref)
    clear_slots(k_ref, vt_ref, ROWS)
    qd_ref[...] = jnp.zeros_like(qd_ref)
    acc_ref[...] = jnp.zeros_like(acc_ref)

    def load(t, carry):
        tokens = tokens_ref[pl.ds(2 * t, 2)].reshape(2 * BLOCK, WIDTH)
        rows = (2 * t, 2 * t + 1)
        put_keys_values(tokens, rows, wide_ref, value_t_ref, k_ref, vt_ref)
        put_queries(tokens, rows, query_t_ref, qd_ref)
        return carry

    lax.fori_loop(0, ROWS // 2, load, 0)
    copies = [
        pltpu.make_async_copy(k_ref.at[pl.ds(0, ROWS)], k_out, sem.at[0]),
        pltpu.make_async_copy(vt_ref.at[pl.ds(0, ROWS)], vt_out, sem.at[1]),
        pltpu.make_async_copy(qd_ref, qd_out, sem.at[2]),
    ]
    for copy in copies:
        copy.start()
    pos = jnp.int32(0)
    for i in range(ROWS):
        for d in range(SPAN):
            r = i + d - RADIUS
            if not 0 <= r < ROWS:
                continue
            list_ref[pos] = r
            row_ref[pos] = i
            pos = pos + (mask_ref[i, d, 1] > 0).astype(jnp.int32)
        list_ref[pos] = ROWS
        row_ref[pos] = i
        pos = (pos + 1) // 2 * 2
    for n in range(2 * GROUP):
        list_ref[pos + n] = ROWS
        row_ref[pos + n] = 0
    steps = (pos + 2 * GROUP - 1) // (2 * GROUP)
    fast_rows(steps, list_ref, row_ref, k_ref, vt_ref, qd_ref, acc_ref)
    tail = [
        pltpu.make_async_copy(acc_ref.at[:, :, pl.ds(0, 48), pl.ds(0, 128)], first_out, sem.at[3]),
        pltpu.make_async_copy(acc_ref.at[:, :, pl.ds(48, 48), pl.ds(128, 128)], second_out, sem.at[4]),
        pltpu.make_async_copy(acc_ref.at[:, :, pl.ds(96, 8)], sums_out, sem.at[5]),
    ]
    for copy in tail:
        copy.start()
    for copy in copies + tail:
        copy.wait()


def frame_kernel(
    mask_ref, west_ref, east_ref, halo_ref, west_halo_ref, east_halo_ref,
    w_key_ref, w_value_ref, w_out_ref, own_k, own_vt, own_qd, first_in, second_in, sums_in,
    out_ref,
    k_ref, vt_ref, qd_ref, acc_ref, top_ref, hold_ref, wide_ref, value_t_ref, list_ref, row_ref, begin_ref, sem,
):
    lat = lax.axis_index("lat")
    last = lax.axis_size("lat") - 1
    own = pl.ds(own_slot(0), ROWS)
    copies = [
        pltpu.make_async_copy(own_qd, qd_ref, sem.at[2]),
        pltpu.make_async_copy(first_in, acc_ref.at[:, :, pl.ds(0, 48), pl.ds(0, 128)], sem.at[3]),
        pltpu.make_async_copy(second_in, acc_ref.at[:, :, pl.ds(48, 48), pl.ds(128, 128)], sem.at[4]),
        pltpu.make_async_copy(sums_in, acc_ref.at[:, :, pl.ds(96, 8)], sem.at[5]),
    ]
    for copy in copies:
        copy.start()
    prepare_keys(w_key_ref, wide_ref)
    value_t_ref[...] = flipped(w_value_ref)
    clear_slots(k_ref, vt_ref, DUMMY)

    def take(tokens, slots):
        put_keys_values(tokens.reshape(2 * BLOCK, WIDTH), slots, wide_ref, value_t_ref, k_ref, vt_ref)

    def load(t, carry):
        for column, ref in ((0, west_ref), (2, east_ref)):
            slot = column * FRAME + RADIUS + 2 * t
            take(ref[pl.ds(2 * t, 2)], (slot, slot + 1))
        return carry

    lax.fori_loop(0, ROWS // 2, load, 0)
    for column, ref in ((0, west_halo_ref), (1, halo_ref), (2, east_halo_ref)):
        for n, row in ((0, 0), (2, ROWS + RADIUS)):
            slot = column * FRAME + row
            take(ref[n : n + 2], (slot, slot + 1))

    def keep_of(i):
        if i == 0:
            return (lat != 0).astype(jnp.int32)
        if i == ROWS - 1:
            return (lat != last).astype(jnp.int32)
        return None

    def inside(i, d, e):
        return e == 1 and 0 <= i + d - RADIUS < ROWS

    steps = build_lists(mask_ref, lambda i, d, e: not inside(i, d, e), list_ref, row_ref, begin_ref, keep_of)
    for copy in copies:
        copy.wait()
    fast_rows(steps, list_ref, row_ref, k_ref, vt_ref, qd_ref, acc_ref)

    def finish(t, carry):
        mixed = jnp.concatenate([normalised(acc_ref, 2 * t), normalised(acc_ref, 2 * t + 1)], axis=1)
        result = dot(mixed, w_out_ref[...], ((0,), (0,))).astype(BF16)
        out_ref[pl.ds(2 * t, 2)] = result.reshape(2, BLOCK, WIDTH)
        return carry

    lax.fori_loop(0, ROWS // 2, finish, 0)
    hold_ref[...] = jnp.ones_like(hold_ref)
    for i in range(ROWS):
        for p in range(PAIRS):
            hold_ref[0:1] = jnp.minimum(hold_ref[0:1], sums_hold(acc_ref[i, p, 96:97, :]))
    holds = jnp.min(hold_ref[...]) > 0.5

    @pl.when(jnp.logical_not(holds))
    def _():
        more = [
            pltpu.make_async_copy(own_k, k_ref.at[own], sem.at[0]),
            pltpu.make_async_copy(own_vt, vt_ref.at[own], sem.at[1]),
        ]
        for copy in more:
            copy.start()
        for copy in more:
            copy.wait()
        build_lists(mask_ref, lambda i, d, e: True, list_ref, row_ref, begin_ref, lambda i: None)

        def again(i, carry):
            safe_row(
                i, i, begin_ref[2 * i], begin_ref[2 * i + 1], lambda n: list_ref[n],
                k_ref, vt_ref, qd_ref, acc_ref, top_ref,
            )
            return carry

        lax.fori_loop(0, ROWS, again, 0)
        lax.fori_loop(0, ROWS // 2, finish, 0)


def cap_kernel(
    query_tokens_ref, tokens_ref, w_query_ref, w_key_ref, w_value_ref, out_ref,
    k_ref, vt_ref, qd_ref, acc_ref, top_ref, hold_ref, wide_ref, query_t_ref, value_t_ref,
):
    lat = lax.axis_index("lat")
    last = lax.axis_size("lat") - 1
    blocks = tokens_ref.shape[0] // BLOCK

    def give(shift):
        for p in range(PAIRS):
            out_ref[96 * p : 96 * p + 48] = acc_ref[0, p, 0:48, 0:128]
            out_ref[96 * p + 48 : 96 * p + 96] = acc_ref[0, p, 48:96, 128:256]
            for half in range(2):
                lanes = slice(128 * half, 128 * half + 128)
                n = 2 * p + half
                out_ref[WIDTH + n : WIDTH + n + 1] = acc_ref[0, p, 96:97, lanes]
                out_ref[WIDTH + HEADS + n : WIDTH + HEADS + n + 1] = shift(p)[:, lanes]

    @pl.when(jnp.logical_and(lat != 0, lat != last))
    def _():
        prepare_keys(w_key_ref, wide_ref)
        query_t_ref[...] = flipped(w_query_ref)
        value_t_ref[...] = flipped(w_value_ref)
        clear_slots(k_ref, vt_ref, None)
        qd_ref[...] = jnp.zeros_like(qd_ref)
        acc_ref[...] = jnp.zeros_like(acc_ref)
        put_queries(query_tokens_ref[...], (0,), query_t_ref, qd_ref)

        def load(t, carry):
            tokens = tokens_ref[pl.ds(pl.multiple_of(t * 2 * BLOCK, 2 * BLOCK), 2 * BLOCK)]
            put_keys_values(tokens, (2 * t, 2 * t + 1), wide_ref, value_t_ref, k_ref, vt_ref)
            return carry

        lax.fori_loop(0, blocks // 2, load, 0)
        tiles = [(2 * t, 2 * t + 1) for t in range(blocks // 2)]
        run_tiles(tiles, blocks // 2, [0] * (blocks // 2), k_ref, vt_ref, qd_ref, acc_ref)
        give(lambda p: jnp.zeros((1, 256), F32))
        hold_ref[...] = jnp.ones_like(hold_ref)
        for p in range(PAIRS):
            hold_ref[0:1] = jnp.minimum(hold_ref[0:1], sums_hold(acc_ref[0, p, 96:97, :]))
        holds = jnp.min(hold_ref[...]) > 0.5

        @pl.when(jnp.logical_not(holds))
        def _():
            safe_row(0, 0, 0, blocks, lambda n: n, k_ref, vt_ref, qd_ref, acc_ref, top_ref)
            give(lambda p: top_ref[p, 0:1])


def join_kernel(mask_ref, a_ref, b_ref, c_ref, w_out_ref, layer_ref, out_ref, row_ref, sem):
    lat = lax.axis_index("lat")
    last = lax.axis_size("lat") - 1

    @pl.when(jnp.logical_or(lat == 0, lat == last))
    def _():
        row = jnp.where(lat == 0, 0, ROWS - 1)
        counts = [0, 0, 0]
        for d in range(SPAN):
            north = d - RADIUS if d >= RADIUS else RADIUS - 1 - d
            south = RADIUS - d if d <= RADIUS else d - RADIUS - 1
            bit = (mask_ref[row, d, 1] > 0).astype(jnp.int32)
            for r in range(3):
                hit = jnp.where(lat == 0, jnp.int32(north == r), jnp.int32(south == r))
                counts[r] = counts[r] + bit * hit
        parts = (a_ref, b_ref, c_ref)
        shifts = [ref[WIDTH + HEADS : WIDTH + 2 * HEADS] for ref in parts]
        low = [jnp.where(n > 0, s, -jnp.inf) for n, s in zip(counts, shifts)]
        top = jnp.maximum(jnp.maximum(low[0], low[1]), low[2])
        factors = [jnp.where(n > 0, jnp.exp2(s - top), 0.0) * n.astype(F32) for n, s in zip(counts, low)]
        total = sum(f * ref[WIDTH : WIDTH + HEADS] for f, ref in zip(factors, parts))
        heads = []
        for h in range(HEADS):
            rows = slice(HEAD_DIM * h, HEAD_DIM * h + HEAD_DIM)
            mixed = sum(f[h : h + 1] * ref[rows] for f, ref in zip(factors, parts))
            heads.append(mixed / total[h : h + 1])
        mixed = jnp.concatenate(heads, axis=0).astype(BF16)
        row_ref[...] = dot(mixed, w_out_ref[...], ((0,), (0,))).astype(BF16)
        copy = pltpu.make_async_copy(row_ref, out_ref.at[row], sem)
        copy.start()
        copy.wait()


def at_device(lat, lon):
    return {"lat": lat, "lon": lon}


def remote(src, dst, send_sem, recv_sem, to):
    return pltpu.make_async_remote_copy(
        src_ref=src, dst_ref=dst, send_sem=send_sem, recv_sem=recv_sem,
        device_id=at_device(*to), device_id_type=pl.DeviceIdType.MESH,
    )


def landed(dst, sem):
    pltpu.make_async_copy(dst, dst, sem).wait()


class Plan:
    def __init__(self):
        self.lat, self.lon = lat, lon = lax.axis_index("lat"), lax.axis_index("lon")
        self.lon_count, self.last = lax.axis_size("lon"), lax.axis_size("lat") - 1
        self.half = half = self.lon_count // 2
        self.is_north, self.is_south = lat == 0, lat == self.last
        self.at_pole = jnp.logical_or(self.is_north, self.is_south)
        self.east = (lat, lax.rem(lon + 1, self.lon_count))
        self.west = (lat, lax.rem(lon + self.lon_count - 1, self.lon_count))
        self.far = (lat, lax.rem(lon + half, self.lon_count))
        self.odd = lax.rem(lon, 2) == 1
        self.place = lax.rem(lon, half)
        self.side = lon // half
        base = lon - self.place
        self.ring_east = (lat, base + lax.rem(self.place + 1, half))
        self.ring_west = (lat, base + lax.rem(self.place + half - 1, half))
        flip = lat + 1 - 2 * lax.rem(lat, 2)
        first_half = self.side == 0
        self.relay = (jnp.where(first_half, flip, lat), self.far[1])
        self.source = (jnp.where(first_half, lat, flip), self.far[1])
        self.pole = jnp.where(lat < (self.last + 1) // 2, 0, self.last)

    def relay_of(self, lat):
        flip = lat + 1 - 2 * lax.rem(lat, 2)
        return (jnp.where(self.side == 0, flip, lat), self.far[1])

    def helper(self, r):
        return (jnp.where(self.is_north, 1 + r, self.last - 1 - r), self.lon)

    def cap_row(self, r):
        return jnp.where(self.is_north, r, ROWS - 1 - r)


def meet(plan):
    barrier = pltpu.get_barrier_semaphore()

    def tell(to):
        pl.semaphore_signal(barrier, inc=1, device_id=at_device(*to), device_id_type=pl.DeviceIdType.MESH)

    def tell_if(wanted, to):
        @pl.when(wanted)
        def _():
            tell(to)

    even = jnp.logical_not(plan.odd)
    inner = jnp.logical_not(plan.at_pole)
    lat, lon, last = plan.lat, plan.lon, plan.last
    tell(plan.east)
    tell(plan.west)
    tell_if(jnp.logical_and(even, lat < last), (lat + 1, lon))
    tell_if(jnp.logical_and(even, lat > 0), (lat - 1, lon))
    tell_if(plan.odd, plan.source)
    tell_if(jnp.logical_and(plan.odd, lat < last), plan.relay_of(lat + 1))
    tell_if(jnp.logical_and(plan.odd, lat > 0), plan.relay_of(lat - 1))
    tell_if(plan.at_pole, plan.far)
    tell_if(inner, (plan.pole, lon))
    tell_if(inner, plan.far)
    tell_if(inner, plan.ring_east)
    tell_if(inner, plan.ring_west)
    to_lat = jnp.where(plan.odd, plan.source[0], lat)
    count = 2 + jnp.where(to_lat < last, 1, 0) + jnp.where(to_lat > 0, 1, 0)
    count = count + jnp.where(plan.odd, 1, 0) + jnp.where(plan.at_pole, 4, 3)
    pl.semaphore_wait(barrier, count)


def exchange_kernel(
    tokens_ref, west_ref, east_ref, halo_ref, west_halo_ref, east_halo_ref, query_ref, cap_ref, relay_ref,
    side_send, side_recv, halo_send, halo_recv, far_send, far_recv, relay_send, relay_recv, corner_send, corner_recv,
    give_send, query_recv, cap_recv, sib_send, sib_recv, ring_send, ring_recv,
):
    plan = Plan()
    lat, lon, last = plan.lat, plan.lon, plan.last
    inner = jnp.logical_not(plan.at_pole)
    even = jnp.logical_not(plan.odd)
    ends = (pl.ds(ROWS - RADIUS, RADIUS), pl.ds(0, RADIUS))
    pairs = (pl.ds(0, RADIUS), pl.ds(RADIUS, RADIUS))
    meet(plan)

    def gifts():
        copies = []
        for r in range(3):
            row, first = plan.cap_row(r), plan.cap_row(0)
            to = plan.helper(r)
            copies.append(remote(
                tokens_ref.at[row], cap_ref.at[plan.place, plan.side], give_send.at[r], cap_recv, to))
            copies.append(remote(tokens_ref.at[first], query_ref, give_send.at[3 + r], query_recv, to))
        return copies

    def far_rows():
        copies = []
        for n in range(RADIUS):
            row = jnp.where(plan.is_north, n, ROWS - 1 - n)
            slot = jnp.where(plan.is_north, RADIUS - 1 - n, RADIUS + n)
            copies.append(remote(
                tokens_ref.at[row], halo_ref.at[slot], far_send.at[n], far_recv.at[n], plan.far))
        return copies

    def lat_rows(n):
        to = (lat + 1 - 2 * n, lon)
        return remote(tokens_ref.at[ends[n]], halo_ref.at[pairs[n]], halo_send.at[n], halo_recv.at[n], to)

    def lat_rows_by_relay(n):
        return remote(tokens_ref.at[ends[n]], relay_ref.at[pairs[n]], halo_send.at[n], relay_recv.at[n], plan.relay)

    def relayed(n):
        to = (plan.source[0] + 1 - 2 * n, plan.source[1])
        return remote(relay_ref.at[pairs[n]], halo_ref.at[pairs[n]], relay_send.at[n], halo_recv.at[n], to)

    def has(n, at):
        return at < last if n == 0 else at > 0

    def when_each(wanted, act):
        for n in range(2):
            @pl.when(wanted(n))
            def _(n=n):
                act(n)

    @pl.when(plan.at_pole)
    def _():
        for copy in gifts() + far_rows():
            copy.start()

    when_each(lambda n: jnp.logical_and(even, has(n, lat)), lambda n: lat_rows(n).start())
    when_each(lambda n: jnp.logical_and(plan.odd, has(n, lat)), lambda n: lat_rows_by_relay(n).start())
    wide = [
        remote(tokens_ref, west_ref, side_send.at[0], side_recv.at[0], plan.east),
        remote(tokens_ref, east_ref, side_send.at[1], side_recv.at[1], plan.west),
    ]
    for copy in wide:
        copy.start()

    def pass_on(n):
        landed(relay_ref.at[pairs[n]], relay_recv.at[n])
        relayed(n).start()

    when_each(lambda n: jnp.logical_and(plan.odd, has(n, plan.source[0])), pass_on)

    mine = cap_ref.at[plan.place, plan.side]
    theirs = cap_ref.at[plan.place, 1 - plan.side]
    sibling = remote(mine, mine, sib_send, sib_recv, plan.far)

    @pl.when(inner)
    def _():
        landed(mine, cap_recv)
        sibling.start()

    count = plan.half
    east_steps, west_steps = count // 2, count // 2 - 1

    def ring(step, eastward):
        shift = count - (step - 1) if eastward else step - 1
        spot = cap_ref.at[lax.rem(plan.place + shift, count)]
        n = 0 if eastward else 1
        return remote(
            spot, spot, ring_send.at[n, step - 1], ring_recv.at[n, step - 1],
            plan.ring_east if eastward else plan.ring_west)

    def got(step, eastward):
        shift = count - step if eastward else step
        spot = cap_ref.at[lax.rem(plan.place + shift, count)]
        landed(spot, ring_recv.at[0 if eastward else 1, step - 1])

    @pl.when(inner)
    def _():
        landed(theirs, sib_recv)
        ring(1, True).start()
        ring(1, False).start()

    when_each(lambda n: has(1 - n, lat), lambda n: landed(halo_ref.at[pairs[n]], halo_recv.at[n]))

    @pl.when(plan.at_pole)
    def _():
        for n in range(RADIUS):
            landed(halo_ref.at[jnp.where(plan.is_north, RADIUS - 1 - n, RADIUS + n)], far_recv.at[n])

    corners = [
        remote(halo_ref, west_halo_ref, corner_send.at[0], corner_recv.at[0], plan.east),
        remote(halo_ref, east_halo_ref, corner_send.at[1], corner_recv.at[1], plan.west),
    ]
    for copy in corners:
        copy.start()

    @pl.when(inner)
    def _():
        for step in range(2, east_steps + 1):
            got(step - 1, True)
            ring(step, True).start()
            if step <= west_steps:
                got(step - 1, False)
                ring(step, False).start()
        got(east_steps, True)
        got(west_steps, False)
        landed(query_ref, query_recv)
        sibling.wait_send()
        for step in range(1, east_steps + 1):
            ring(step, True).wait_send()
            if step <= west_steps:
                ring(step, False).wait_send()

    for copy in wide + corners:
        copy.wait()
    when_each(lambda n: jnp.logical_and(even, has(n, lat)), lambda n: lat_rows(n).wait_send())
    when_each(lambda n: jnp.logical_and(plan.odd, has(n, lat)), lambda n: lat_rows_by_relay(n).wait_send())
    when_each(lambda n: jnp.logical_and(plan.odd, has(n, plan.source[0])), lambda n: relayed(n).wait_send())

    @pl.when(plan.at_pole)
    def _():
        for copy in gifts() + far_rows():
            copy.wait_send()


def per_device(tokens, neighbor_mask, w_query, w_key, w_value, w_out):
    lat_count = lax.axis_size("lat")
    lon_count = lax.axis_size("lon")
    last = lat_count - 1
    params = pltpu.CompilerParams(vmem_limit_bytes=VMEM_LIMIT)
    half = lon_count // 2
    strip = lambda *dims: jax.ShapeDtypeStruct((*dims, BLOCK, WIDTH), BF16)
    dma = pltpu.SemaphoreType.DMA
    west, east, halo, west_halo, east_halo, query_tokens, cap_blocks, _ = pl.pallas_call(
        exchange_kernel,
        out_shape=[
            strip(ROWS), strip(ROWS), strip(4), strip(4), strip(4), strip(), strip(half, 2), strip(4),
        ],
        in_specs=[ANY_SPEC],
        out_specs=[ANY_SPEC] * 8,
        scratch_shapes=[dma((2,))] * 10 + [dma((6,)), dma, dma, dma, dma, dma((2, half // 2)), dma((2, half // 2))],
        compiler_params=pltpu.CompilerParams(collective_id=0, has_side_effects=True),
        name="exchange_tokens",
    )(tokens)
    cap_tokens = cap_blocks.reshape(lon_count * BLOCK, WIDTH)

    lists = [pltpu.SMEM((272,), jnp.int32), pltpu.SMEM((272,), jnp.int32), pltpu.SMEM((2 * ROWS,), jnp.int32)]
    k_shape = lambda n: (n, BLOCK, LANES)
    vt_shape = lambda n: (n, PAIRS, VROWS, BLOCK)
    qd_shape = lambda n: (n, PAIRS, 128, 256)
    acc_shape = lambda n: (n, PAIRS, VROWS, 256)
    square = pltpu.VMEM((WIDTH, WIDTH), BF16)
    wide = pltpu.VMEM((WIDTH, LANES), BF16)
    own = pl.pallas_call(
        own_kernel,
        out_shape=[
            jax.ShapeDtypeStruct(k_shape(ROWS), BF16),
            jax.ShapeDtypeStruct(vt_shape(ROWS), BF16),
            jax.ShapeDtypeStruct(qd_shape(ROWS), BF16),
            jax.ShapeDtypeStruct((ROWS, PAIRS, 48, 128), F32),
            jax.ShapeDtypeStruct((ROWS, PAIRS, 48, 128), F32),
            jax.ShapeDtypeStruct((ROWS, PAIRS, 8, 256), F32),
        ],
        in_specs=[SMEM_SPEC] + [VMEM_SPEC] * 4,
        out_specs=[ANY_SPEC] * 6,
        scratch_shapes=[
            pltpu.VMEM(k_shape(ROWS + 1), BF16),
            pltpu.VMEM(vt_shape(ROWS + 1), BF16),
            pltpu.VMEM(qd_shape(ROWS), BF16),
            pltpu.VMEM(acc_shape(ROWS), F32),
            wide, square, square, *lists,
            pltpu.SemaphoreType.DMA((6,)),
        ],
        compiler_params=params,
        cost_estimate=pl.CostEstimate(flops=8 * 10**9, bytes_accessed=12 * 2**20, transcendentals=0),
        name="own_column",
    )(neighbor_mask, tokens, w_query, w_key, w_value)
    capped = pl.pallas_call(
        cap_kernel,
        out_shape=jax.ShapeDtypeStruct((WIDTH + 2 * HEADS, BLOCK), F32),
        in_specs=[VMEM_SPEC] * 5,
        out_specs=VMEM_SPEC,
        scratch_shapes=[
            pltpu.VMEM(k_shape(lon_count), BF16),
            pltpu.VMEM(vt_shape(lon_count), BF16),
            pltpu.VMEM(qd_shape(1), BF16),
            pltpu.VMEM(acc_shape(1), F32),
            pltpu.VMEM((PAIRS, 8, 256), F32),
            pltpu.VMEM((8, 256), F32),
            wide, square, square,
        ],
        compiler_params=params,
        cost_estimate=pl.CostEstimate(flops=4 * 10**9, bytes_accessed=3 * 2**20, transcendentals=0),
        name="cap_rows",
    )(query_tokens, cap_tokens, w_query, w_key, w_value)
    returned = [
        lax.ppermute(capped, "lat", [(1 + r, 0), (last - 1 - r, last)]) for r in range(3)
    ]
    layer = pl.pallas_call(
        frame_kernel,
        out_shape=jax.ShapeDtypeStruct((ROWS, BLOCK, WIDTH), BF16),
        in_specs=[SMEM_SPEC] + [VMEM_SPEC] * 8 + [ANY_SPEC] * 6,
        out_specs=VMEM_SPEC,
        scratch_shapes=[
            pltpu.VMEM(k_shape(DUMMY + 1), BF16),
            pltpu.VMEM(vt_shape(DUMMY + 1), BF16),
            pltpu.VMEM(qd_shape(ROWS), BF16),
            pltpu.VMEM(acc_shape(ROWS), F32),
            pltpu.VMEM((PAIRS, 8, 256), F32),
            pltpu.VMEM((8, 256), F32),
            wide, square, *lists,
            pltpu.SemaphoreType.DMA((6,)),
        ],
        compiler_params=params,
        cost_estimate=pl.CostEstimate(flops=12 * 10**9, bytes_accessed=16 * 2**20, transcendentals=0),
        name="frame_columns",
    )(neighbor_mask, west, east, halo, west_halo, east_halo, w_key, w_value, w_out, *own)
    return pl.pallas_call(
        join_kernel,
        out_shape=jax.ShapeDtypeStruct((ROWS, BLOCK, WIDTH), BF16),
        in_specs=[SMEM_SPEC] + [VMEM_SPEC] * 4 + [ANY_SPEC],
        out_specs=ANY_SPEC,
        scratch_shapes=[pltpu.VMEM((BLOCK, WIDTH), BF16), pltpu.SemaphoreType.DMA],
        input_output_aliases={5: 0},
        compiler_params=params,
        name="join_cap",
    )(neighbor_mask, *returned, w_out, layer)


def solution(mesh):
    placed = (P("lat", "lon", None), P("lat", None, None), P(), P(), P(), P())
    return jax.shard_map(
        per_device, mesh=mesh, in_specs=placed, out_specs=P("lat", "lon", None), check_vma=False
    )
```

```python
import functools

import jax
import jax.numpy as jnp
from jax import lax
from jax.experimental import pallas as pl
from jax.experimental.pallas import tpu as pltpu
from jax.sharding import PartitionSpec as P

HEADS = 8
HEAD_DIM = 48
PAIRS = 4
WIDTH = 384
BLOCK = 128
ROWS = 12
RADIUS = 2
SPAN = 5
FRAME = ROWS + 2 * RADIUS
SLOTS = 3 * FRAME
VROWS = 112
LANES = 128 * PAIRS
AHEAD = 8
CHUNKS = 3
SCORE_SCALE = HEAD_DIM ** -0.5 * 1.4426950408889634
SUM_LOW = 1e-30
SUM_HIGH = 1e30
VMEM_LIMIT = 56 * 2**20
F32 = jnp.float32
BF16 = jnp.bfloat16
VMEM_SPEC = pl.BlockSpec(memory_space=pltpu.VMEM)
SMEM_SPEC = pl.BlockSpec(memory_space=pltpu.SMEM)
ANY_SPEC = pl.BlockSpec(memory_space=pl.ANY)


def dot(a, b, dims=((1,), (0,))):
    return lax.dot_general(a, b, (dims, ((), ())), preferred_element_type=F32)


def prepare_keys(w_key_ref, wide_ref):
    wide_ref[...] = jnp.zeros_like(wide_ref)
    for p in range(PAIRS):
        wide_ref[:, 128 * p : 128 * p + 96] = w_key_ref[:, 96 * p : 96 * p + 96]


def flipped(ref):
    return ref[...].astype(F32).T.astype(BF16)


def put_keys_values(tokens, slots, wide_ref, value_t_ref, k_ref, vt_ref):
    keys = dot(tokens, wide_ref[...]).astype(BF16)
    values = dot(value_t_ref[...], tokens, ((1,), (1,))).astype(BF16)
    for n, slot in enumerate(slots):
        k_ref[slot] = keys[128 * n : 128 * n + 128]
        for p in range(PAIRS):
            vt_ref[slot, p, 0:96] = values[96 * p : 96 * p + 96, 128 * n : 128 * n + 128]


def put_queries(tokens, rows, query_t_ref, qd_ref):
    queries = dot(query_t_ref[...], tokens, ((1,), (1,))).astype(BF16)
    for n, row in enumerate(rows):
        for p in range(PAIRS):
            part = queries[96 * p : 96 * p + 96, 128 * n : 128 * n + 128]
            qd_ref[row, p, 0:48, 0:128] = part[0:48]
            qd_ref[row, p, 48:96, 128:256] = part[48:96]


def put_ones(vt_ref):
    ones = jnp.ones((VROWS - 96, 128), BF16)

    def body(slot, carry):
        for p in range(PAIRS):
            vt_ref[slot, p, 96:VROWS] = ones
        return carry

    lax.fori_loop(0, vt_ref.shape[0], body, 0)


def safe_row(q, acc_at, begin, end, slot_of, k_ref, vt_ref, qd_ref, acc_ref, top_ref):
    top_ref[...] = jnp.full(top_ref.shape, -jnp.inf, F32)

    def scores(n, p):
        return dot(k_ref[slot_of(n), :, 128 * p : 128 * p + 128], qd_ref[q, p]) * SCORE_SCALE

    def find_top(n, carry):
        for p in range(PAIRS):
            top_ref[p] = jnp.maximum(top_ref[p], jnp.max(scores(n, p), axis=0, keepdims=True))
        return carry

    lax.fori_loop(begin, end, find_top, 0)
    acc_ref[acc_at] = jnp.zeros(acc_ref.shape[1:], F32)

    def add(n, carry):
        for p in range(PAIRS):
            weights = jnp.exp2(scores(n, p) - top_ref[p, 0:1]).astype(BF16)
            acc_ref[acc_at, p] += dot(vt_ref[slot_of(n), p], weights)
        return carry

    lax.fori_loop(begin, end, add, 0)


def sums_hold(sums):
    return jnp.where((sums >= SUM_LOW) & (sums <= SUM_HIGH), 1.0, 0.0)


def normalised(acc_ref, row):
    parts = []
    for p in range(PAIRS):
        sums = 1.0 / acc_ref[row, p, 96:97, :]
        parts.append(acc_ref[row, p, 0:48, 0:128] * sums[:, 0:128])
        parts.append(acc_ref[row, p, 48:96, 128:256] * sums[:, 128:256])
    return jnp.concatenate(parts, axis=0).astype(BF16)


def masked_values(vt_ref, slot, p, bit):
    return vt_ref[slot, p] * jnp.full((VROWS, BLOCK), bit, F32).astype(BF16)


def attend(rows, columns, mask_ref, k_ref, vt_ref, qd_ref, acc_ref):
    tiles = []
    for i in rows:
        blocks = [
            (e * FRAME + i + d, mask_ref[i, d, e].astype(F32)) for e in columns for d in range(SPAN)
        ]
        tiles += [(i, blocks[n : n + 2]) for n in range(0, len(blocks), 2)]
    chunks = [(i, tile, p) for i, tile in tiles for p in range(PAIRS)]

    def scores(chunk):
        i, tile, p = chunk
        keys = [k_ref[slot, :, 128 * p : 128 * p + 128] for slot, _ in tile]
        return dot(jnp.concatenate(keys, axis=0) if len(keys) > 1 else keys[0], qd_ref[i, p])

    def values(chunk, weights):
        i, tile, p = chunk
        parts = [masked_values(vt_ref, slot, p, bit) for slot, bit in tile]
        return dot(jnp.concatenate(parts, axis=1) if len(parts) > 1 else parts[0], weights)

    held = {}
    for step in range(len(chunks) + AHEAD):
        if step < len(chunks):
            held[step] = scores(chunks[step])
        if step >= AHEAD:
            chunk = chunks[step - AHEAD]
            weights = jnp.exp2(held.pop(step - AHEAD) * SCORE_SCALE).astype(BF16)
            acc_ref[chunk[0], chunk[2]] += values(chunk, weights)


def attend_cap(blocks, k_ref, vt_ref, qd_ref, acc_ref, top_ref):
    def scores(p):
        qd = qd_ref[0, p]
        return [
            dot(jnp.concatenate([k_ref[n + m, :, 128 * p : 128 * p + 128] for m in range(2)], axis=0), qd)
            for n in range(0, blocks, 2)
        ]

    def finish(p, tiles):
        tops = [jnp.max(tile, axis=0, keepdims=True) for tile in tiles]
        top = functools.reduce(jnp.maximum, tops) * SCORE_SCALE
        total = None
        for n, tile in enumerate(tiles):
            weights = jnp.exp2(tile * SCORE_SCALE - top).astype(BF16)
            part = dot(jnp.concatenate([vt_ref[2 * n, p], vt_ref[2 * n + 1, p]], axis=1), weights)
            total = part if total is None else total + part
        acc_ref[p] = total
        top_ref[p, 0:1] = top

    held = scores(0)
    for p in range(PAIRS):
        later = scores(p + 1) if p + 1 < PAIRS else None
        finish(p, held)
        held = later


def at_device(lat, lon):
    return {"lat": lat, "lon": lon}


def remote(src, dst, send_sem, recv_sem, to):
    return pltpu.make_async_remote_copy(
        src_ref=src, dst_ref=dst, send_sem=send_sem, recv_sem=recv_sem,
        device_id=at_device(*to), device_id_type=pl.DeviceIdType.MESH,
    )


def landed(dst, sem):
    pltpu.make_async_copy(dst, dst, sem).wait()


class Plan:
    def __init__(self):
        self.lat, self.lon = lat, lon = lax.axis_index("lat"), lax.axis_index("lon")
        self.lon_count, self.last = lax.axis_size("lon"), lax.axis_size("lat") - 1
        self.half = half = self.lon_count // 2
        self.is_north, self.is_south = lat == 0, lat == self.last
        self.at_pole = jnp.logical_or(self.is_north, self.is_south)
        self.inner = jnp.logical_not(self.at_pole)
        self.east = (lat, lax.rem(lon + 1, self.lon_count))
        self.west = (lat, lax.rem(lon + self.lon_count - 1, self.lon_count))
        self.far = (lat, lax.rem(lon + half, self.lon_count))
        self.place = lax.rem(lon, half)
        self.side = lon // half
        base = lon - self.place
        self.ring_east = (lat, base + lax.rem(self.place + 1, half))
        self.ring_west = (lat, base + lax.rem(self.place + half - 1, half))
        north_half = lat < (self.last + 1) // 2
        self.pole = (jnp.where(north_half, 0, self.last), lon)
        self.part = jnp.where(north_half, lat - 1, self.last - 1 - lat)

    def helper(self, r):
        return (jnp.where(self.is_north, 1 + r, self.last - 1 - r), self.lon)

    def cap_row(self, r):
        return jnp.where(self.is_north, r, ROWS - 1 - r)


def tell_senders(plan):
    barrier = pltpu.get_barrier_semaphore()

    def tell(to):
        pl.semaphore_signal(barrier, inc=1, device_id=at_device(*to), device_id_type=pl.DeviceIdType.MESH)

    def tell_if(wanted, targets):
        @pl.when(wanted)
        def _():
            for to in targets:
                tell(to)

    lat, lon = plan.lat, plan.lon
    tell(plan.east)
    tell(plan.west)
    tell_if(lat < plan.last, [(lat + 1, lon)])
    tell_if(lat > 0, [(lat - 1, lon)])
    tell_if(plan.at_pole, [plan.far] + [plan.helper(r) for r in range(3)])
    tell_if(plan.inner, [plan.pole, plan.far, plan.ring_east, plan.ring_west])


def wait_receivers(plan):
    pl.semaphore_wait(pltpu.get_barrier_semaphore(), jnp.where(plan.at_pole, 7, 8))


def grid_kernel(
    mask_ref, tokens_ref, w_query_ref, w_key_ref, w_value_ref,
    mixed_ref, hold_ref, west_out, east_out, halos_out,
    west_ref, east_ref, halos_ref, query_ref, cap_ref, part_ref, back_ref,
    k_ref, vt_ref, qd_ref, acc_ref, cap_k, cap_vt, cap_qd, cap_acc, cap_top, wide_ref, query_t_ref, value_t_ref,
    side_send, side_recv, halo_send, halo_recv, far_send, far_recv, corner_send, corner_recv,
    give_send, query_recv, cap_recv, sib_send, sib_recv, ring_send, ring_recv, part_send, part_recv, keep_sem,
):
    plan = Plan()
    lat, last = plan.lat, plan.last
    ends = (pl.ds(ROWS - RADIUS, RADIUS), pl.ds(0, RADIUS))
    pairs = (pl.ds(0, RADIUS), pl.ds(RADIUS, RADIUS))
    halo_ref, west_halo_ref, east_halo_ref = halos_ref.at[0], halos_ref.at[1], halos_ref.at[2]
    chunk = ROWS // CHUNKS
    count = plan.half
    east_steps, west_steps = count // 2, count // 2 - 1

    tell_senders(plan)
    prepare_keys(w_key_ref, wide_ref)
    query_t_ref[...] = flipped(w_query_ref)
    value_t_ref[...] = flipped(w_value_ref)
    put_ones(vt_ref)
    put_ones(cap_vt)
    qd_ref[...] = jnp.zeros_like(qd_ref)
    cap_qd[...] = jnp.zeros_like(cap_qd)
    acc_ref[...] = jnp.zeros_like(acc_ref)
    hold_ref[...] = jnp.ones_like(hold_ref)
    wait_receivers(plan)

    def gifts():
        copies = []
        for r in range(3):
            to = plan.helper(r)
            copies.append(remote(
                tokens_ref.at[plan.cap_row(r)], cap_ref.at[plan.place, plan.side], give_send.at[r], cap_recv, to))
            copies.append(remote(tokens_ref.at[plan.cap_row(0)], query_ref, give_send.at[3 + r], query_recv, to))
        return copies

    def far_slot(n):
        return jnp.where(plan.is_north, RADIUS - 1 - n, RADIUS + n)

    def far_rows():
        rows = [jnp.where(plan.is_north, n, ROWS - 1 - n) for n in range(RADIUS)]
        return [
            remote(tokens_ref.at[rows[n]], halo_ref.at[far_slot(n)], far_send.at[n], far_recv.at[n], plan.far)
            for n in range(RADIUS)
        ]

    def lat_rows(n):
        to = (lat + 1 - 2 * n, plan.lon)
        return remote(tokens_ref.at[ends[n]], halo_ref.at[pairs[n]], halo_send.at[n], halo_recv.at[n], to)

    def has(n):
        return lat < last if n == 0 else lat > 0

    def when_each(wanted, act):
        for n in range(2):
            @pl.when(wanted(n))
            def _(n=n):
                act(n)

    def side_rows(n):
        part = pl.ds(n * chunk, chunk)
        return [
            remote(tokens_ref.at[part], west_ref.at[part], side_send.at[0, n], side_recv.at[0, n], plan.east),
            remote(tokens_ref.at[part], east_ref.at[part], side_send.at[1, n], side_recv.at[1, n], plan.west),
        ]

    mine = cap_ref.at[plan.place, plan.side]
    theirs = cap_ref.at[plan.place, 1 - plan.side]
    sibling = remote(mine, mine, sib_send, sib_recv, plan.far)

    def ring(step, eastward):
        shift = count - (step - 1) if eastward else step - 1
        spot = cap_ref.at[lax.rem(plan.place + shift, count)]
        n = 0 if eastward else 1
        return remote(
            spot, spot, ring_send.at[n, step - 1], ring_recv.at[n, step - 1],
            plan.ring_east if eastward else plan.ring_west)

    def got(step, eastward):
        shift = count - step if eastward else step
        spot = cap_ref.at[lax.rem(plan.place + shift, count)]
        landed(spot, ring_recv.at[0 if eastward else 1, step - 1])

    def ring_on(step):
        @pl.when(plan.inner)
        def _():
            if step == 0:
                landed(mine, cap_recv)
                sibling.start()
            elif step == 1:
                landed(theirs, sib_recv)
            else:
                got(step - 1, True)
                if step - 1 <= west_steps:
                    got(step - 1, False)
            if 1 <= step <= east_steps:
                ring(step, True).start()
            if 1 <= step <= west_steps:
                ring(step, False).start()

    def take(tokens, slot):
        put_keys_values(
            tokens.reshape(2 * BLOCK, WIDTH), (slot, slot + 1), wide_ref, value_t_ref, k_ref, vt_ref)

    def attend_pairs(first, steps, columns):
        def body(t, carry):
            attend((first + 2 * t, first + 2 * t + 1), columns, mask_ref, k_ref, vt_ref, qd_ref, acc_ref)
            return carry

        lax.fori_loop(0, steps, body, 0)

    def finish(i):
        mixed_ref[i] = normalised(acc_ref, i)
        for p in range(PAIRS):
            hold_ref[0:1] = jnp.minimum(hold_ref[0:1], sums_hold(acc_ref[i, p, 96:97, :]))

    def take_sides(n):
        for copy in side_rows(n):
            copy.wait_recv()

        def body(t, carry):
            row = n * chunk + 2 * t
            take(west_ref[pl.ds(row, 2)], RADIUS + row)
            take(east_ref[pl.ds(row, 2)], 2 * FRAME + RADIUS + row)
            return carry

        lax.fori_loop(0, chunk // 2, body, 0)

    @pl.when(plan.at_pole)
    def _():
        for copy in gifts() + far_rows():
            copy.start()

    when_each(has, lambda n: lat_rows(n).start())
    for copy in side_rows(0):
        copy.start()

    def own(t, carry):
        tokens = tokens_ref[pl.ds(2 * t, 2)].reshape(2 * BLOCK, WIDTH)
        slot = FRAME + RADIUS + 2 * t
        put_keys_values(tokens, (slot, slot + 1), wide_ref, value_t_ref, k_ref, vt_ref)
        put_queries(tokens, (2 * t, 2 * t + 1), query_t_ref, qd_ref)
        return carry

    lax.fori_loop(0, ROWS // 2, own, 0)
    ring_on(0)
    for copy in side_rows(1):
        copy.start()
    attend_pairs(2, 2, (1,))
    ring_on(1)
    attend_pairs(6, 2, (1,))
    ring_on(2)
    for copy in side_rows(2):
        copy.start()
    when_each(lambda n: has(1 - n), lambda n: landed(halo_ref.at[pairs[n]], halo_recv.at[n]))

    @pl.when(plan.at_pole)
    def _():
        for n in range(RADIUS):
            landed(halo_ref.at[far_slot(n)], far_recv.at[n])

    corners = [
        remote(halo_ref, west_halo_ref, corner_send.at[0], corner_recv.at[0], plan.east),
        remote(halo_ref, east_halo_ref, corner_send.at[1], corner_recv.at[1], plan.west),
    ]
    for copy in corners:
        copy.start()

    def take_halo(column, which):
        take(halos_ref[which, 0:2], column * FRAME)
        take(halos_ref[which, 2:4], column * FRAME + ROWS + RADIUS)

    take_halo(1, 0)
    take_sides(0)
    ring_on(3)
    take_sides(1)
    attend_pairs(2, 2, (0, 2))
    ring_on(4)
    take_sides(2)
    keep = [
        pltpu.make_async_copy(west_ref, west_out, keep_sem.at[0]),
        pltpu.make_async_copy(east_ref, east_out, keep_sem.at[1]),
    ]
    for copy in keep:
        copy.start()
    attend_pairs(6, 2, (0, 2))
    ring_on(5)

    def send_part():
        return remote(part_ref, back_ref.at[plan.part], part_send, part_recv.at[plan.part], plan.pole)

    @pl.when(plan.inner)
    def _():
        landed(query_ref, query_recv)
        queries = jnp.concatenate([query_ref[...], query_ref[...]], axis=0)
        put_queries(queries, (0,), query_t_ref, cap_qd)

        def load(t, carry):
            tokens = cap_ref[t].reshape(2 * BLOCK, WIDTH)
            put_keys_values(tokens, (2 * t, 2 * t + 1), wide_ref, value_t_ref, cap_k, cap_vt)
            return carry

        lax.fori_loop(0, count, load, 0)
        attend_cap(2 * count, cap_k, cap_vt, cap_qd, cap_acc, cap_top)
        for p in range(PAIRS):
            part_ref[96 * p : 96 * p + 48] = cap_acc[p, 0:48, 0:128]
            part_ref[96 * p + 48 : 96 * p + 96] = cap_acc[p, 48:96, 128:256]
            for half in range(2):
                lanes = slice(128 * half, 128 * half + 128)
                n = 2 * p + half
                part_ref[WIDTH + n : WIDTH + n + 1] = cap_acc[p, 96:97, lanes]
                part_ref[WIDTH + HEADS + n : WIDTH + HEADS + n + 1] = cap_top[p, 0:1, lanes]
        send_part().start()

    def finish_row(t, carry):
        finish(2 + t)
        return carry

    lax.fori_loop(0, ROWS - 4, finish_row, 0)
    for copy in corners:
        copy.wait_recv()
    keep.append(pltpu.make_async_copy(halos_ref, halos_out, keep_sem.at[2]))
    keep[-1].start()
    take_halo(0, 1)
    take_halo(2, 2)

    def outer(t, carry):
        i = t + (ROWS - 4) * (t // 2)
        polar = jnp.logical_or(
            jnp.logical_and(plan.is_north, i == 0), jnp.logical_and(plan.is_south, i == ROWS - 1))

        @pl.when(jnp.logical_not(polar))
        def _():
            attend((i,), (0, 1, 2), mask_ref, k_ref, vt_ref, qd_ref, acc_ref)
            finish(i)

        return carry

    lax.fori_loop(0, 4, outer, 0)

    @pl.when(plan.at_pole)
    def _():
        row = jnp.where(plan.is_north, 0, ROWS - 1)
        counts = [0, 0, 0]
        for d in range(SPAN):
            north = d - RADIUS if d >= RADIUS else RADIUS - 1 - d
            south = RADIUS - d if d <= RADIUS else d - RADIUS - 1
            bit = mask_ref[row, d, 1].astype(F32)
            for r in range(3):
                hit = jnp.where(plan.is_north, float(north == r), float(south == r))
                counts[r] = counts[r] + bit * hit
        for r in range(3):
            landed(back_ref.at[r], part_recv.at[r])
        sums, tops = pl.ds(WIDTH, HEADS), pl.ds(WIDTH + HEADS, HEADS)
        used = [jnp.full((HEADS, BLOCK), n, F32) for n in counts]
        low = [jnp.where(used[r] > 0.5, back_ref[r, tops], -jnp.inf) for r in range(3)]
        top = jnp.maximum(jnp.maximum(low[0], low[1]), low[2])
        factors = [jnp.exp2(low[r] - top) * used[r] for r in range(3)]
        total = 1.0 / sum(factors[r] * back_ref[r, sums] for r in range(3))
        heads = []
        for h in range(HEADS):
            rows = pl.ds(HEAD_DIM * h, HEAD_DIM)
            heads.append(sum(factors[r][h : h + 1] * back_ref[r, rows] for r in range(3)) * total[h : h + 1])
        mixed_ref[row] = jnp.concatenate(heads, axis=0).astype(BF16)
        for copy in gifts() + far_rows():
            copy.wait_send()

    @pl.when(plan.inner)
    def _():
        sibling.wait_send()
        for step in range(1, east_steps + 1):
            ring(step, True).wait_send()
            if step <= west_steps:
                ring(step, False).wait_send()
        send_part().wait_send()

    when_each(has, lambda n: lat_rows(n).wait_send())
    for n in range(CHUNKS):
        for copy in side_rows(n):
            copy.wait_send()
    for copy in corners:
        copy.wait_send()
    for copy in keep:
        copy.wait()


def output_kernel(
    mask_ref, mixed_ref, hold_ref, w_out_ref, w_query_in, w_key_in, w_value_in, tokens_in, west_in, east_in, halos_in,
    out_ref,
    fixed_ref, strip_ref, weight_ref, k_ref, vt_ref, qd_ref, acc_ref, top_ref, wide_ref, query_t_ref, value_t_ref,
    list_ref, begin_ref, sem,
):
    lat = lax.axis_index("lat")
    last = lax.axis_size("lat") - 1

    def product(from_ref):
        def body(t, carry):
            both = jnp.concatenate([from_ref[2 * t], from_ref[2 * t + 1]], axis=1)
            result = dot(both, w_out_ref[...], ((0,), (0,))).astype(BF16)
            out_ref[pl.ds(2 * t, 2)] = result.reshape(2, BLOCK, WIDTH)
            return carry

        lax.fori_loop(0, ROWS // 2, body, 0, unroll=3)

    product(mixed_ref)
    holds = jnp.min(hold_ref[...]) > 0.5

    @pl.when(jnp.logical_not(holds))
    def _():
        def fetch(src, dst):
            copy = pltpu.make_async_copy(src, dst, sem)
            copy.start()
            copy.wait()

        fetch(w_key_in, weight_ref)
        prepare_keys(weight_ref, wide_ref)
        fetch(w_query_in, weight_ref)
        query_t_ref[...] = flipped(weight_ref)
        fetch(w_value_in, weight_ref)
        value_t_ref[...] = flipped(weight_ref)
        put_ones(vt_ref)
        qd_ref[...] = jnp.zeros_like(qd_ref)

        def take(src, slot):
            fetch(src, strip_ref)
            tokens = strip_ref[...].reshape(2 * BLOCK, WIDTH)
            put_keys_values(tokens, (slot, slot + 1), wide_ref, value_t_ref, k_ref, vt_ref)
            return tokens

        def load(t, carry):
            part = pl.ds(2 * t, 2)
            take(west_in.at[part], RADIUS + 2 * t)
            take(east_in.at[part], 2 * FRAME + RADIUS + 2 * t)
            tokens = take(tokens_in.at[part], FRAME + RADIUS + 2 * t)
            put_queries(tokens, (2 * t, 2 * t + 1), query_t_ref, qd_ref)
            return carry

        lax.fori_loop(0, ROWS // 2, load, 0)
        for column, which in ((1, 0), (0, 1), (2, 2)):
            take(halos_in.at[which, pl.ds(0, 2)], column * FRAME)
            take(halos_in.at[which, pl.ds(2, 2)], column * FRAME + ROWS + RADIUS)
        fixed_ref[...] = mixed_ref[...]

        def again(i, carry):
            pos = jnp.int32(0)
            for d in range(SPAN):
                for e in range(3):
                    list_ref[pos] = e * FRAME + i + d
                    pos = pos + (mask_ref[i, d, e] > 0).astype(jnp.int32)
            begin_ref[0] = pos
            polar = jnp.logical_or(
                jnp.logical_and(lat == 0, i == 0), jnp.logical_and(lat == last, i == ROWS - 1))

            @pl.when(jnp.logical_not(polar))
            def _():
                safe_row(
                    i, 0, 0, begin_ref[0], lambda n: list_ref[n], k_ref, vt_ref, qd_ref, acc_ref, top_ref)
                fixed_ref[i] = normalised(acc_ref, 0)

            return carry

        lax.fori_loop(0, ROWS, again, 0)
        product(fixed_ref)


def per_device(tokens, neighbor_mask, w_query, w_key, w_value, w_out):
    lon_count = lax.axis_size("lon")
    half = lon_count // 2
    strip = lambda *dims: jax.ShapeDtypeStruct((*dims, BLOCK, WIDTH), BF16)
    landing = lambda *dims: pltpu.VMEM((*dims, BLOCK, WIDTH), BF16)
    dma = pltpu.SemaphoreType.DMA
    keys = lambda n: pltpu.VMEM((n, BLOCK, LANES), BF16)
    values = lambda n: pltpu.VMEM((n, PAIRS, VROWS, BLOCK), BF16)
    queries = lambda n: pltpu.VMEM((n, PAIRS, 128, 256), BF16)
    square = pltpu.VMEM((WIDTH, WIDTH), BF16)
    wide = pltpu.VMEM((WIDTH, LANES), BF16)
    tops = pltpu.VMEM((PAIRS, 8, 256), F32)
    mixed = jax.ShapeDtypeStruct((ROWS, WIDTH, BLOCK), BF16)
    mixed, hold, west, east, halos = pl.pallas_call(
        grid_kernel,
        out_shape=[mixed, jax.ShapeDtypeStruct((8, 256), F32), strip(ROWS), strip(ROWS), strip(3, 4)],
        in_specs=[SMEM_SPEC] + [VMEM_SPEC] * 4,
        out_specs=[VMEM_SPEC] * 2 + [ANY_SPEC] * 3,
        scratch_shapes=[
            landing(ROWS), landing(ROWS), landing(3, 4), landing(), landing(half, 2),
            pltpu.VMEM((WIDTH + 2 * HEADS, BLOCK), F32),
            pltpu.VMEM((3, WIDTH + 2 * HEADS, BLOCK), F32),
            keys(SLOTS), values(SLOTS), queries(ROWS),
            pltpu.VMEM((ROWS, PAIRS, VROWS, 256), F32),
            keys(lon_count), values(lon_count), queries(1),
            pltpu.VMEM((PAIRS, VROWS, 256), F32),
            tops, wide, square, square,
            dma((2, CHUNKS)), dma((2, CHUNKS)), dma((2,)), dma((2,)), dma((2,)), dma((2,)), dma((2,)), dma((2,)),
            dma((6,)), dma, dma, dma, dma, dma((2, half // 2)), dma((2, half // 2)), dma, dma((3,)), dma((3,)),
        ],
        compiler_params=pltpu.CompilerParams(
            collective_id=0, has_side_effects=True, vmem_limit_bytes=VMEM_LIMIT),
        name="grid_attention",
    )(neighbor_mask, tokens, w_query, w_key, w_value)
    return pl.pallas_call(
        output_kernel,
        out_shape=strip(ROWS),
        in_specs=[SMEM_SPEC] + [VMEM_SPEC] * 3 + [ANY_SPEC] * 7,
        out_specs=VMEM_SPEC,
        scratch_shapes=[
            pltpu.VMEM((ROWS, WIDTH, BLOCK), BF16), landing(2), square,
            keys(SLOTS), values(SLOTS), queries(ROWS),
            pltpu.VMEM((1, PAIRS, VROWS, 256), F32),
            tops, wide, square, square,
            pltpu.SMEM((SPAN * 3 + 1,), jnp.int32), pltpu.SMEM((1,), jnp.int32), dma,
        ],
        compiler_params=pltpu.CompilerParams(vmem_limit_bytes=VMEM_LIMIT),
        name="output_product",
    )(neighbor_mask, mixed, hold, w_out, w_query, w_key, w_value, tokens, west, east, halos)


def solution(mesh):
    placed = (P("lat", "lon", None), P("lat", None, None), P(), P(), P(), P())
    return jax.shard_map(
        per_device, mesh=mesh, in_specs=placed, out_specs=P("lat", "lon", None), check_vma=False
    )
```

```python
import functools

import jax
import jax.numpy as jnp
from jax import lax
from jax.experimental import pallas as pl
from jax.experimental.pallas import tpu as pltpu
from jax.sharding import PartitionSpec as P

HEADS = 8
HEAD_DIM = 48
PAIRS = 4
WIDTH = 384
BLOCK = 128
ROWS = 12
RADIUS = 2
SPAN = 5
FRAME = ROWS + 2 * RADIUS
SLOTS = 3 * FRAME
VROWS = 112
LANES = 128 * PAIRS
AHEAD = 8
CHUNKS = 3
OUTER_ROWS = (0, 1, ROWS - 2, ROWS - 1)
SCORE_SCALE = HEAD_DIM ** -0.5 * 1.4426950408889634
SUM_LOW = 1e-30
SUM_HIGH = 1e30
VMEM_LIMIT = 56 * 2**20
F32 = jnp.float32
BF16 = jnp.bfloat16
VMEM_SPEC = pl.BlockSpec(memory_space=pltpu.VMEM)
SMEM_SPEC = pl.BlockSpec(memory_space=pltpu.SMEM)
ANY_SPEC = pl.BlockSpec(memory_space=pl.ANY)


def dot(a, b, dims=((1,), (0,))):
    return lax.dot_general(a, b, (dims, ((), ())), preferred_element_type=F32)


def prepare_keys(w_key_ref, wide_ref):
    wide_ref[...] = jnp.zeros_like(wide_ref)
    for p in range(PAIRS):
        wide_ref[:, 128 * p : 128 * p + 96] = w_key_ref[:, 96 * p : 96 * p + 96]


def flipped(ref):
    return ref[...].astype(F32).T.astype(BF16)


def put_tokens(strips, wide_ref, value_t_ref, k_ref, vt_ref):
    keys = [dot(tokens, wide_ref[...]) for tokens, _ in strips]
    values = [dot(value_t_ref[...], tokens, ((1,), (1,))) for tokens, _ in strips]
    for (_, slot), key, value in zip(strips, keys, values):
        key, value = key.astype(BF16), value.astype(BF16)
        for n in range(2):
            k_ref[slot + n] = key[128 * n : 128 * n + 128]
            for p in range(PAIRS):
                vt_ref[slot + n, p, 0:96] = value[96 * p : 96 * p + 96, 128 * n : 128 * n + 128]


def put_queries(strips, query_t_ref, qd_ref):
    queries = [dot(query_t_ref[...], tokens, ((1,), (1,))) for tokens, _ in strips]
    for (_, rows), query in zip(strips, queries):
        query = query.astype(BF16)
        for n, row in enumerate(rows):
            for p in range(PAIRS):
                part = query[96 * p : 96 * p + 96, 128 * n : 128 * n + 128]
                qd_ref[row, p, 0:48, 0:128] = part[0:48]
                qd_ref[row, p, 48:96, 128:256] = part[48:96]


def put_ones(vt_ref):
    ones = jnp.ones((VROWS - 96, 128), BF16)

    def body(slot, carry):
        for p in range(PAIRS):
            vt_ref[slot, p, 96:VROWS] = ones
        return carry

    lax.fori_loop(0, vt_ref.shape[0], body, 0)


def safe_row(q, acc_at, begin, end, slot_of, k_ref, vt_ref, qd_ref, acc_ref, top_ref):
    top_ref[...] = jnp.full(top_ref.shape, -jnp.inf, F32)

    def scores(n, p):
        return dot(k_ref[slot_of(n), :, 128 * p : 128 * p + 128], qd_ref[q, p]) * SCORE_SCALE

    def find_top(n, carry):
        for p in range(PAIRS):
            top_ref[p] = jnp.maximum(top_ref[p], jnp.max(scores(n, p), axis=0, keepdims=True))
        return carry

    lax.fori_loop(begin, end, find_top, 0)
    acc_ref[acc_at] = jnp.zeros(acc_ref.shape[1:], F32)

    def add(n, carry):
        for p in range(PAIRS):
            weights = jnp.exp2(scores(n, p) - top_ref[p, 0:1]).astype(BF16)
            acc_ref[acc_at, p] += dot(vt_ref[slot_of(n), p], weights)
        return carry

    lax.fori_loop(begin, end, add, 0)


def sums_hold(sums):
    return jnp.where((sums >= SUM_LOW) & (sums <= SUM_HIGH), 1.0, 0.0)


def normalised(acc_ref, row):
    parts = []
    for p in range(PAIRS):
        sums = 1.0 / acc_ref[row, p, 96:97, :]
        parts.append(acc_ref[row, p, 0:48, 0:128] * sums[:, 0:128])
        parts.append(acc_ref[row, p, 48:96, 128:256] * sums[:, 128:256])
    return jnp.concatenate(parts, axis=0).astype(BF16)


def masked_values(vt_ref, slot, p, bit):
    return vt_ref[slot, p] * jnp.full((VROWS, BLOCK), bit, F32).astype(BF16)


def attend(work, fresh, mask_ref, k_ref, vt_ref, qd_ref, acc_ref):
    tiles = []
    for i, blocks in work:
        known = [(e * FRAME + i + d, mask_ref[i, d, e].astype(F32)) for d, e in blocks]
        tiles += [(i, known[n : n + 2], fresh and n == 0) for n in range(0, len(known), 2)]
    chunks = [(i, tile, p, begin) for i, tile, begin in tiles for p in range(PAIRS)]

    def scores(chunk):
        i, tile, p, _ = chunk
        keys = [k_ref[slot, :, 128 * p : 128 * p + 128] for slot, _ in tile]
        return dot(jnp.concatenate(keys, axis=0) if len(keys) > 1 else keys[0], qd_ref[i, p])

    def values(chunk, weights):
        i, tile, p, _ = chunk
        parts = [masked_values(vt_ref, slot, p, bit) for slot, bit in tile]
        return dot(jnp.concatenate(parts, axis=1) if len(parts) > 1 else parts[0], weights)

    held = {}
    for step in range(len(chunks) + AHEAD):
        if step < len(chunks):
            held[step] = scores(chunks[step])
        if step >= AHEAD:
            chunk = chunks[step - AHEAD]
            i, _, p, begin = chunk
            weights = jnp.exp2(held.pop(step - AHEAD) * SCORE_SCALE).astype(BF16)
            if begin:
                acc_ref[i, p] = values(chunk, weights)
            else:
                acc_ref[i, p] += values(chunk, weights)


def attend_cap(blocks, k_ref, vt_ref, qd_ref, acc_ref, top_ref):
    def scores(q, p):
        qd = qd_ref[q, p]
        return [
            dot(jnp.concatenate([k_ref[n + m, :, 128 * p : 128 * p + 128] for m in range(2)], axis=0), qd)
            for n in range(0, blocks, 2)
        ]

    def finish(q, p, tiles):
        tops = [jnp.max(tile, axis=0, keepdims=True) for tile in tiles]
        top = functools.reduce(jnp.maximum, tops) * SCORE_SCALE
        total = None
        for n, tile in enumerate(tiles):
            weights = jnp.exp2(tile * SCORE_SCALE - top).astype(BF16)
            part = dot(jnp.concatenate([vt_ref[2 * n, p], vt_ref[2 * n + 1, p]], axis=1), weights)
            total = part if total is None else total + part
        acc_ref[q, p] = total
        top_ref[q, p, 0:1] = top

    turns = [(q, p) for p in range(PAIRS) for q in range(2)]
    held = []
    for n, turn in enumerate(turns + [None, None]):
        if turn is not None:
            held.append(scores(*turn))
        if n >= 2:
            finish(*turns[n - 2], held.pop(0))


def at_device(lat, lon):
    return {"lat": lat, "lon": lon}


def remote(src, dst, send_sem, recv_sem, to):
    return pltpu.make_async_remote_copy(
        src_ref=src, dst_ref=dst, send_sem=send_sem, recv_sem=recv_sem,
        device_id=at_device(*to), device_id_type=pl.DeviceIdType.MESH,
    )


def landed(dst, sem):
    pltpu.make_async_copy(dst, dst, sem).wait()


class Plan:
    def __init__(self):
        self.lat, self.lon = lat, lon = lax.axis_index("lat"), lax.axis_index("lon")
        self.lon_count, self.last = lax.axis_size("lon"), lax.axis_size("lat") - 1
        self.half = half = self.lon_count // 2
        self.is_north, self.is_south = lat == 0, lat == self.last
        self.at_pole = jnp.logical_or(self.is_north, self.is_south)
        self.inner = jnp.logical_not(self.at_pole)
        self.east = (lat, lax.rem(lon + 1, self.lon_count))
        self.west = (lat, lax.rem(lon + self.lon_count - 1, self.lon_count))
        self.far = (lat, lax.rem(lon + half, self.lon_count))
        self.side = lon // half
        self.y, self.core = lax.rem(lon, half) // 2, lax.rem(lon, 2)
        self.y_count = half // 2
        self.crosses_east, self.crosses_west = lax.rem(lon, half) == half - 1, lax.rem(lon, half) == 0
        self.other_core = (lat, lon + 1 - 2 * self.core)
        self.z_count = (self.last + 1) // 2
        south = lax.rem(lat, 2)
        self.pole = (jnp.where(south == 1, self.last, 0), lon)
        away = jnp.where(south == 1, self.z_count - 1 - lat // 2, lat // 2)
        self.part = jnp.where(away == 1, 0, jnp.where(away == 2, 2, 1))

    def along_y(self, step):
        y = lax.rem(self.y + step, self.y_count)
        return (self.lat, self.side * self.half + 2 * y + self.core)

    def helper(self, r, lon=None):
        away = (1, self.z_count - 1, 2)[r]
        return (jnp.where(self.is_north, 2 * away, self.last - 2 * away), self.lon if lon is None else lon)

    def cap_row(self, r):
        return jnp.where(self.is_north, r, ROWS - 1 - r)


def tell_senders(plan):
    barrier = pltpu.get_barrier_semaphore()

    def tell(to):
        pl.semaphore_signal(barrier, inc=1, device_id=at_device(*to), device_id_type=pl.DeviceIdType.MESH)

    def tell_if(wanted, targets):
        @pl.when(wanted)
        def _():
            for to in targets:
                tell(to)

    lat, lon = plan.lat, plan.lon
    tell(plan.east)
    tell(plan.west)
    tell_if(lat < plan.last, [(lat + 1, lon)])
    tell_if(lat > 0, [(lat - 1, lon)])
    tell_if(plan.at_pole, [plan.far] + [plan.helper(r, at) for r in range(3) for at in (lon, plan.far[1])])
    tell_if(plan.inner, [plan.pole, plan.far, plan.other_core] + [plan.along_y(n) for n in (1, 2, 3)])


def wait_receivers(plan):
    pl.semaphore_wait(pltpu.get_barrier_semaphore(), jnp.where(plan.at_pole, 7, 11))


def grid_kernel(
    mask_ref, tokens_ref, w_query_ref, w_key_ref, w_value_ref,
    mixed_ref, hold_ref, west_out, east_out, halos_out,
    west_ref, east_ref, halos_ref, query_ref, cap_ref, part_ref, stat_ref, back_ref, back_stat_ref,
    k_ref, vt_ref, qd_ref, acc_ref, cap_k, cap_vt, cap_qd, cap_acc, cap_top, wide_ref, query_t_ref, value_t_ref,
    side_send, side_recv, halo_send, halo_recv, far_send, far_recv, corner_send, corner_recv,
    give_send, query_recv, cap_recv, sib_send, sib_recv, y_send, y_recv, core_send, core_recv, part_send, part_recv, stat_send, stat_recv, keep_sem,
):
    plan = Plan()
    lat, last = plan.lat, plan.last
    ends = (pl.ds(ROWS - RADIUS, RADIUS), pl.ds(0, RADIUS))
    pairs = (pl.ds(0, RADIUS), pl.ds(RADIUS, RADIUS))
    halo_ref, west_halo_ref, east_halo_ref = halos_ref.at[0], halos_ref.at[1], halos_ref.at[2]
    chunk = ROWS // CHUNKS
    y_count = plan.y_count

    tell_senders(plan)
    prepare_keys(w_key_ref, wide_ref)
    query_t_ref[...] = flipped(w_query_ref)
    value_t_ref[...] = flipped(w_value_ref)
    put_ones(vt_ref)
    put_ones(cap_vt)
    qd_ref[...] = jnp.zeros_like(qd_ref)
    cap_qd[...] = jnp.zeros_like(cap_qd)
    hold_ref[...] = jnp.ones_like(hold_ref)
    wait_receivers(plan)

    def gifts():
        keys = [
            remote(tokens_ref.at[plan.cap_row(r)], cap_ref.at[plan.core, plan.y], give_send.at[r], cap_recv, plan.helper(r))
            for r in range(3)
        ]
        queries = [
            remote(tokens_ref.at[plan.cap_row(0)], query_ref.at[0], give_send.at[3 + r], query_recv, plan.helper(r))
            for r in range(3)
        ]
        return keys + queries

    def far_slot(n):
        return jnp.where(plan.is_north, RADIUS - 1 - n, RADIUS + n)

    def far_rows():
        rows = [jnp.where(plan.is_north, n, ROWS - 1 - n) for n in range(RADIUS)]
        return [
            remote(tokens_ref.at[rows[n]], halo_ref.at[far_slot(n)], far_send.at[n], far_recv.at[n], plan.far)
            for n in range(RADIUS)
        ]

    def lat_rows(n):
        to = (lat + 1 - 2 * n, plan.lon)
        return remote(tokens_ref.at[ends[n]], halo_ref.at[pairs[n]], halo_send.at[n], halo_recv.at[n], to)

    def has(n):
        return lat < last if n == 0 else lat > 0

    def when_each(wanted, act):
        for n in range(2):
            @pl.when(wanted(n))
            def _(n=n):
                act(n)

    def side_rows(n):
        part = pl.ds(n * chunk, chunk)
        return [
            remote(tokens_ref.at[part], west_ref.at[part], side_send.at[0, n], side_recv.at[0, n], plan.east),
            remote(tokens_ref.at[part], east_ref.at[part], side_send.at[1, n], side_recv.at[1, n], plan.west),
        ]

    mine = cap_ref.at[plan.core, plan.y]
    sibling = remote(query_ref.at[0], query_ref.at[1], sib_send, sib_recv, plan.far)

    def along_y(step):
        spot = cap_ref.at[plan.core, plan.y]
        return remote(spot, spot, y_send.at[step], y_recv.at[step], plan.along_y(step))

    def to_core(step):
        spot = cap_ref.at[plan.core, lax.rem(plan.y + y_count - step, y_count)]
        return remote(spot, spot, core_send.at[step], core_recv.at[step], plan.other_core)

    def from_y(step):
        landed(cap_ref.at[plan.core, lax.rem(plan.y + y_count - step, y_count)], y_recv.at[step])

    def from_core(step):
        landed(cap_ref.at[1 - plan.core, lax.rem(plan.y + y_count - step, y_count)], core_recv.at[step])

    def cap_stage(stage):
        @pl.when(plan.inner)
        def _():
            if stage == 0:
                landed(mine, cap_recv)
                for step in range(1, y_count):
                    along_y(step).start()
                to_core(0).start()
            if stage == 1:
                landed(query_ref.at[0], query_recv)
                sibling.start()
            if stage == 2:
                for step in range(1, y_count):
                    from_y(step)
                    to_core(step).start()
            if stage == 3:
                for step in range(y_count):
                    from_core(step)
                landed(query_ref.at[1], sib_recv)

    def put(strips):
        put_tokens([(tokens.reshape(2 * BLOCK, WIDTH), slot) for tokens, slot in strips], wide_ref, value_t_ref, k_ref, vt_ref)

    def add(work, fresh=False):
        attend(work, fresh, mask_ref, k_ref, vt_ref, qd_ref, acc_ref)

    def add_rows(first, count, columns, fresh=False):
        blocks = [(d, e) for e in columns for d in range(SPAN)]
        add([(first + n, blocks) for n in range(count)], fresh)

    def outer_work(columns, inside):
        work = []
        for i in OUTER_ROWS:
            reach = [d for d in range(SPAN) if (0 <= i + d - RADIUS < ROWS) == inside]
            work.append((i, [(d, e) for e in columns for d in reach]))
        return work

    def finish(i):
        mixed_ref[i] = normalised(acc_ref, i)
        for p in range(PAIRS):
            hold_ref[0:1] = jnp.minimum(hold_ref[0:1], sums_hold(acc_ref[i, p, 96:97, :]))

    def take_sides(n):
        for copy in side_rows(n):
            copy.wait_recv()
        strips = []
        for row in range(n * chunk, n * chunk + chunk, 2):
            strips.append((west_ref[row : row + 2], RADIUS + row))
            strips.append((east_ref[row : row + 2], 2 * FRAME + RADIUS + row))
        put(strips)

    def halo_strips(column, which):
        return [
            (halos_ref[which, 0:2], column * FRAME), (halos_ref[which, 2:4], column * FRAME + ROWS + RADIUS)]

    @pl.when(plan.at_pole)
    def _():
        for copy in gifts() + far_rows():
            copy.start()

    when_each(has, lambda n: lat_rows(n).start())
    crossing = (plan.crosses_east, plan.crosses_west)
    for n in range(CHUNKS):
        for copy, crosses in zip(side_rows(n), crossing):
            pl.when(jnp.logical_or(crosses, n == 0))(copy.start)

    def start_others(n):
        for copy, crosses in zip(side_rows(n), crossing):
            pl.when(jnp.logical_not(crosses))(copy.start)

    def own(t, carry):
        first = [4 * t, 4 * t + 2]
        strips = [tokens_ref[pl.ds(n, 2)] for n in first]
        put([(tokens, FRAME + RADIUS + n) for tokens, n in zip(strips, first)])
        put_queries(
            [(tokens.reshape(2 * BLOCK, WIDTH), (n, n + 1)) for tokens, n in zip(strips, first)], query_t_ref, qd_ref)
        return carry

    lax.fori_loop(0, ROWS // 4, own, 0)
    cap_stage(0)
    add_rows(2, 4, (1,), True)
    cap_stage(1)
    start_others(1)
    add_rows(6, 4, (1,), True)
    start_others(2)
    add(outer_work((1,), True), True)
    take_sides(0)
    cap_stage(2)
    when_each(lambda n: has(1 - n), lambda n: landed(halo_ref.at[pairs[n]], halo_recv.at[n]))

    @pl.when(plan.at_pole)
    def _():
        for n in range(RADIUS):
            landed(halo_ref.at[far_slot(n)], far_recv.at[n])

    corners = [
        remote(halo_ref, west_halo_ref, corner_send.at[0], corner_recv.at[0], plan.east),
        remote(halo_ref, east_halo_ref, corner_send.at[1], corner_recv.at[1], plan.west),
    ]
    for copy in corners:
        copy.start()
    put(halo_strips(1, 0))
    take_sides(1)
    add_rows(2, 4, (0, 2))
    cap_stage(3)

    def send_parts():
        copies = []
        for q, to in enumerate((plan.pole, (plan.pole[0], plan.far[1]))):
            copies.append(remote(
                part_ref.at[q], back_ref.at[plan.part, q], part_send.at[q], part_recv.at[plan.part, q], to))
            copies.append(remote(
                stat_ref.at[q], back_stat_ref.at[plan.part, q], stat_send.at[q], stat_recv.at[plan.part, q], to))
        return copies

    @pl.when(plan.inner)
    def _():
        put_queries([(query_ref[...].reshape(2 * BLOCK, WIDTH), (0, 1))], query_t_ref, cap_qd)
        strips = [
            (cap_ref[core].reshape(y_count // 2, 2 * BLOCK, WIDTH)[n], core * y_count + 2 * n)
            for core in range(2) for n in range(y_count // 2)
        ]
        put_tokens(strips, wide_ref, value_t_ref, cap_k, cap_vt)
        attend_cap(2 * y_count, cap_k, cap_vt, cap_qd, cap_acc, cap_top)
        for q in range(2):
            for p in range(PAIRS):
                part_ref[q, 96 * p : 96 * p + 48] = cap_acc[q, p, 0:48, 0:128].astype(BF16)
                part_ref[q, 96 * p + 48 : 96 * p + 96] = cap_acc[q, p, 48:96, 128:256].astype(BF16)
                for half in range(2):
                    lanes = slice(128 * half, 128 * half + 128)
                    n = 2 * p + half
                    stat_ref[q, n : n + 1] = cap_acc[q, p, 96:97, lanes]
                    stat_ref[q, HEADS + n : HEADS + n + 1] = cap_top[q, p, 0:1, lanes]
        for copy in send_parts():
            copy.start()

    take_sides(2)
    keep = [
        pltpu.make_async_copy(west_ref, west_out, keep_sem.at[0]),
        pltpu.make_async_copy(east_ref, east_out, keep_sem.at[1]),
    ]
    for copy in keep:
        copy.start()
    add_rows(6, 4, (0, 2))
    add(outer_work((0, 2), True))
    add(outer_work((1,), False))

    def finish_row(t, carry):
        finish(2 + t)
        return carry

    lax.fori_loop(0, ROWS - 4, finish_row, 0)
    for copy in corners:
        copy.wait_recv()
    keep.append(pltpu.make_async_copy(halos_ref, halos_out, keep_sem.at[2]))
    keep[-1].start()
    put(halo_strips(0, 1) + halo_strips(2, 2))
    add(outer_work((0, 2), False))
    for i in OUTER_ROWS:
        finish(i)

    @pl.when(plan.at_pole)
    def _():
        row = jnp.where(plan.is_north, 0, ROWS - 1)
        counts = [0, 0, 0]
        for d in range(SPAN):
            north = d - RADIUS if d >= RADIUS else RADIUS - 1 - d
            south = RADIUS - d if d <= RADIUS else d - RADIUS - 1
            bit = mask_ref[row, d, 1].astype(F32)
            for r in range(3):
                hit = jnp.where(plan.is_north, float(north == r), float(south == r))
                counts[r] = counts[r] + bit * hit
        parts = [(r, q) for r in range(3) for q in range(2)]
        for r, q in parts:
            landed(back_stat_ref.at[r, q], stat_recv.at[r, q])
            landed(back_ref.at[r, q], part_recv.at[r, q])
        sums, tops = pl.ds(0, HEADS), pl.ds(HEADS, HEADS)
        used = [jnp.full((HEADS, BLOCK), counts[r], F32) for r, _ in parts]
        low = [jnp.where(n > 0.5, back_stat_ref[r, q, tops], -jnp.inf) for n, (r, q) in zip(used, parts)]
        top = functools.reduce(jnp.maximum, low)
        factors = [jnp.exp2(t - top) * n for t, n in zip(low, used)]
        total = 1.0 / sum(f * back_stat_ref[r, q, sums] for f, (r, q) in zip(factors, parts))
        heads = []
        for h in range(HEADS):
            rows = pl.ds(HEAD_DIM * h, HEAD_DIM)
            heads.append(
                sum(f[h : h + 1] * back_ref[r, q, rows].astype(F32) for f, (r, q) in zip(factors, parts))
                * total[h : h + 1])
        mixed_ref[row] = jnp.concatenate(heads, axis=0).astype(BF16)
        for copy in gifts() + far_rows():
            copy.wait_send()

    @pl.when(plan.inner)
    def _():
        sibling.wait_send()
        for step in range(y_count):
            to_core(step).wait_send()
            if step > 0:
                along_y(step).wait_send()
        for copy in send_parts():
            copy.wait_send()

    when_each(has, lambda n: lat_rows(n).wait_send())
    for n in range(CHUNKS):
        for copy in side_rows(n):
            copy.wait_send()
    for copy in corners:
        copy.wait_send()
    for copy in keep:
        copy.wait()


def output_kernel(
    mask_ref, mixed_ref, hold_ref, w_out_ref, w_query_in, w_key_in, w_value_in, tokens_in, west_in, east_in, halos_in,
    out_ref,
    fixed_ref, strip_ref, weight_ref, k_ref, vt_ref, qd_ref, acc_ref, top_ref, wide_ref, query_t_ref, value_t_ref,
    list_ref, begin_ref, sem,
):
    lat = lax.axis_index("lat")
    last = lax.axis_size("lat") - 1

    def product(from_ref):
        def body(t, carry):
            both = jnp.concatenate([from_ref[2 * t], from_ref[2 * t + 1]], axis=1)
            result = dot(both, w_out_ref[...], ((0,), (0,))).astype(BF16)
            out_ref[pl.ds(2 * t, 2)] = result.reshape(2, BLOCK, WIDTH)
            return carry

        lax.fori_loop(0, ROWS // 2, body, 0, unroll=3)

    product(mixed_ref)
    holds = jnp.min(hold_ref[...]) > 0.5

    @pl.when(jnp.logical_not(holds))
    def _():
        def fetch(src, dst):
            copy = pltpu.make_async_copy(src, dst, sem)
            copy.start()
            copy.wait()

        fetch(w_key_in, weight_ref)
        prepare_keys(weight_ref, wide_ref)
        fetch(w_query_in, weight_ref)
        query_t_ref[...] = flipped(weight_ref)
        fetch(w_value_in, weight_ref)
        value_t_ref[...] = flipped(weight_ref)
        put_ones(vt_ref)
        qd_ref[...] = jnp.zeros_like(qd_ref)

        def take(src, slot):
            fetch(src, strip_ref)
            tokens = strip_ref[...].reshape(2 * BLOCK, WIDTH)
            put_tokens([(tokens, slot)], wide_ref, value_t_ref, k_ref, vt_ref)
            return tokens

        def load(t, carry):
            part = pl.ds(2 * t, 2)
            take(west_in.at[part], RADIUS + 2 * t)
            take(east_in.at[part], 2 * FRAME + RADIUS + 2 * t)
            tokens = take(tokens_in.at[part], FRAME + RADIUS + 2 * t)
            put_queries([(tokens, (2 * t, 2 * t + 1))], query_t_ref, qd_ref)
            return carry

        lax.fori_loop(0, ROWS // 2, load, 0)
        for column, which in ((1, 0), (0, 1), (2, 2)):
            take(halos_in.at[which, pl.ds(0, 2)], column * FRAME)
            take(halos_in.at[which, pl.ds(2, 2)], column * FRAME + ROWS + RADIUS)
        fixed_ref[...] = mixed_ref[...]

        def again(i, carry):
            pos = jnp.int32(0)
            for d in range(SPAN):
                for e in range(3):
                    list_ref[pos] = e * FRAME + i + d
                    pos = pos + (mask_ref[i, d, e] > 0).astype(jnp.int32)
            begin_ref[0] = pos
            polar = jnp.logical_or(
                jnp.logical_and(lat == 0, i == 0), jnp.logical_and(lat == last, i == ROWS - 1))

            @pl.when(jnp.logical_not(polar))
            def _():
                safe_row(
                    i, 0, 0, begin_ref[0], lambda n: list_ref[n], k_ref, vt_ref, qd_ref, acc_ref, top_ref)
                fixed_ref[i] = normalised(acc_ref, 0)

            return carry

        lax.fori_loop(0, ROWS, again, 0)
        product(fixed_ref)


def per_device(tokens, neighbor_mask, w_query, w_key, w_value, w_out):
    lon_count = lax.axis_size("lon")
    half = lon_count // 2
    strip = lambda *dims: jax.ShapeDtypeStruct((*dims, BLOCK, WIDTH), BF16)
    landing = lambda *dims: pltpu.VMEM((*dims, BLOCK, WIDTH), BF16)
    dma = pltpu.SemaphoreType.DMA
    keys = lambda n: pltpu.VMEM((n, BLOCK, LANES), BF16)
    values = lambda n: pltpu.VMEM((n, PAIRS, VROWS, BLOCK), BF16)
    queries = lambda n: pltpu.VMEM((n, PAIRS, 128, 256), BF16)
    square = pltpu.VMEM((WIDTH, WIDTH), BF16)
    wide = pltpu.VMEM((WIDTH, LANES), BF16)
    tops = pltpu.VMEM((PAIRS, 8, 256), F32)
    mixed = jax.ShapeDtypeStruct((ROWS, WIDTH, BLOCK), BF16)
    mixed, hold, west, east, halos = pl.pallas_call(
        grid_kernel,
        out_shape=[mixed, jax.ShapeDtypeStruct((8, 256), F32), strip(ROWS), strip(ROWS), strip(3, 4)],
        in_specs=[SMEM_SPEC] + [VMEM_SPEC] * 4,
        out_specs=[VMEM_SPEC] * 2 + [ANY_SPEC] * 3,
        scratch_shapes=[
            landing(ROWS), landing(ROWS), landing(3, 4), landing(2), landing(2, half // 2),
            pltpu.VMEM((2, WIDTH, BLOCK), BF16), pltpu.VMEM((2, 2 * HEADS, BLOCK), F32),
            pltpu.VMEM((3, 2, WIDTH, BLOCK), BF16), pltpu.VMEM((3, 2, 2 * HEADS, BLOCK), F32),
            keys(SLOTS), values(SLOTS), queries(ROWS),
            pltpu.VMEM((ROWS, PAIRS, VROWS, 256), F32),
            keys(half), values(half), queries(2),
            pltpu.VMEM((2, PAIRS, VROWS, 256), F32), pltpu.VMEM((2, PAIRS, 8, 256), F32),
            wide, square, square,
            dma((2, CHUNKS)), dma((2, CHUNKS)), dma((2,)), dma((2,)), dma((2,)), dma((2,)), dma((2,)), dma((2,)),
            dma((6,)), dma, dma, dma, dma, *[dma((half // 2,))] * 4,
            dma((2,)), dma((3, 2)), dma((2,)), dma((3, 2)), dma((3,)),
        ],
        compiler_params=pltpu.CompilerParams(
            collective_id=0, has_side_effects=True, vmem_limit_bytes=VMEM_LIMIT),
        name="grid_attention",
    )(neighbor_mask, tokens, w_query, w_key, w_value)
    return pl.pallas_call(
        output_kernel,
        out_shape=strip(ROWS),
        in_specs=[SMEM_SPEC] + [VMEM_SPEC] * 3 + [ANY_SPEC] * 7,
        out_specs=VMEM_SPEC,
        scratch_shapes=[
            pltpu.VMEM((ROWS, WIDTH, BLOCK), BF16), landing(2), square,
            keys(SLOTS), values(SLOTS), queries(ROWS),
            pltpu.VMEM((1, PAIRS, VROWS, 256), F32),
            tops, wide, square, square,
            pltpu.SMEM((SPAN * 3 + 1,), jnp.int32), pltpu.SMEM((1,), jnp.int32), dma,
        ],
        compiler_params=pltpu.CompilerParams(vmem_limit_bytes=VMEM_LIMIT),
        name="output_product",
    )(neighbor_mask, mixed, hold, w_out, w_query, w_key, w_value, tokens, west, east, halos)


def solution(mesh):
    placed = (P("lat", "lon", None), P("lat", None, None), P(), P(), P(), P())
    return jax.shard_map(
        per_device, mesh=mesh, in_specs=placed, out_specs=P("lat", "lon", None), check_vma=False
    )
```

```python
import functools

import jax
import jax.numpy as jnp
from jax import lax
from jax.experimental import pallas as pl
from jax.experimental.pallas import tpu as pltpu
from jax.sharding import PartitionSpec as P

HEADS = 8
HEAD_DIM = 48
PAIRS = 4
WIDTH = 384
BLOCK = 128
ROWS = 12
RADIUS = 2
SPAN = 5
FRAME = ROWS + 2 * RADIUS
SLOTS = 3 * FRAME
VROWS = 112
LANES = 128 * PAIRS
AHEAD = 8
CHUNKS = 3
OUTER_ROWS = (0, 1, ROWS - 2, ROWS - 1)
SCORE_SCALE = HEAD_DIM ** -0.5 * 1.4426950408889634
SUM_LOW = 1e-30
SUM_HIGH = 1e30
VMEM_LIMIT = 56 * 2**20
F32 = jnp.float32
BF16 = jnp.bfloat16
VMEM_SPEC = pl.BlockSpec(memory_space=pltpu.VMEM)
SMEM_SPEC = pl.BlockSpec(memory_space=pltpu.SMEM)
ANY_SPEC = pl.BlockSpec(memory_space=pl.ANY)


def dot(a, b, dims=((1,), (0,))):
    return lax.dot_general(a, b, (dims, ((), ())), preferred_element_type=F32)


def prepare_keys(w_key_ref, wide_ref):
    wide_ref[...] = jnp.zeros_like(wide_ref)
    for p in range(PAIRS):
        wide_ref[:, 128 * p : 128 * p + 96] = w_key_ref[:, 96 * p : 96 * p + 96]


def flipped(ref):
    return ref[...].astype(F32).T.astype(BF16)


def put_tokens(strips, wide_ref, value_t_ref, k_ref, vt_ref):
    keys = [dot(tokens, wide_ref[...]) for tokens, _ in strips]
    values = [dot(value_t_ref[...], tokens, ((1,), (1,))) for tokens, _ in strips]
    for (_, slot), key, value in zip(strips, keys, values):
        key, value = key.astype(BF16), value.astype(BF16)
        for n in range(2):
            k_ref[slot + n] = key[128 * n : 128 * n + 128]
            for p in range(PAIRS):
                vt_ref[slot + n, p, 0:96] = value[96 * p : 96 * p + 96, 128 * n : 128 * n + 128]


def put_queries(strips, query_t_ref, qd_ref):
    queries = [dot(query_t_ref[...], tokens, ((1,), (1,))) for tokens, _ in strips]
    for (_, rows), query in zip(strips, queries):
        query = query.astype(BF16)
        for n, row in enumerate(rows):
            for p in range(PAIRS):
                part = query[96 * p : 96 * p + 96, 128 * n : 128 * n + 128]
                qd_ref[row, p, 0:48, 0:128] = part[0:48]
                qd_ref[row, p, 48:96, 128:256] = part[48:96]


def put_ones(vt_ref):
    ones = jnp.ones((VROWS - 96, 128), BF16)

    def body(slot, carry):
        for p in range(PAIRS):
            vt_ref[slot, p, 96:VROWS] = ones
        return carry

    lax.fori_loop(0, vt_ref.shape[0], body, 0)


def safe_row(q, acc_at, begin, end, slot_of, k_ref, vt_ref, qd_ref, acc_ref, top_ref):
    top_ref[...] = jnp.full(top_ref.shape, -jnp.inf, F32)

    def scores(n, p):
        return dot(k_ref[slot_of(n), :, 128 * p : 128 * p + 128], qd_ref[q, p]) * SCORE_SCALE

    def find_top(n, carry):
        for p in range(PAIRS):
            top_ref[p] = jnp.maximum(top_ref[p], jnp.max(scores(n, p), axis=0, keepdims=True))
        return carry

    lax.fori_loop(begin, end, find_top, 0)
    acc_ref[acc_at] = jnp.zeros(acc_ref.shape[1:], F32)

    def add(n, carry):
        for p in range(PAIRS):
            weights = jnp.exp2(scores(n, p) - top_ref[p, 0:1]).astype(BF16)
            acc_ref[acc_at, p] += dot(vt_ref[slot_of(n), p], weights)
        return carry

    lax.fori_loop(begin, end, add, 0)


def sums_hold(sums):
    return jnp.where((sums >= SUM_LOW) & (sums <= SUM_HIGH), 1.0, 0.0)


def normalised(acc_ref, row):
    parts = []
    for p in range(PAIRS):
        sums = 1.0 / acc_ref[row, p, 96:97, :]
        parts.append(acc_ref[row, p, 0:48, 0:128] * sums[:, 0:128])
        parts.append(acc_ref[row, p, 48:96, 128:256] * sums[:, 128:256])
    return jnp.concatenate(parts, axis=0).astype(BF16)


def masked_values(vt_ref, slot, p, bit):
    return vt_ref[slot, p] * jnp.full((VROWS, BLOCK), bit, F32).astype(BF16)


def attend(work, fresh, mask_ref, k_ref, vt_ref, qd_ref, acc_ref):
    tiles = []
    for i, blocks in work:
        known = [(e * FRAME + i + d, mask_ref[i, d, e].astype(F32)) for d, e in blocks]
        tiles += [(i, known[n : n + 2], fresh and n == 0) for n in range(0, len(known), 2)]
    chunks = [(i, tile, p, begin) for i, tile, begin in tiles for p in range(PAIRS)]

    def scores(chunk):
        i, tile, p, _ = chunk
        keys = [k_ref[slot, :, 128 * p : 128 * p + 128] for slot, _ in tile]
        return dot(jnp.concatenate(keys, axis=0) if len(keys) > 1 else keys[0], qd_ref[i, p])

    def values(chunk, weights):
        i, tile, p, _ = chunk
        parts = [masked_values(vt_ref, slot, p, bit) for slot, bit in tile]
        return dot(jnp.concatenate(parts, axis=1) if len(parts) > 1 else parts[0], weights)

    held = {}
    for step in range(len(chunks) + AHEAD):
        if step < len(chunks):
            held[step] = scores(chunks[step])
        if step >= AHEAD:
            chunk = chunks[step - AHEAD]
            i, _, p, begin = chunk
            weights = jnp.exp2(held.pop(step - AHEAD) * SCORE_SCALE).astype(BF16)
            if begin:
                acc_ref[i, p] = values(chunk, weights)
            else:
                acc_ref[i, p] += values(chunk, weights)


def attend_cap(blocks, k_ref, vt_ref, qd_ref, acc_ref, top_ref):
    def scores(q, p):
        qd = qd_ref[q, p]
        return [
            dot(jnp.concatenate([k_ref[n + m, :, 128 * p : 128 * p + 128] for m in range(2)], axis=0), qd)
            for n in range(0, blocks, 2)
        ]

    def finish(q, p, tiles):
        tops = [jnp.max(tile, axis=0, keepdims=True) for tile in tiles]
        top = functools.reduce(jnp.maximum, tops) * SCORE_SCALE
        total = None
        for n, tile in enumerate(tiles):
            weights = jnp.exp2(tile * SCORE_SCALE - top).astype(BF16)
            part = dot(jnp.concatenate([vt_ref[2 * n, p], vt_ref[2 * n + 1, p]], axis=1), weights)
            total = part if total is None else total + part
        acc_ref[q, p] = total
        top_ref[q, p, 0:1] = top

    turns = [(q, p) for p in range(PAIRS) for q in range(2)]
    held = []
    for n, turn in enumerate(turns + [None, None]):
        if turn is not None:
            held.append(scores(*turn))
        if n >= 2:
            finish(*turns[n - 2], held.pop(0))


def at_device(lat, lon):
    return {"lat": lat, "lon": lon}


def remote(src, dst, send_sem, recv_sem, to):
    return pltpu.make_async_remote_copy(
        src_ref=src, dst_ref=dst, send_sem=send_sem, recv_sem=recv_sem,
        device_id=at_device(*to), device_id_type=pl.DeviceIdType.MESH,
    )


def landed(dst, sem):
    pltpu.make_async_copy(dst, dst, sem).wait()


class Plan:
    def __init__(self):
        self.lat, self.lon = lat, lon = lax.axis_index("lat"), lax.axis_index("lon")
        self.lon_count, self.last = lax.axis_size("lon"), lax.axis_size("lat") - 1
        self.half = half = self.lon_count // 2
        self.is_north, self.is_south = lat == 0, lat == self.last
        self.at_pole = jnp.logical_or(self.is_north, self.is_south)
        self.inner = jnp.logical_not(self.at_pole)
        self.east = (lat, lax.rem(lon + 1, self.lon_count))
        self.west = (lat, lax.rem(lon + self.lon_count - 1, self.lon_count))
        self.far = (lat, lax.rem(lon + half, self.lon_count))
        self.side = lon // half
        self.y, self.core = lax.rem(lon, half) // 2, lax.rem(lon, 2)
        self.y_count = half // 2
        self.other_core = (lat, lon + 1 - 2 * self.core)
        self.z_count = (self.last + 1) // 2
        south = lax.rem(lat, 2)
        self.pole = (jnp.where(south == 1, self.last, 0), lon)
        away = jnp.where(south == 1, self.z_count - 1 - lat // 2, lat // 2)
        self.part = jnp.where(away == 1, 0, jnp.where(away == 2, 2, 1))

    def along_y(self, step):
        y = lax.rem(self.y + step, self.y_count)
        return (self.lat, self.side * self.half + 2 * y + self.core)

    def helper(self, r, lon=None):
        away = (1, self.z_count - 1, 2)[r]
        return (jnp.where(self.is_north, 2 * away, self.last - 2 * away), self.lon if lon is None else lon)

    def cap_row(self, r):
        return jnp.where(self.is_north, r, ROWS - 1 - r)


def tell_senders(plan):
    barrier = pltpu.get_barrier_semaphore()

    def tell(to):
        pl.semaphore_signal(barrier, inc=1, device_id=at_device(*to), device_id_type=pl.DeviceIdType.MESH)

    def tell_if(wanted, targets):
        @pl.when(wanted)
        def _():
            for to in targets:
                tell(to)

    lat, lon = plan.lat, plan.lon
    tell(plan.east)
    tell(plan.west)
    tell_if(lat < plan.last, [(lat + 1, lon)])
    tell_if(lat > 0, [(lat - 1, lon)])
    tell_if(plan.at_pole, [plan.far] + [plan.helper(r, at) for r in range(3) for at in (lon, plan.far[1])])
    tell_if(plan.inner, [plan.pole, plan.far, plan.other_core] + [plan.along_y(n) for n in (1, 2, 3)])


def wait_receivers(plan):
    pl.semaphore_wait(pltpu.get_barrier_semaphore(), jnp.where(plan.at_pole, 7, 11))


def grid_kernel(
    mask_ref, tokens_ref, w_query_ref, w_key_ref, w_value_ref,
    mixed_ref, hold_ref, west_out, east_out, halos_out,
    west_ref, east_ref, halos_ref, query_ref, cap_ref, part_ref, stat_ref, back_ref, back_stat_ref,
    k_ref, vt_ref, qd_ref, acc_ref, cap_k, cap_vt, cap_qd, cap_acc, cap_top, wide_ref, query_t_ref, value_t_ref,
    side_send, side_recv, halo_send, halo_recv, far_send, far_recv, corner_send, corner_recv,
    give_send, query_recv, cap_recv, sib_send, sib_recv, y_send, y_recv, core_send, core_recv, part_send, part_recv, stat_send, stat_recv, keep_sem,
):
    plan = Plan()
    lat, last = plan.lat, plan.last
    ends = (pl.ds(ROWS - RADIUS, RADIUS), pl.ds(0, RADIUS))
    pairs = (pl.ds(0, RADIUS), pl.ds(RADIUS, RADIUS))
    halo_ref, west_halo_ref, east_halo_ref = halos_ref.at[0], halos_ref.at[1], halos_ref.at[2]
    chunk = ROWS // CHUNKS
    y_count = plan.y_count

    tell_senders(plan)
    prepare_keys(w_key_ref, wide_ref)
    query_t_ref[...] = flipped(w_query_ref)
    value_t_ref[...] = flipped(w_value_ref)
    put_ones(vt_ref)
    put_ones(cap_vt)
    qd_ref[...] = jnp.zeros_like(qd_ref)
    cap_qd[...] = jnp.zeros_like(cap_qd)
    hold_ref[...] = jnp.ones_like(hold_ref)
    wait_receivers(plan)

    def gifts():
        keys = [
            remote(tokens_ref.at[plan.cap_row(r)], cap_ref.at[plan.core, plan.y], give_send.at[r], cap_recv, plan.helper(r))
            for r in range(3)
        ]
        queries = [
            remote(tokens_ref.at[plan.cap_row(0)], query_ref.at[0], give_send.at[3 + r], query_recv, plan.helper(r))
            for r in range(1, 3)
        ]
        return [keys[2], queries[1], keys[1], queries[0], keys[0]]

    def far_slot(n):
        return jnp.where(plan.is_north, RADIUS - 1 - n, RADIUS + n)

    def far_rows():
        rows = [jnp.where(plan.is_north, n, ROWS - 1 - n) for n in range(RADIUS)]
        return [
            remote(tokens_ref.at[rows[n]], halo_ref.at[far_slot(n)], far_send.at[n], far_recv.at[n], plan.far)
            for n in range(RADIUS)
        ]

    def lat_rows(n):
        to = (lat + 1 - 2 * n, plan.lon)
        return remote(tokens_ref.at[ends[n]], halo_ref.at[pairs[n]], halo_send.at[n], halo_recv.at[n], to)

    def has(n):
        return lat < last if n == 0 else lat > 0

    def when_each(wanted, act):
        for n in range(2):
            @pl.when(wanted(n))
            def _(n=n):
                act(n)

    def side_rows(n):
        part = pl.ds(n * chunk, chunk)
        return [
            remote(tokens_ref.at[part], west_ref.at[part], side_send.at[0, n], side_recv.at[0, n], plan.east),
            remote(tokens_ref.at[part], east_ref.at[part], side_send.at[1, n], side_recv.at[1, n], plan.west),
        ]

    mine = cap_ref.at[plan.core, plan.y]
    sibling = remote(query_ref.at[0], query_ref.at[1], sib_send, sib_recv, plan.far)

    def along_y(step):
        spot = cap_ref.at[plan.core, plan.y]
        return remote(spot, spot, y_send.at[step], y_recv.at[step], plan.along_y(step))

    def to_core(step):
        spot = cap_ref.at[plan.core, lax.rem(plan.y + y_count - step, y_count)]
        return remote(spot, spot, core_send.at[step], core_recv.at[step], plan.other_core)

    def from_y(step):
        landed(cap_ref.at[plan.core, lax.rem(plan.y + y_count - step, y_count)], y_recv.at[step])

    def from_core(step):
        landed(cap_ref.at[1 - plan.core, lax.rem(plan.y + y_count - step, y_count)], core_recv.at[step])

    def cap_stage(stage):
        @pl.when(plan.inner)
        def _():
            if stage == 0:
                landed(mine, cap_recv)
                for step in range(1, y_count):
                    along_y(step).start()
                to_core(0).start()
            if stage == 1:
                @pl.when(plan.part > 0)
                def _():
                    landed(query_ref.at[0], query_recv)

                @pl.when(plan.part == 0)
                def _():
                    query_ref[0] = mine[...]

                sibling.start()
            if stage == 2:
                for step in range(1, y_count):
                    from_y(step)
                    to_core(step).start()
            if stage == 3:
                for step in range(y_count):
                    from_core(step)
                landed(query_ref.at[1], sib_recv)

    def put(strips):
        put_tokens([(tokens.reshape(2 * BLOCK, WIDTH), slot) for tokens, slot in strips], wide_ref, value_t_ref, k_ref, vt_ref)

    def add(work, fresh=False):
        attend(work, fresh, mask_ref, k_ref, vt_ref, qd_ref, acc_ref)

    def add_rows(first, count, columns, fresh=False):
        blocks = [(d, e) for e in columns for d in range(SPAN)]
        add([(first + n, blocks) for n in range(count)], fresh)

    def outer_work(columns, inside):
        work = []
        for i in OUTER_ROWS:
            reach = [d for d in range(SPAN) if (0 <= i + d - RADIUS < ROWS) == inside]
            work.append((i, [(d, e) for e in columns for d in reach]))
        return work

    def finish(i):
        mixed_ref[i] = normalised(acc_ref, i)
        for p in range(PAIRS):
            hold_ref[0:1] = jnp.minimum(hold_ref[0:1], sums_hold(acc_ref[i, p, 96:97, :]))

    def take_sides(n):
        for copy in side_rows(n):
            copy.wait_recv()
        strips = []
        for row in range(n * chunk, n * chunk + chunk, 2):
            strips.append((west_ref[row : row + 2], RADIUS + row))
            strips.append((east_ref[row : row + 2], 2 * FRAME + RADIUS + row))
        put(strips)

    def halo_strips(column, which):
        return [
            (halos_ref[which, 0:2], column * FRAME), (halos_ref[which, 2:4], column * FRAME + ROWS + RADIUS)]

    when_each(has, lambda n: lat_rows(n).start())

    @pl.when(plan.at_pole)
    def _():
        for copy in far_rows() + gifts():
            copy.start()

    def start_sides(n):
        for copy in side_rows(n):
            copy.start()

    start_sides(0)

    def own(t, carry):
        first = [4 * t, 4 * t + 2]
        strips = [tokens_ref[pl.ds(n, 2)] for n in first]
        put([(tokens, FRAME + RADIUS + n) for tokens, n in zip(strips, first)])
        put_queries(
            [(tokens.reshape(2 * BLOCK, WIDTH), (n, n + 1)) for tokens, n in zip(strips, first)], query_t_ref, qd_ref)
        return carry

    lax.fori_loop(0, ROWS // 4, own, 0)
    cap_stage(0)
    start_sides(1)
    add_rows(2, 4, (1,), True)
    cap_stage(1)
    add_rows(6, 4, (1,), True)
    start_sides(2)
    add(outer_work((1,), True), True)
    cap_stage(2)
    take_sides(0)
    when_each(lambda n: has(1 - n), lambda n: landed(halo_ref.at[pairs[n]], halo_recv.at[n]))

    @pl.when(plan.at_pole)
    def _():
        for n in range(RADIUS):
            landed(halo_ref.at[far_slot(n)], far_recv.at[n])

    corners = [
        remote(halo_ref, west_halo_ref, corner_send.at[0], corner_recv.at[0], plan.east),
        remote(halo_ref, east_halo_ref, corner_send.at[1], corner_recv.at[1], plan.west),
    ]
    for copy in corners:
        copy.start()
    put(halo_strips(1, 0))
    add(outer_work((1,), False))
    cap_stage(3)

    def send_parts():
        copies = []
        for q, to in enumerate((plan.pole, (plan.pole[0], plan.far[1]))):
            copies.append(remote(
                part_ref.at[q], back_ref.at[plan.part, q], part_send.at[q], part_recv.at[plan.part, q], to))
            copies.append(remote(
                stat_ref.at[q], back_stat_ref.at[plan.part, q], stat_send.at[q], stat_recv.at[plan.part, q], to))
        return copies

    @pl.when(plan.inner)
    def _():
        put_queries([(query_ref[...].reshape(2 * BLOCK, WIDTH), (0, 1))], query_t_ref, cap_qd)
        strips = [
            (cap_ref[core].reshape(y_count // 2, 2 * BLOCK, WIDTH)[n], core * y_count + 2 * n)
            for core in range(2) for n in range(y_count // 2)
        ]
        put_tokens(strips, wide_ref, value_t_ref, cap_k, cap_vt)
        attend_cap(2 * y_count, cap_k, cap_vt, cap_qd, cap_acc, cap_top)
        for q in range(2):
            for p in range(PAIRS):
                part_ref[q, 96 * p : 96 * p + 48] = cap_acc[q, p, 0:48, 0:128].astype(BF16)
                part_ref[q, 96 * p + 48 : 96 * p + 96] = cap_acc[q, p, 48:96, 128:256].astype(BF16)
                for half in range(2):
                    lanes = slice(128 * half, 128 * half + 128)
                    n = 2 * p + half
                    stat_ref[q, n : n + 1] = cap_acc[q, p, 96:97, lanes]
                    stat_ref[q, HEADS + n : HEADS + n + 1] = cap_top[q, p, 0:1, lanes]
        for copy in send_parts():
            copy.start()

    take_sides(1)
    add_rows(2, 4, (0, 2))
    take_sides(2)
    keep = [
        pltpu.make_async_copy(west_ref, west_out, keep_sem.at[0]),
        pltpu.make_async_copy(east_ref, east_out, keep_sem.at[1]),
    ]
    for copy in keep:
        copy.start()
    add_rows(6, 4, (0, 2))
    add(outer_work((0, 2), True))

    def finish_row(t, carry):
        finish(2 + t)
        return carry

    lax.fori_loop(0, ROWS - 4, finish_row, 0)
    for copy in corners:
        copy.wait_recv()
    keep.append(pltpu.make_async_copy(halos_ref, halos_out, keep_sem.at[2]))
    keep[-1].start()
    put(halo_strips(0, 1) + halo_strips(2, 2))
    add(outer_work((0, 2), False))
    for i in OUTER_ROWS:
        finish(i)

    @pl.when(plan.at_pole)
    def _():
        row = jnp.where(plan.is_north, 0, ROWS - 1)
        counts = [0, 0, 0]
        for d in range(SPAN):
            north = d - RADIUS if d >= RADIUS else RADIUS - 1 - d
            south = RADIUS - d if d <= RADIUS else d - RADIUS - 1
            bit = mask_ref[row, d, 1].astype(F32)
            for r in range(3):
                hit = jnp.where(plan.is_north, float(north == r), float(south == r))
                counts[r] = counts[r] + bit * hit
        parts = [(r, q) for r in range(3) for q in range(2)]
        for r, q in parts:
            landed(back_stat_ref.at[r, q], stat_recv.at[r, q])
            landed(back_ref.at[r, q], part_recv.at[r, q])
        sums, tops = pl.ds(0, HEADS), pl.ds(HEADS, HEADS)
        used = [jnp.full((HEADS, BLOCK), counts[r], F32) for r, _ in parts]
        low = [jnp.where(n > 0.5, back_stat_ref[r, q, tops], -jnp.inf) for n, (r, q) in zip(used, parts)]
        top = functools.reduce(jnp.maximum, low)
        factors = [jnp.exp2(t - top) * n for t, n in zip(low, used)]
        total = 1.0 / sum(f * back_stat_ref[r, q, sums] for f, (r, q) in zip(factors, parts))
        heads = []
        for h in range(HEADS):
            rows = pl.ds(HEAD_DIM * h, HEAD_DIM)
            heads.append(
                sum(f[h : h + 1] * back_ref[r, q, rows].astype(F32) for f, (r, q) in zip(factors, parts))
                * total[h : h + 1])
        mixed_ref[row] = jnp.concatenate(heads, axis=0).astype(BF16)
        for copy in gifts() + far_rows():
            copy.wait_send()

    @pl.when(plan.inner)
    def _():
        sibling.wait_send()
        for step in range(y_count):
            to_core(step).wait_send()
            if step > 0:
                along_y(step).wait_send()
        for copy in send_parts():
            copy.wait_send()

    when_each(has, lambda n: lat_rows(n).wait_send())
    for n in range(CHUNKS):
        for copy in side_rows(n):
            copy.wait_send()
    for copy in corners:
        copy.wait_send()
    for copy in keep:
        copy.wait()


def output_kernel(
    mask_ref, mixed_ref, hold_ref, w_out_ref, w_query_in, w_key_in, w_value_in, tokens_in, west_in, east_in, halos_in,
    out_ref,
    fixed_ref, strip_ref, weight_ref, k_ref, vt_ref, qd_ref, acc_ref, top_ref, wide_ref, query_t_ref, value_t_ref,
    list_ref, begin_ref, sem,
):
    lat = lax.axis_index("lat")
    last = lax.axis_size("lat") - 1

    def product(from_ref):
        def body(t, carry):
            both = jnp.concatenate([from_ref[2 * t], from_ref[2 * t + 1]], axis=1)
            result = dot(both, w_out_ref[...], ((0,), (0,))).astype(BF16)
            out_ref[pl.ds(2 * t, 2)] = result.reshape(2, BLOCK, WIDTH)
            return carry

        lax.fori_loop(0, ROWS // 2, body, 0, unroll=3)

    product(mixed_ref)
    holds = jnp.min(hold_ref[...]) > 0.5

    @pl.when(jnp.logical_not(holds))
    def _():
        def fetch(src, dst):
            copy = pltpu.make_async_copy(src, dst, sem)
            copy.start()
            copy.wait()

        fetch(w_key_in, weight_ref)
        prepare_keys(weight_ref, wide_ref)
        fetch(w_query_in, weight_ref)
        query_t_ref[...] = flipped(weight_ref)
        fetch(w_value_in, weight_ref)
        value_t_ref[...] = flipped(weight_ref)
        put_ones(vt_ref)
        qd_ref[...] = jnp.zeros_like(qd_ref)

        def take(src, slot):
            fetch(src, strip_ref)
            tokens = strip_ref[...].reshape(2 * BLOCK, WIDTH)
            put_tokens([(tokens, slot)], wide_ref, value_t_ref, k_ref, vt_ref)
            return tokens

        def load(t, carry):
            part = pl.ds(2 * t, 2)
            take(west_in.at[part], RADIUS + 2 * t)
            take(east_in.at[part], 2 * FRAME + RADIUS + 2 * t)
            tokens = take(tokens_in.at[part], FRAME + RADIUS + 2 * t)
            put_queries([(tokens, (2 * t, 2 * t + 1))], query_t_ref, qd_ref)
            return carry

        lax.fori_loop(0, ROWS // 2, load, 0)
        for column, which in ((1, 0), (0, 1), (2, 2)):
            take(halos_in.at[which, pl.ds(0, 2)], column * FRAME)
            take(halos_in.at[which, pl.ds(2, 2)], column * FRAME + ROWS + RADIUS)
        fixed_ref[...] = mixed_ref[...]

        def again(i, carry):
            pos = jnp.int32(0)
            for d in range(SPAN):
                for e in range(3):
                    list_ref[pos] = e * FRAME + i + d
                    pos = pos + (mask_ref[i, d, e] > 0).astype(jnp.int32)
            begin_ref[0] = pos
            polar = jnp.logical_or(
                jnp.logical_and(lat == 0, i == 0), jnp.logical_and(lat == last, i == ROWS - 1))

            @pl.when(jnp.logical_not(polar))
            def _():
                safe_row(
                    i, 0, 0, begin_ref[0], lambda n: list_ref[n], k_ref, vt_ref, qd_ref, acc_ref, top_ref)
                fixed_ref[i] = normalised(acc_ref, 0)

            return carry

        lax.fori_loop(0, ROWS, again, 0)
        product(fixed_ref)


def per_device(tokens, neighbor_mask, w_query, w_key, w_value, w_out):
    lon_count = lax.axis_size("lon")
    half = lon_count // 2
    strip = lambda *dims: jax.ShapeDtypeStruct((*dims, BLOCK, WIDTH), BF16)
    landing = lambda *dims: pltpu.VMEM((*dims, BLOCK, WIDTH), BF16)
    dma = pltpu.SemaphoreType.DMA
    keys = lambda n: pltpu.VMEM((n, BLOCK, LANES), BF16)
    values = lambda n: pltpu.VMEM((n, PAIRS, VROWS, BLOCK), BF16)
    queries = lambda n: pltpu.VMEM((n, PAIRS, 128, 256), BF16)
    square = pltpu.VMEM((WIDTH, WIDTH), BF16)
    wide = pltpu.VMEM((WIDTH, LANES), BF16)
    tops = pltpu.VMEM((PAIRS, 8, 256), F32)
    mixed = jax.ShapeDtypeStruct((ROWS, WIDTH, BLOCK), BF16)
    mixed, hold, west, east, halos = pl.pallas_call(
        grid_kernel,
        out_shape=[mixed, jax.ShapeDtypeStruct((8, 256), F32), strip(ROWS), strip(ROWS), strip(3, 4)],
        in_specs=[SMEM_SPEC] + [VMEM_SPEC] * 4,
        out_specs=[VMEM_SPEC] * 2 + [ANY_SPEC] * 3,
        scratch_shapes=[
            landing(ROWS), landing(ROWS), landing(3, 4), landing(2), landing(2, half // 2),
            pltpu.VMEM((2, WIDTH, BLOCK), BF16), pltpu.VMEM((2, 2 * HEADS, BLOCK), F32),
            pltpu.VMEM((3, 2, WIDTH, BLOCK), BF16), pltpu.VMEM((3, 2, 2 * HEADS, BLOCK), F32),
            keys(SLOTS), values(SLOTS), queries(ROWS),
            pltpu.VMEM((ROWS, PAIRS, VROWS, 256), F32),
            keys(half), values(half), queries(2),
            pltpu.VMEM((2, PAIRS, VROWS, 256), F32), pltpu.VMEM((2, PAIRS, 8, 256), F32),
            wide, square, square,
            dma((2, CHUNKS)), dma((2, CHUNKS)), dma((2,)), dma((2,)), dma((2,)), dma((2,)), dma((2,)), dma((2,)),
            dma((6,)), dma, dma, dma, dma, *[dma((half // 2,))] * 4,
            dma((2,)), dma((3, 2)), dma((2,)), dma((3, 2)), dma((3,)),
        ],
        compiler_params=pltpu.CompilerParams(
            collective_id=0, has_side_effects=True, vmem_limit_bytes=VMEM_LIMIT),
        name="grid_attention",
    )(neighbor_mask, tokens, w_query, w_key, w_value)
    return pl.pallas_call(
        output_kernel,
        out_shape=strip(ROWS),
        in_specs=[SMEM_SPEC] + [VMEM_SPEC] * 3 + [ANY_SPEC] * 7,
        out_specs=VMEM_SPEC,
        scratch_shapes=[
            pltpu.VMEM((ROWS, WIDTH, BLOCK), BF16), landing(2), square,
            keys(SLOTS), values(SLOTS), queries(ROWS),
            pltpu.VMEM((1, PAIRS, VROWS, 256), F32),
            tops, wide, square, square,
            pltpu.SMEM((SPAN * 3 + 1,), jnp.int32), pltpu.SMEM((1,), jnp.int32), dma,
        ],
        compiler_params=pltpu.CompilerParams(vmem_limit_bytes=VMEM_LIMIT),
        name="output_product",
    )(neighbor_mask, mixed, hold, w_out, w_query, w_key, w_value, tokens, west, east, halos)


def solution(mesh):
    placed = (P("lat", "lon", None), P("lat", None, None), P(), P(), P(), P())
    return jax.shard_map(
        per_device, mesh=mesh, in_specs=placed, out_specs=P("lat", "lon", None), check_vma=False
    )
```

```python
import functools

import jax
import jax.numpy as jnp
from jax import lax
from jax.experimental import pallas as pl
from jax.experimental.pallas import tpu as pltpu
from jax.sharding import PartitionSpec as P

HEADS = 8
HEAD_DIM = 48
PAIRS = 4
WIDTH = 384
BLOCK = 128
ROWS = 12
RADIUS = 2
SPAN = 5
FRAME = ROWS + 2 * RADIUS
SLOTS = 3 * FRAME
VROWS = 112
LANES = 128 * PAIRS
AHEAD = 8
CHUNKS = 3
OUTER_ROWS = (0, 1, ROWS - 2, ROWS - 1)
SCORE_SCALE = HEAD_DIM ** -0.5 * 1.4426950408889634
SUM_LOW = 1e-30
SUM_HIGH = 1e30
VMEM_LIMIT = 56 * 2**20
F32 = jnp.float32
BF16 = jnp.bfloat16
VMEM_SPEC = pl.BlockSpec(memory_space=pltpu.VMEM)
SMEM_SPEC = pl.BlockSpec(memory_space=pltpu.SMEM)
ANY_SPEC = pl.BlockSpec(memory_space=pl.ANY)


def dot(a, b, dims=((1,), (0,))):
    return lax.dot_general(a, b, (dims, ((), ())), preferred_element_type=F32)


def prepare_keys(w_key_ref, wide_ref):
    wide_ref[...] = jnp.zeros_like(wide_ref)
    for p in range(PAIRS):
        wide_ref[:, 128 * p : 128 * p + 96] = w_key_ref[:, 96 * p : 96 * p + 96]


def flipped(ref):
    return ref[...].astype(F32).T.astype(BF16)


def put_tokens(strips, wide_ref, value_t_ref, k_ref, vt_ref):
    keys = [dot(tokens, wide_ref[...]) for tokens, _ in strips]
    values = [dot(value_t_ref[...], tokens, ((1,), (1,))) for tokens, _ in strips]
    for (_, slot), key, value in zip(strips, keys, values):
        key, value = key.astype(BF16), value.astype(BF16)
        for n in range(2):
            k_ref[slot + n] = key[128 * n : 128 * n + 128]
            for p in range(PAIRS):
                vt_ref[slot + n, p, 0:96] = value[96 * p : 96 * p + 96, 128 * n : 128 * n + 128]


def put_queries(strips, query_t_ref, qd_ref):
    queries = [dot(query_t_ref[...], tokens, ((1,), (1,))) for tokens, _ in strips]
    for (_, rows), query in zip(strips, queries):
        query = query.astype(BF16)
        for n, row in enumerate(rows):
            for p in range(PAIRS):
                part = query[96 * p : 96 * p + 96, 128 * n : 128 * n + 128]
                qd_ref[row, p, 0:48, 0:128] = part[0:48]
                qd_ref[row, p, 48:96, 128:256] = part[48:96]


def put_ones(vt_ref):
    ones = jnp.ones((VROWS - 96, 128), BF16)

    def body(slot, carry):
        for p in range(PAIRS):
            vt_ref[slot, p, 96:VROWS] = ones
        return carry

    lax.fori_loop(0, vt_ref.shape[0], body, 0)


def safe_row(q, acc_at, begin, end, slot_of, k_ref, vt_ref, qd_ref, acc_ref, top_ref):
    top_ref[...] = jnp.full(top_ref.shape, -jnp.inf, F32)

    def scores(n, p):
        return dot(k_ref[slot_of(n), :, 128 * p : 128 * p + 128], qd_ref[q, p]) * SCORE_SCALE

    def find_top(n, carry):
        for p in range(PAIRS):
            top_ref[p] = jnp.maximum(top_ref[p], jnp.max(scores(n, p), axis=0, keepdims=True))
        return carry

    lax.fori_loop(begin, end, find_top, 0)
    acc_ref[acc_at] = jnp.zeros(acc_ref.shape[1:], F32)

    def add(n, carry):
        for p in range(PAIRS):
            weights = jnp.exp2(scores(n, p) - top_ref[p, 0:1]).astype(BF16)
            acc_ref[acc_at, p] += dot(vt_ref[slot_of(n), p], weights)
        return carry

    lax.fori_loop(begin, end, add, 0)


def sums_hold(sums):
    return jnp.where((sums >= SUM_LOW) & (sums <= SUM_HIGH), 1.0, 0.0)


def normalised(acc_ref, row):
    parts = []
    for p in range(PAIRS):
        sums = 1.0 / acc_ref[row, p, 96:97, :]
        parts.append(acc_ref[row, p, 0:48, 0:128] * sums[:, 0:128])
        parts.append(acc_ref[row, p, 48:96, 128:256] * sums[:, 128:256])
    return jnp.concatenate(parts, axis=0).astype(BF16)


def masked_values(vt_ref, slot, p, bit):
    return vt_ref[slot, p] * jnp.full((VROWS, BLOCK), bit, F32).astype(BF16)


def attend(work, fresh, mask_ref, k_ref, vt_ref, qd_ref, acc_ref):
    tiles = []
    for i, blocks in work:
        known = [(e * FRAME + i + d, mask_ref[i, d, e].astype(F32)) for d, e in blocks]
        tiles += [(i, known[n : n + 2], fresh and n == 0) for n in range(0, len(known), 2)]
    chunks = [(i, tile, p, begin) for i, tile, begin in tiles for p in range(PAIRS)]

    def scores(chunk):
        i, tile, p, _ = chunk
        keys = [k_ref[slot, :, 128 * p : 128 * p + 128] for slot, _ in tile]
        return dot(jnp.concatenate(keys, axis=0) if len(keys) > 1 else keys[0], qd_ref[i, p])

    def values(chunk, weights):
        i, tile, p, _ = chunk
        parts = [masked_values(vt_ref, slot, p, bit) for slot, bit in tile]
        return dot(jnp.concatenate(parts, axis=1) if len(parts) > 1 else parts[0], weights)

    held = {}
    for step in range(len(chunks) + AHEAD):
        if step < len(chunks):
            held[step] = scores(chunks[step])
        if step >= AHEAD:
            chunk = chunks[step - AHEAD]
            i, _, p, begin = chunk
            weights = jnp.exp2(held.pop(step - AHEAD) * SCORE_SCALE).astype(BF16)
            if begin:
                acc_ref[i, p] = values(chunk, weights)
            else:
                acc_ref[i, p] += values(chunk, weights)


def attend_cap(blocks, k_ref, vt_ref, qd_ref, acc_ref, top_ref):
    def scores(q, p):
        qd = qd_ref[q, p]
        return [
            dot(jnp.concatenate([k_ref[n + m, :, 128 * p : 128 * p + 128] for m in range(2)], axis=0), qd)
            for n in range(0, blocks, 2)
        ]

    def finish(q, p, tiles):
        tops = [jnp.max(tile, axis=0, keepdims=True) for tile in tiles]
        top = functools.reduce(jnp.maximum, tops) * SCORE_SCALE
        total = None
        for n, tile in enumerate(tiles):
            weights = jnp.exp2(tile * SCORE_SCALE - top).astype(BF16)
            part = dot(jnp.concatenate([vt_ref[2 * n, p], vt_ref[2 * n + 1, p]], axis=1), weights)
            total = part if total is None else total + part
        acc_ref[q, p] = total
        top_ref[q, p, 0:1] = top

    turns = [(q, p) for p in range(PAIRS) for q in range(2)]
    held = []
    for n, turn in enumerate(turns + [None, None]):
        if turn is not None:
            held.append(scores(*turn))
        if n >= 2:
            finish(*turns[n - 2], held.pop(0))


def at_device(lat, lon):
    return {"lat": lat, "lon": lon}


def remote(src, dst, send_sem, recv_sem, to):
    return pltpu.make_async_remote_copy(
        src_ref=src, dst_ref=dst, send_sem=send_sem, recv_sem=recv_sem,
        device_id=at_device(*to), device_id_type=pl.DeviceIdType.MESH,
    )


def landed(dst, sem):
    pltpu.make_async_copy(dst, dst, sem).wait()


class Plan:
    def __init__(self):
        self.lat, self.lon = lat, lon = lax.axis_index("lat"), lax.axis_index("lon")
        self.lon_count, self.last = lax.axis_size("lon"), lax.axis_size("lat") - 1
        self.half = half = self.lon_count // 2
        self.is_north, self.is_south = lat == 0, lat == self.last
        self.at_pole = jnp.logical_or(self.is_north, self.is_south)
        self.inner = jnp.logical_not(self.at_pole)
        self.east = (lat, lax.rem(lon + 1, self.lon_count))
        self.west = (lat, lax.rem(lon + self.lon_count - 1, self.lon_count))
        self.far = (lat, lax.rem(lon + half, self.lon_count))
        self.side = lon // half
        self.y, self.core = lax.rem(lon, half) // 2, lax.rem(lon, 2)
        self.y_count = half // 2
        self.other_core = (lat, lon + 1 - 2 * self.core)
        self.z_count = (self.last + 1) // 2
        south = lax.rem(lat, 2)
        self.pole = (jnp.where(south == 1, self.last, 0), lon)
        away = jnp.where(south == 1, self.z_count - 1 - lat // 2, lat // 2)
        self.part = jnp.where(away == 1, 0, jnp.where(away == 2, 2, 1))

    def along_y(self, step):
        y = lax.rem(self.y + step, self.y_count)
        return (self.lat, self.side * self.half + 2 * y + self.core)

    def helper(self, r, lon=None):
        away = (1, self.z_count - 1, 2)[r]
        return (jnp.where(self.is_north, 2 * away, self.last - 2 * away), self.lon if lon is None else lon)

    def cap_row(self, r):
        return jnp.where(self.is_north, r, ROWS - 1 - r)


def tell_senders(plan):
    barrier = pltpu.get_barrier_semaphore()

    def tell(to):
        pl.semaphore_signal(barrier, inc=1, device_id=at_device(*to), device_id_type=pl.DeviceIdType.MESH)

    def tell_if(wanted, targets):
        @pl.when(wanted)
        def _():
            for to in targets:
                tell(to)

    lat, lon = plan.lat, plan.lon
    tell(plan.east)
    tell(plan.west)
    tell_if(lat < plan.last, [(lat + 1, lon)])
    tell_if(lat > 0, [(lat - 1, lon)])
    tell_if(plan.at_pole, [plan.far] + [plan.helper(r, at) for r in range(3) for at in (lon, plan.far[1])])
    tell_if(plan.inner, [plan.pole, plan.far, plan.other_core] + [plan.along_y(n) for n in (1, 2, 3)])


def wait_receivers(plan):
    pl.semaphore_wait(pltpu.get_barrier_semaphore(), jnp.where(plan.at_pole, 7, 11))


def grid_kernel(
    mask_ref, tokens_ref, w_query_ref, w_key_ref, w_value_ref,
    mixed_ref, hold_ref, west_out, east_out, halos_out,
    west_ref, east_ref, halos_ref, query_ref, cap_ref, part_ref, stat_ref, back_ref, back_stat_ref,
    k_ref, vt_ref, qd_ref, acc_ref, cap_k, cap_vt, cap_qd, cap_acc, cap_top, wide_ref, query_t_ref, value_t_ref,
    side_send, side_recv, halo_send, halo_recv, far_send, far_recv, corner_send, corner_recv,
    give_send, query_recv, cap_recv, sib_send, sib_recv, y_send, y_recv, core_send, core_recv, part_send, part_recv, stat_send, stat_recv, keep_sem,
):
    plan = Plan()
    lat, last = plan.lat, plan.last
    ends = (pl.ds(ROWS - RADIUS, RADIUS), pl.ds(0, RADIUS))
    pairs = (pl.ds(0, RADIUS), pl.ds(RADIUS, RADIUS))
    halo_ref, west_halo_ref, east_halo_ref = halos_ref.at[0], halos_ref.at[1], halos_ref.at[2]
    chunk = ROWS // CHUNKS
    y_count = plan.y_count

    tell_senders(plan)
    prepare_keys(w_key_ref, wide_ref)
    query_t_ref[...] = flipped(w_query_ref)
    value_t_ref[...] = flipped(w_value_ref)
    put_ones(vt_ref)
    put_ones(cap_vt)
    qd_ref[...] = jnp.zeros_like(qd_ref)
    cap_qd[...] = jnp.zeros_like(cap_qd)
    hold_ref[...] = jnp.ones_like(hold_ref)
    wait_receivers(plan)

    def gifts():
        keys = [
            remote(tokens_ref.at[plan.cap_row(r)], cap_ref.at[plan.core, plan.y], give_send.at[r], cap_recv, plan.helper(r))
            for r in range(3)
        ]
        queries = [
            remote(tokens_ref.at[plan.cap_row(0)], query_ref.at[0], give_send.at[3 + r], query_recv, plan.helper(r))
            for r in range(1, 3)
        ]
        return [keys[2], queries[1], keys[0], keys[1], queries[0]]

    def far_slot(n):
        return jnp.where(plan.is_north, RADIUS - 1 - n, RADIUS + n)

    def far_rows():
        rows = [jnp.where(plan.is_north, n, ROWS - 1 - n) for n in range(RADIUS)]
        return [
            remote(tokens_ref.at[rows[n]], halo_ref.at[far_slot(n)], far_send.at[n], far_recv.at[n], plan.far)
            for n in range(RADIUS)
        ]

    def lat_rows(n):
        to = (lat + 1 - 2 * n, plan.lon)
        return remote(tokens_ref.at[ends[n]], halo_ref.at[pairs[n]], halo_send.at[n], halo_recv.at[n], to)

    def has(n):
        return lat < last if n == 0 else lat > 0

    def when_each(wanted, act):
        for n in range(2):
            @pl.when(wanted(n))
            def _(n=n):
                act(n)

    def side_rows(n):
        part = pl.ds(n * chunk, chunk)
        return [
            remote(tokens_ref.at[part], west_ref.at[part], side_send.at[0, n], side_recv.at[0, n], plan.east),
            remote(tokens_ref.at[part], east_ref.at[part], side_send.at[1, n], side_recv.at[1, n], plan.west),
        ]

    mine = cap_ref.at[plan.core, plan.y]
    sibling = remote(query_ref.at[0], query_ref.at[1], sib_send, sib_recv, plan.far)

    def along_y(step):
        spot = cap_ref.at[plan.core, plan.y]
        return remote(spot, spot, y_send.at[step], y_recv.at[step], plan.along_y(step))

    def to_core(step):
        spot = cap_ref.at[plan.core, lax.rem(plan.y + y_count - step, y_count)]
        return remote(spot, spot, core_send.at[step], core_recv.at[step], plan.other_core)

    def from_y(step):
        landed(cap_ref.at[plan.core, lax.rem(plan.y + y_count - step, y_count)], y_recv.at[step])

    def from_core(step):
        landed(cap_ref.at[1 - plan.core, lax.rem(plan.y + y_count - step, y_count)], core_recv.at[step])

    def cap_stage(stage):
        @pl.when(plan.inner)
        def _():
            if stage == 0:
                landed(mine, cap_recv)
                for step in range(1, y_count):
                    along_y(step).start()
                to_core(0).start()
            if stage == 1:
                @pl.when(plan.part > 0)
                def _():
                    landed(query_ref.at[0], query_recv)

                @pl.when(plan.part == 0)
                def _():
                    query_ref[0] = mine[...]

                sibling.start()
            if stage == 2:
                for step in range(1, y_count):
                    from_y(step)
                    to_core(step).start()
            if stage == 3:
                for step in range(y_count):
                    from_core(step)
                landed(query_ref.at[1], sib_recv)

    def put(strips):
        put_tokens([(tokens.reshape(2 * BLOCK, WIDTH), slot) for tokens, slot in strips], wide_ref, value_t_ref, k_ref, vt_ref)

    def add(work, fresh=False):
        attend(work, fresh, mask_ref, k_ref, vt_ref, qd_ref, acc_ref)

    def add_rows(first, count, columns, fresh=False):
        blocks = [(d, e) for e in columns for d in range(SPAN)]
        add([(first + n, blocks) for n in range(count)], fresh)

    def outer_work(columns, inside):
        work = []
        for i in OUTER_ROWS:
            reach = [d for d in range(SPAN) if (0 <= i + d - RADIUS < ROWS) == inside]
            work.append((i, [(d, e) for e in columns for d in reach]))
        return work

    def finish(i):
        mixed_ref[i] = normalised(acc_ref, i)
        for p in range(PAIRS):
            hold_ref[0:1] = jnp.minimum(hold_ref[0:1], sums_hold(acc_ref[i, p, 96:97, :]))

    def take_sides(n):
        for copy in side_rows(n):
            copy.wait_recv()
        strips = []
        for row in range(n * chunk, n * chunk + chunk, 2):
            strips.append((west_ref[row : row + 2], RADIUS + row))
            strips.append((east_ref[row : row + 2], 2 * FRAME + RADIUS + row))
        put(strips)

    def halo_strips(column, which):
        return [
            (halos_ref[which, 0:2], column * FRAME), (halos_ref[which, 2:4], column * FRAME + ROWS + RADIUS)]

    when_each(has, lambda n: lat_rows(n).start())

    @pl.when(plan.at_pole)
    def _():
        for copy in far_rows() + gifts():
            copy.start()

    def start_sides(n):
        for copy in side_rows(n):
            copy.start()

    start_sides(0)

    def own(t, carry):
        first = [4 * t, 4 * t + 2]
        strips = [tokens_ref[pl.ds(n, 2)] for n in first]
        put([(tokens, FRAME + RADIUS + n) for tokens, n in zip(strips, first)])
        put_queries(
            [(tokens.reshape(2 * BLOCK, WIDTH), (n, n + 1)) for tokens, n in zip(strips, first)], query_t_ref, qd_ref)
        return carry

    lax.fori_loop(0, ROWS // 4, own, 0)
    cap_stage(0)
    start_sides(1)
    add_rows(2, 4, (1,), True)
    cap_stage(1)
    add_rows(6, 4, (1,), True)
    start_sides(2)
    add(outer_work((1,), True), True)
    cap_stage(2)
    take_sides(0)
    when_each(lambda n: has(1 - n), lambda n: landed(halo_ref.at[pairs[n]], halo_recv.at[n]))

    @pl.when(plan.at_pole)
    def _():
        for n in range(RADIUS):
            landed(halo_ref.at[far_slot(n)], far_recv.at[n])

    corners = [
        remote(halo_ref, west_halo_ref, corner_send.at[0], corner_recv.at[0], plan.east),
        remote(halo_ref, east_halo_ref, corner_send.at[1], corner_recv.at[1], plan.west),
    ]
    for copy in corners:
        copy.start()
    put(halo_strips(1, 0))
    add(outer_work((1,), False))
    cap_stage(3)

    def send_parts():
        copies = []
        for q, to in enumerate((plan.pole, (plan.pole[0], plan.far[1]))):
            copies.append(remote(
                part_ref.at[q], back_ref.at[plan.part, q], part_send.at[q], part_recv.at[plan.part, q], to))
            copies.append(remote(
                stat_ref.at[q], back_stat_ref.at[plan.part, q], stat_send.at[q], stat_recv.at[plan.part, q], to))
        return copies

    @pl.when(plan.inner)
    def _():
        put_queries([(query_ref[...].reshape(2 * BLOCK, WIDTH), (0, 1))], query_t_ref, cap_qd)
        strips = [
            (cap_ref[core].reshape(y_count // 2, 2 * BLOCK, WIDTH)[n], core * y_count + 2 * n)
            for core in range(2) for n in range(y_count // 2)
        ]
        put_tokens(strips, wide_ref, value_t_ref, cap_k, cap_vt)
        attend_cap(2 * y_count, cap_k, cap_vt, cap_qd, cap_acc, cap_top)
        for q in range(2):
            for p in range(PAIRS):
                part_ref[q, 96 * p : 96 * p + 48] = cap_acc[q, p, 0:48, 0:128].astype(BF16)
                part_ref[q, 96 * p + 48 : 96 * p + 96] = cap_acc[q, p, 48:96, 128:256].astype(BF16)
                for half in range(2):
                    lanes = slice(128 * half, 128 * half + 128)
                    n = 2 * p + half
                    stat_ref[q, n : n + 1] = cap_acc[q, p, 96:97, lanes]
                    stat_ref[q, HEADS + n : HEADS + n + 1] = cap_top[q, p, 0:1, lanes]
        for copy in send_parts():
            copy.start()

    take_sides(1)
    add_rows(2, 4, (0, 2))
    take_sides(2)
    keep = [
        pltpu.make_async_copy(west_ref, west_out, keep_sem.at[0]),
        pltpu.make_async_copy(east_ref, east_out, keep_sem.at[1]),
    ]
    for copy in keep:
        copy.start()
    add_rows(6, 4, (0, 2))
    add(outer_work((0, 2), True))

    def finish_row(t, carry):
        finish(2 + t)
        return carry

    lax.fori_loop(0, ROWS - 4, finish_row, 0)
    for copy in corners:
        copy.wait_recv()
    keep.append(pltpu.make_async_copy(halos_ref, halos_out, keep_sem.at[2]))
    keep[-1].start()
    put(halo_strips(0, 1) + halo_strips(2, 2))
    add(outer_work((0, 2), False))
    for i in OUTER_ROWS:
        finish(i)

    @pl.when(plan.at_pole)
    def _():
        row = jnp.where(plan.is_north, 0, ROWS - 1)
        counts = [0, 0, 0]
        for d in range(SPAN):
            north = d - RADIUS if d >= RADIUS else RADIUS - 1 - d
            south = RADIUS - d if d <= RADIUS else d - RADIUS - 1
            bit = mask_ref[row, d, 1].astype(F32)
            for r in range(3):
                hit = jnp.where(plan.is_north, float(north == r), float(south == r))
                counts[r] = counts[r] + bit * hit
        parts = [(r, q) for r in range(3) for q in range(2)]
        for r, q in parts:
            landed(back_stat_ref.at[r, q], stat_recv.at[r, q])
            landed(back_ref.at[r, q], part_recv.at[r, q])
        sums, tops = pl.ds(0, HEADS), pl.ds(HEADS, HEADS)
        used = [jnp.full((HEADS, BLOCK), counts[r], F32) for r, _ in parts]
        low = [jnp.where(n > 0.5, back_stat_ref[r, q, tops], -jnp.inf) for n, (r, q) in zip(used, parts)]
        top = functools.reduce(jnp.maximum, low)
        factors = [jnp.exp2(t - top) * n for t, n in zip(low, used)]
        total = 1.0 / sum(f * back_stat_ref[r, q, sums] for f, (r, q) in zip(factors, parts))
        heads = []
        for h in range(HEADS):
            rows = pl.ds(HEAD_DIM * h, HEAD_DIM)
            heads.append(
                sum(f[h : h + 1] * back_ref[r, q, rows].astype(F32) for f, (r, q) in zip(factors, parts))
                * total[h : h + 1])
        mixed_ref[row] = jnp.concatenate(heads, axis=0).astype(BF16)
        for copy in gifts() + far_rows():
            copy.wait_send()

    @pl.when(plan.inner)
    def _():
        sibling.wait_send()
        for step in range(y_count):
            to_core(step).wait_send()
            if step > 0:
                along_y(step).wait_send()
        for copy in send_parts():
            copy.wait_send()

    when_each(has, lambda n: lat_rows(n).wait_send())
    for n in range(CHUNKS):
        for copy in side_rows(n):
            copy.wait_send()
    for copy in corners:
        copy.wait_send()
    for copy in keep:
        copy.wait()


def output_kernel(
    mask_ref, mixed_ref, hold_ref, w_out_ref, w_query_in, w_key_in, w_value_in, tokens_in, west_in, east_in, halos_in,
    out_ref,
    fixed_ref, strip_ref, weight_ref, k_ref, vt_ref, qd_ref, acc_ref, top_ref, wide_ref, query_t_ref, value_t_ref,
    list_ref, begin_ref, sem,
):
    lat = lax.axis_index("lat")
    last = lax.axis_size("lat") - 1

    def product(from_ref):
        def body(t, carry):
            both = jnp.concatenate([from_ref[2 * t], from_ref[2 * t + 1]], axis=1)
            result = dot(both, w_out_ref[...], ((0,), (0,))).astype(BF16)
            out_ref[pl.ds(2 * t, 2)] = result.reshape(2, BLOCK, WIDTH)
            return carry

        lax.fori_loop(0, ROWS // 2, body, 0, unroll=3)

    product(mixed_ref)
    holds = jnp.min(hold_ref[...]) > 0.5

    @pl.when(jnp.logical_not(holds))
    def _():
        def fetch(src, dst):
            copy = pltpu.make_async_copy(src, dst, sem)
            copy.start()
            copy.wait()

        fetch(w_key_in, weight_ref)
        prepare_keys(weight_ref, wide_ref)
        fetch(w_query_in, weight_ref)
        query_t_ref[...] = flipped(weight_ref)
        fetch(w_value_in, weight_ref)
        value_t_ref[...] = flipped(weight_ref)
        put_ones(vt_ref)
        qd_ref[...] = jnp.zeros_like(qd_ref)

        def take(src, slot):
            fetch(src, strip_ref)
            tokens = strip_ref[...].reshape(2 * BLOCK, WIDTH)
            put_tokens([(tokens, slot)], wide_ref, value_t_ref, k_ref, vt_ref)
            return tokens

        def load(t, carry):
            part = pl.ds(2 * t, 2)
            take(west_in.at[part], RADIUS + 2 * t)
            take(east_in.at[part], 2 * FRAME + RADIUS + 2 * t)
            tokens = take(tokens_in.at[part], FRAME + RADIUS + 2 * t)
            put_queries([(tokens, (2 * t, 2 * t + 1))], query_t_ref, qd_ref)
            return carry

        lax.fori_loop(0, ROWS // 2, load, 0)
        for column, which in ((1, 0), (0, 1), (2, 2)):
            take(halos_in.at[which, pl.ds(0, 2)], column * FRAME)
            take(halos_in.at[which, pl.ds(2, 2)], column * FRAME + ROWS + RADIUS)
        fixed_ref[...] = mixed_ref[...]

        def again(i, carry):
            pos = jnp.int32(0)
            for d in range(SPAN):
                for e in range(3):
                    list_ref[pos] = e * FRAME + i + d
                    pos = pos + (mask_ref[i, d, e] > 0).astype(jnp.int32)
            begin_ref[0] = pos
            polar = jnp.logical_or(
                jnp.logical_and(lat == 0, i == 0), jnp.logical_and(lat == last, i == ROWS - 1))

            @pl.when(jnp.logical_not(polar))
            def _():
                safe_row(
                    i, 0, 0, begin_ref[0], lambda n: list_ref[n], k_ref, vt_ref, qd_ref, acc_ref, top_ref)
                fixed_ref[i] = normalised(acc_ref, 0)

            return carry

        lax.fori_loop(0, ROWS, again, 0)
        product(fixed_ref)


def per_device(tokens, neighbor_mask, w_query, w_key, w_value, w_out):
    lon_count = lax.axis_size("lon")
    half = lon_count // 2
    strip = lambda *dims: jax.ShapeDtypeStruct((*dims, BLOCK, WIDTH), BF16)
    landing = lambda *dims: pltpu.VMEM((*dims, BLOCK, WIDTH), BF16)
    dma = pltpu.SemaphoreType.DMA
    keys = lambda n: pltpu.VMEM((n, BLOCK, LANES), BF16)
    values = lambda n: pltpu.VMEM((n, PAIRS, VROWS, BLOCK), BF16)
    queries = lambda n: pltpu.VMEM((n, PAIRS, 128, 256), BF16)
    square = pltpu.VMEM((WIDTH, WIDTH), BF16)
    wide = pltpu.VMEM((WIDTH, LANES), BF16)
    tops = pltpu.VMEM((PAIRS, 8, 256), F32)
    mixed = jax.ShapeDtypeStruct((ROWS, WIDTH, BLOCK), BF16)
    mixed, hold, west, east, halos = pl.pallas_call(
        grid_kernel,
        out_shape=[mixed, jax.ShapeDtypeStruct((8, 256), F32), strip(ROWS), strip(ROWS), strip(3, 4)],
        in_specs=[SMEM_SPEC] + [VMEM_SPEC] * 4,
        out_specs=[VMEM_SPEC] * 2 + [ANY_SPEC] * 3,
        scratch_shapes=[
            landing(ROWS), landing(ROWS), landing(3, 4), landing(2), landing(2, half // 2),
            pltpu.VMEM((2, WIDTH, BLOCK), BF16), pltpu.VMEM((2, 2 * HEADS, BLOCK), F32),
            pltpu.VMEM((3, 2, WIDTH, BLOCK), BF16), pltpu.VMEM((3, 2, 2 * HEADS, BLOCK), F32),
            keys(SLOTS), values(SLOTS), queries(ROWS),
            pltpu.VMEM((ROWS, PAIRS, VROWS, 256), F32),
            keys(half), values(half), queries(2),
            pltpu.VMEM((2, PAIRS, VROWS, 256), F32), pltpu.VMEM((2, PAIRS, 8, 256), F32),
            wide, square, square,
            dma((2, CHUNKS)), dma((2, CHUNKS)), dma((2,)), dma((2,)), dma((2,)), dma((2,)), dma((2,)), dma((2,)),
            dma((6,)), dma, dma, dma, dma, *[dma((half // 2,))] * 4,
            dma((2,)), dma((3, 2)), dma((2,)), dma((3, 2)), dma((3,)),
        ],
        compiler_params=pltpu.CompilerParams(
            collective_id=0, has_side_effects=True, vmem_limit_bytes=VMEM_LIMIT),
        name="grid_attention",
    )(neighbor_mask, tokens, w_query, w_key, w_value)
    return pl.pallas_call(
        output_kernel,
        out_shape=strip(ROWS),
        in_specs=[SMEM_SPEC] + [VMEM_SPEC] * 3 + [ANY_SPEC] * 7,
        out_specs=VMEM_SPEC,
        scratch_shapes=[
            pltpu.VMEM((ROWS, WIDTH, BLOCK), BF16), landing(2), square,
            keys(SLOTS), values(SLOTS), queries(ROWS),
            pltpu.VMEM((1, PAIRS, VROWS, 256), F32),
            tops, wide, square, square,
            pltpu.SMEM((SPAN * 3 + 1,), jnp.int32), pltpu.SMEM((1,), jnp.int32), dma,
        ],
        compiler_params=pltpu.CompilerParams(vmem_limit_bytes=VMEM_LIMIT),
        name="output_product",
    )(neighbor_mask, mixed, hold, w_out, w_query, w_key, w_value, tokens, west, east, halos)


def solution(mesh):
    placed = (P("lat", "lon", None), P("lat", None, None), P(), P(), P(), P())
    return jax.shard_map(
        per_device, mesh=mesh, in_specs=placed, out_specs=P("lat", "lon", None), check_vma=False
    )
```
